32 devices in a mesh: dp: 8 (over z, y), seq: 4 (over x, core).
Axes of the slice: x: 2, y: 2, z: 4, core: 2. Of those that a mesh axis runs over, the one named last changes fastest.
Arguments:
- hidden_in: bfloat16 [128, 512, 768], P('dp', 'seq'), may hold values from -6 to 6
- segment_ids: int32 [128, 512], P('dp'), may hold values from 0 to 2, as said below
- cluster_perm: int32 [128, 12, 512], P('dp'), may hold values from 0 to 511, each once within a row
- w_qkv: bfloat16 [768, 2304], replicated, may hold values from -0.21875 to 0.21875
- bias_qv: float32 [1536], replicated, may hold values from -3 to 3
- w_out: bfloat16 [768, 768], replicated, may hold values from -0.875 to 0.875
- bias_out: float32 [768], replicated, may hold values from -2 to 2
- gain_attn: float32 [768], replicated, may hold values from 0.5 to 1.5
- shift_attn: float32 [768], replicated, may hold values from -2 to 2
- w_up: bfloat16 [768, 3072], replicated, may hold values from -0.21875 to 0.21875
- bias_up: float32 [3072], replicated, may hold values from -3 to 3
- w_down: bfloat16 [3072, 768], replicated, may hold values from -0.109375 to 0.109375
- bias_down: float32 [768], replicated, may hold values from -2 to 2
- gain_ffn: float32 [768], replicated, may hold values from 0.5 to 1.5
- shift_ffn: float32 [768], replicated, may hold values from -2 to 2
- grad_out: bfloat16 [128, 512, 768], P('dp', 'seq'), may hold values from -6 to 6
Outputs:
- out_hidden: bfloat16 [128, 512, 768], P('dp', 'seq')
- grad_in: bfloat16 [128, 512, 768], P('dp', 'seq')
- grad_w_qkv: float32 [768, 2304], P(('dp', 'seq'))
- grad_bias_qv: float32 [1536], P(('dp', 'seq'))
- grad_w_out: float32 [768, 768], P(('dp', 'seq'))
- grad_bias_out: float32 [768], P(('dp', 'seq'))
- grad_gain_attn: float32 [768], P(('dp', 'seq'))
- grad_shift_attn: float32 [768], P(('dp', 'seq'))
- grad_w_up: float32 [768, 3072], P(('dp', 'seq'))
- grad_bias_up: float32 [3072], P(('dp', 'seq'))
- grad_w_down: float32 [3072, 768], P(('dp', 'seq'))
- grad_bias_down: float32 [768], P(('dp', 'seq'))
- grad_gain_ffn: float32 [768], P(('dp', 'seq'))
- grad_shift_ffn: float32 [768], P(('dp', 'seq'))
The draws below stay inside these ranges and needn't reach their ends.
Inputs may be any that keep to these rules, and one draw needn't show every extreme that they name: `cluster_perm`: for each row and head, a permutation of the row's 512 positions; a head's cluster c holds the tokens at its entries c * 128 to (c + 1) * 128 - 1. `segment_ids`: each row holds documents 0, 1, 2 in order; document 0 ends within the row's first 128 tokens and document 2 begins within its last 128 tokens.
All inputs are finite; a program needn't handle non-finite values.
Results may differ from the reference program's by a relative error of at most 0.015.
Values may be sent and summed in bfloat16 or wider, within the bound.
No kernel may reach another device: no remote copies, remote signals or barrier semaphores. Data moves between devices by JAX's collectives and lax.ppermute only.
A program may use at most 256 MiB of HBM per device.

```python
import math
import jax
import jax.numpy as jnp
from jax import lax

D = 768
H = 12
HD = 64
FF = 3072
LEN = 512
CL = 128
ROWS = 128
BLK = 128


def draw_segment_ids(key, part):
    key = jax.random.fold_in(key, 7)
    first_key, second_key = jax.random.split(key)
    first_end = jax.random.randint(first_key, (ROWS, 1), 1, BLK)
    last_start = jax.random.randint(second_key, (ROWS, 1), LEN - BLK + 1, LEN)
    position = jnp.arange(LEN, dtype=jnp.int32)[None, :]
    return (position >= first_end).astype(jnp.int32) + (position >= last_start).astype(jnp.int32)


def raised(drawn, stream_key, source, target, blocks, factor):
    owner, partner = [(jnp.arange(drawn.shape[dim]) // (drawn.shape[dim] // blocks)).reshape([-1 if axis == dim else 1 for axis in range(drawn.ndim)]) for dim in (source, target)]
    chosen = jax.random.permutation(stream_key, blocks)[partner]
    strong = (owner == chosen) | (owner == (partner + blocks // 2) % blocks)
    return jnp.where(strong, factor * drawn, drawn)


def level_of(own_key, dims, cuts, least, top_value):
    def one(dim, parts):
        steps = jax.random.uniform(jax.random.fold_in(jax.random.fold_in(own_key, 6), dim), (parts,), jnp.float32, least / len(cuts), top_value / len(cuts))
        return jnp.repeat(jnp.exp(steps), dims[dim] // parts).reshape((-1,) + (1,) * (len(dims) - dim - 1))

    gain = one(*cuts[0])
    for cut in cuts[1:]:
        gain = gain * one(*cut)
    return gain


def gaussian(own_key, extent, deviation, reach, cuts=(), kind=jnp.bfloat16):
    result = jax.random.normal(own_key, extent, jnp.float32) * deviation
    if len(cuts) > 0:
        result = level_of(own_key, extent, cuts, -0.22, 0.18) * result
    return jnp.clip(result, min=-reach, max=reach).astype(kind)


def bell_draw_with(rng, extent, spread, bound, pieces, heavy, kind=jnp.bfloat16):
    values = spread * jax.random.normal(rng, extent, jnp.float32)
    if pieces:
        values = values * level_of(rng, extent, pieces, -0.22, 0.18)
    return jnp.clip(raised(values, jax.random.fold_in(rng, 3), *heavy), -bound, bound).astype(kind)


def setup_inputs(seed: int = 0) -> dict:
    streams_of = jax.random.split(jax.random.key(seed), 17)
    hidden_in = bell_draw_with(streams_of[0], (ROWS, LEN, D), 1.0, 6.0, ((0, 8), (1, 4)), (0, 2, 8, 2.0))
    segment_ids = draw_segment_ids(jax.random.fold_in(streams_of[16], 71), 0)
    cluster_perm = jax.vmap(lambda own: jax.random.permutation(own, LEN))(jax.random.split(streams_of[2], ROWS * H)).reshape((ROWS, H, LEN)).astype(jnp.int32)
    w_qkv = gaussian(streams_of[3], (D, 3 * D), D ** -0.5, 0.21875)
    bias_qv = gaussian(streams_of[4], (2 * D,), 0.5, 3.0, (), jnp.float32)
    w_out = gaussian(streams_of[5], (D, D), (D // 16) ** -0.5, 0.875)
    bias_out = gaussian(streams_of[6], (D,), 0.3, 2.0, (), jnp.float32)
    gain_attn = jnp.clip(1.0 + 0.1 * jax.random.normal(streams_of[7], (D,), jnp.float32), 0.5, 1.5)
    shift_attn = gaussian(streams_of[8], (D,), 0.3, 2.0, (), jnp.float32)
    w_up = gaussian(streams_of[9], (D, FF), D ** -0.5, 0.21875)
    bias_up = gaussian(streams_of[10], (FF,), 0.5, 3.0, (), jnp.float32)
    w_down = gaussian(streams_of[11], (FF, D), FF ** -0.5, 0.109375)
    bias_down = gaussian(streams_of[12], (D,), 0.3, 2.0, (), jnp.float32)
    gain_ffn = jnp.clip(1.0 + 0.1 * jax.random.normal(streams_of[13], (D,), jnp.float32), 0.5, 1.5)
    shift_ffn = gaussian(streams_of[14], (D,), 0.3, 2.0, (), jnp.float32)
    grad_out = bell_draw_with(streams_of[15], (ROWS, LEN, D), 1.0, 6.0, ((0, 8), (1, 4)), (0, 2, 8, 2.0))
    return dict(hidden_in=hidden_in, segment_ids=segment_ids, cluster_perm=cluster_perm, w_qkv=w_qkv, bias_qv=bias_qv, w_out=w_out, bias_out=bias_out, gain_attn=gain_attn, shift_attn=shift_attn, w_up=w_up, bias_up=bias_up, w_down=w_down, bias_down=bias_down, gain_ffn=gain_ffn, shift_ffn=shift_ffn, grad_out=grad_out)


@jax.custom_vjp
def low(v):
    return lax.optimization_barrier(v.astype(jnp.bfloat16)).astype(jnp.float32)

@jax.custom_vjp
def low_back(v):
    return v

def low_keep(v):
    return (low(v), None)

def low_pass(kept, grad):
    return (grad,)

def back_keep(v):
    return (v, None)

def back_low(kept, grad):
    return (low(grad),)
low.defvjp(low_keep, low_pass)
low_back.defvjp(back_keep, back_low)
norm_eps = 1e-05
masked_value = -1e+30
highest = lax.Precision.HIGHEST

def matmul(left_side, right_side):
    return jnp.dot(left_side, right_side, precision=highest)

def layer_norm(values, gain_vec, shift_vec):
    center = values - lax.optimization_barrier(jnp.mean(values, -1, keepdims=True))
    return center * lax.rsqrt(lax.optimization_barrier(jnp.mean(center * center, -1, keepdims=True)) + norm_eps) * gain_vec + shift_vec

def cluster_table(order_table):
    row_count, head_count, length = order_table.shape
    member = jnp.arange(length, dtype=jnp.int32) // CL
    row_index = jnp.arange(row_count, dtype=jnp.int32)[:, None, None]
    head_index = jnp.arange(head_count, dtype=jnp.int32)[None, :, None]
    return jnp.zeros(order_table.shape, jnp.int32).at[row_index, head_index, order_table].set(jnp.broadcast_to(member, order_table.shape))

def forward(params, inputs, clusters, segments):
    w_qkv, bias_qv, w_out, bias_out, gain_attn, shift_attn, w_up, bias_up, w_down, bias_down, gain_ffn, shift_ffn = params
    group_rows = inputs.shape[0]
    flat_rows = inputs.reshape(group_rows * LEN, D)
    bias_full = jnp.concatenate([bias_qv[:D], jnp.zeros_like(bias_qv[:D]), bias_qv[D:]])
    projected = low_back(low(matmul(flat_rows, w_qkv) + bias_full))
    shaped = projected.reshape(group_rows, LEN, 3, H, HD)
    queries = shaped[:, :, 0]
    keys_all = shaped[:, :, 1]
    values_all = shaped[:, :, 2]
    score_scale = 1.0 / math.sqrt(HD)
    scores = low_back(jnp.einsum('rihd,rjhd->rhij', queries, keys_all, precision=highest) * score_scale)
    allowed = (clusters[:, :, :, None] == clusters[:, :, None, :]) & (segments[:, None, :, None] == segments[:, None, None, :])
    masked = jnp.where(allowed, scores, masked_value)
    row_peak = lax.optimization_barrier(jnp.max(masked, -1, keepdims=True))
    exponent = jnp.exp(masked - row_peak)
    attn_prob = low(exponent / lax.optimization_barrier(jnp.sum(exponent, -1, keepdims=True)))
    attended = jnp.einsum('rhij,rjhd->rihd', attn_prob, values_all, precision=highest).reshape(group_rows * LEN, D)
    attended = low_back(low(attended))
    branch = low_back(matmul(attended, w_out) + bias_out)
    first_norm = low(layer_norm(flat_rows + branch, gain_attn, shift_attn))
    pre_act = low_back(matmul(first_norm, w_up) + bias_up)
    activated = low(jax.nn.gelu(pre_act, approximate=False))
    ffn_out = low_back(matmul(activated, w_down) + bias_down)
    return layer_norm(first_norm + ffn_out, gain_ffn, shift_ffn).reshape(group_rows, LEN, D)

def reference(hidden_in, segment_ids, cluster_perm, w_qkv, bias_qv, w_out, bias_out, gain_attn, shift_attn, w_up, bias_up, w_down, bias_down, gain_ffn, shift_ffn, grad_out):
    params = tuple((weight.astype(jnp.float32) for weight in (w_qkv, bias_qv, w_out, bias_out, gain_attn, shift_attn, w_up, bias_up, w_down, bias_down, gain_ffn, shift_ffn)))
    clusters = cluster_table(cluster_perm)
    group_rows = math.gcd(ROWS, 8)
    steps_count = ROWS // group_rows

    def regroup(source_array):
        return source_array.reshape((steps_count, group_rows) + source_array.shape[1:])

    def one_group(grad_total, group_item):
        inputs, cluster_group, segment_group, cotangent = group_item

        def apply_layer(weights_all, rows_in):
            return forward(weights_all, rows_in, cluster_group, segment_group)
        output_rows, pullback = jax.vjp(apply_layer, params, inputs)
        param_grads, input_grads = pullback(cotangent)
        grad_total = jax.tree.map(jnp.add, grad_total, param_grads)
        return (grad_total, (output_rows.astype(jnp.bfloat16), input_grads.astype(jnp.bfloat16)))
    zero_grads = jax.tree.map(jnp.zeros_like, params)
    grad_total, (outputs, input_grads) = lax.scan(one_group, zero_grads, (regroup(hidden_in.astype(jnp.float32)), regroup(clusters), regroup(segment_ids), regroup(grad_out.astype(jnp.float32))))
    out_hidden = outputs.reshape(ROWS, LEN, D)
    grad_in = input_grads.reshape(ROWS, LEN, D)
    return (out_hidden, grad_in, grad_total[0], grad_total[1], grad_total[2], grad_total[3], grad_total[4], grad_total[5], grad_total[6], grad_total[7], grad_total[8], grad_total[9], grad_total[10], grad_total[11])
```

```python
import functools
import math

import jax
import jax.numpy as jnp
from jax import lax
from jax.experimental import pallas as pl
from jax.experimental.pallas import tpu as pltpu
from jax.sharding import PartitionSpec as P

CL = 128
DOCS = 3
CODES = 16
NORM_EPS = 1e-05
BIG = 2.0**50
F32 = jnp.float32
BF16 = jnp.bfloat16
NN = (((1,), (0,)), ((), ()))
NT = (((1,), (1,)), ((), ()))
TN = (((0,), (0,)), ((), ()))
VMEM = 62 * 2**20


def mm(a, b, dims=NN):
    return lax.dot_general(a, b, dims, preferred_element_type=F32)


def whole(shape):
    return pl.BlockSpec(shape, lambda i: (0,) * len(shape), pipeline_mode=pl.Buffered(1))


def lead(shape):
    return pl.BlockSpec((1,) + shape, lambda i: (i,) + (0,) * len(shape))


def rows_of(tile, width):
    return pl.BlockSpec((tile, width), lambda i: (i, 0))


def shape_of(shape, dtype):
    return jax.ShapeDtypeStruct(shape, dtype)


def params():
    return pltpu.CompilerParams(vmem_limit_bytes=VMEM)


def cost(flops, nbytes):
    return pl.CostEstimate(flops=int(flops), bytes_accessed=int(nbytes), transcendentals=0)


def attend_kernel(
    x_ref, code_ref, wt_ref, bt_ref, wo_ref, bo_ref, ga_ref, sa_ref,
    qkv_ref, p_ref, il_ref, att_ref, first_ref, n_ref, s_ref, *, heads, hs,
):
    D = heads * hs
    x = x_ref[0]
    L = x.shape[0]
    qkv_ref[0] = (mm(wt_ref[...], x, NT) + bt_ref[...]).astype(BF16)
    it = lax.broadcasted_iota(jnp.int32, (CODES, L), 0)
    for h in range(heads):
        q = qkv_ref[0, h * hs : (h + 1) * hs, :]
        k = qkv_ref[0, D + h * hs : D + (h + 1) * hs, :]
        v = qkv_ref[0, 2 * D + h * hs : 2 * D + (h + 1) * hs, :]
        same = it == code_ref[0, h : h + 1, :]
        qa = jnp.concatenate([q, jnp.where(same, BIG, 0.0).astype(BF16)], 0)
        ka = jnp.concatenate([k, jnp.where(same, 0.0, -BIG).astype(BF16)], 0)
        s = mm(ka, qa, TN)
        e = jnp.exp(s - jnp.max(s, axis=0, keepdims=True))
        il = 1.0 / jnp.sum(e, axis=0, keepdims=True)
        p = e.astype(BF16)
        p_ref[0, h] = p
        il_ref[0, h : h + 1, :] = il
        att_ref[0, h * hs : (h + 1) * hs, :] = (mm(v, p) * il).astype(BF16)
    v1 = x.astype(F32) + mm(att_ref[0], wo_ref[...], TN) + bo_ref[...]
    c = v1 - jnp.mean(v1, -1, keepdims=True)
    s1 = lax.rsqrt(jnp.mean(c * c, -1, keepdims=True) + NORM_EPS)
    n1 = c * s1
    first_ref[0] = (n1 * ga_ref[...] + sa_ref[...]).astype(BF16)
    n_ref[0] = n1.astype(BF16)
    s_ref[0] = jnp.broadcast_to(s1, (L, 128))


def attend(x, code, wt, bt, wo, bo, ga, sa, heads, hs):
    R, L, D = x.shape
    return pl.pallas_call(
        functools.partial(attend_kernel, heads=heads, hs=hs),
        grid=(R,),
        in_specs=[
            lead((L, D)), lead((heads, L)), whole((3 * D, D)), whole((3 * D, 1)),
            whole((D, D)), whole((1, D)), whole((1, D)), whole((1, D)),
        ],
        out_specs=[
            lead((3 * D, L)), lead((heads, L, L)), lead((heads, L)), lead((D, L)),
            lead((L, D)), lead((L, D)), lead((L, 128)),
        ],
        out_shape=[
            shape_of((R, 3 * D, L), BF16), shape_of((R, heads, L, L), BF16),
            shape_of((R, heads, L), F32), shape_of((R, D, L), BF16),
            shape_of((R, L, D), BF16), shape_of((R, L, D), BF16), shape_of((R, L, 128), F32),
        ],
        compiler_params=params(),
        cost_estimate=cost(R * (8 * L * D * D + 4 * 4 * heads * L * L * hs), R * 2 * heads * L * L),
        name="attend",
    )(x, code, wt, bt, wo, bo, ga, sa)


def ffn_kernel(
    first_ref, gout_ref, wu_ref, bu_ref, wd_ref, bd_ref, gf_ref, sf_ref,
    out_ref, gffn_ref, act_ref, slope_ref, sums_ref,
):
    first = first_ref[...]
    u = mm(first, wu_ref[...]) + bu_ref[...]
    half = 0.5 * (1.0 + lax.erf(u * 0.7071067811865476))
    act = (u * half).astype(BF16)
    act_ref[...] = act
    slope_ref[...] = (half + u * jnp.exp(-0.5 * u * u) * 0.3989422804014327).astype(BF16)
    y = first.astype(F32) + mm(act, wd_ref[...]) + bd_ref[...]
    c = y - jnp.mean(y, -1, keepdims=True)
    s2 = lax.rsqrt(jnp.mean(c * c, -1, keepdims=True) + NORM_EPS)
    n2 = c * s2
    out_ref[...] = (n2 * gf_ref[...] + sf_ref[...]).astype(BF16)
    go = gout_ref[...].astype(F32)
    e = go * gf_ref[...]
    g2 = s2 * (e - jnp.mean(e, -1, keepdims=True) - n2 * jnp.mean(e * n2, -1, keepdims=True))
    gl = g2.astype(BF16)
    gffn_ref[...] = gl

    @pl.when(pl.program_id(0) == 0)
    def _():
        sums_ref[...] = jnp.zeros_like(sums_ref)

    sums_ref[0:1, :] += jnp.sum(gl.astype(F32), 0, keepdims=True)
    sums_ref[1:2, :] += jnp.sum(go * n2, 0, keepdims=True)
    sums_ref[2:3, :] += jnp.sum(go, 0, keepdims=True)


def ffn(first, gout, wu, bu, wd, bd, gf, sf, tile):
    T, D = first.shape
    FF = wu.shape[1]
    return pl.pallas_call(
        ffn_kernel,
        grid=(T // tile,),
        in_specs=[
            rows_of(tile, D), rows_of(tile, D), whole((D, FF)), whole((1, FF)),
            whole((FF, D)), whole((1, D)), whole((1, D)), whole((1, D)),
        ],
        out_specs=[
            rows_of(tile, D), rows_of(tile, D), rows_of(tile, FF), rows_of(tile, FF),
            pl.BlockSpec((8, D), lambda i: (0, 0)),
        ],
        out_shape=[
            shape_of((T, D), BF16), shape_of((T, D), BF16), shape_of((T, FF), BF16),
            shape_of((T, FF), BF16), shape_of((8, D), F32),
        ],
        compiler_params=params(),
        cost_estimate=cost(4 * T * D * FF * 1.3, 4 * T * FF + 4 * D * FF),
        name="ffn",
    )(first, gout, wu, bu, wd, bd, gf, sf)


def down_grad_kernel(act_ref, g_ref, o_ref):
    o_ref[...] = mm(act_ref[...], g_ref[...], TN).astype(BF16)


def down_grad(act, g, tile):
    T, FF = act.shape
    D = g.shape[1]
    return pl.pallas_call(
        down_grad_kernel,
        grid=(FF // tile,),
        in_specs=[pl.BlockSpec((T, tile), lambda i: (0, i)), whole((T, D))],
        out_specs=rows_of(tile, D),
        out_shape=shape_of((FF, D), BF16),
        compiler_params=params(),
        cost_estimate=cost(2 * T * D * FF * 1.3, 2 * T * FF + 2 * D * FF),
        name="down_grad",
    )(act, g)


def ffn_back_kernel(
    g_ref, slope_ref, wu_ref, wd_ref, wo_ref, n_ref, s_ref, ga_ref, att_ref, il_ref,
    gpre_ref, gone_ref, gbr_ref, do_ref, de_ref, sums_ref, bsum_ref, *, heads, hs,
):
    g = g_ref[...]
    gp = (mm(g, wd_ref[...], NT) * slope_ref[...].astype(F32)).astype(BF16)
    gpre_ref[...] = gp
    gfirst = mm(gp, wu_ref[...], NT) + g.astype(F32)
    n1 = n_ref[0].astype(F32)
    e = gfirst * ga_ref[...]
    g1 = s_ref[0, :, 0:1] * (
        e - jnp.mean(e, -1, keepdims=True) - n1 * jnp.mean(e * n1, -1, keepdims=True)
    )
    gl = g1.astype(BF16)
    gone_ref[0] = gl
    gbr_ref[...] = gl
    da = mm(wo_ref[...], gl, NT)
    for h in range(heads):
        il = il_ref[0, h : h + 1, :]
        piece = da[h * hs : (h + 1) * hs, :] * il
        do_ref[0, h * hs : (h + 1) * hs, :] = piece.astype(BF16)
        att = att_ref[0, h * hs : (h + 1) * hs, :].astype(F32)
        de_ref[0, h : h + 1, :] = jnp.sum(piece * att, axis=0, keepdims=True)

    @pl.when(pl.program_id(0) == 0)
    def _():
        sums_ref[...] = jnp.zeros_like(sums_ref)
        bsum_ref[...] = jnp.zeros_like(bsum_ref)

    sums_ref[0:1, :] += jnp.sum(gl.astype(F32), 0, keepdims=True)
    sums_ref[1:2, :] += jnp.sum(gfirst * n1, 0, keepdims=True)
    sums_ref[2:3, :] += jnp.sum(gfirst, 0, keepdims=True)
    bsum_ref[0:1, :] += jnp.sum(gp.astype(F32), 0, keepdims=True)


def ffn_back(g, slope, wu, wd, wo, n1, s1, ga, att, il, heads, hs):
    T, D = g.shape
    FF = wu.shape[1]
    R, L = n1.shape[:2]
    return pl.pallas_call(
        functools.partial(ffn_back_kernel, heads=heads, hs=hs),
        grid=(R,),
        in_specs=[
            rows_of(L, D), rows_of(L, FF), whole((D, FF)), whole((FF, D)), whole((D, D)),
            lead((L, D)), lead((L, 128)), whole((1, D)), lead((D, L)), lead((heads, L)),
        ],
        out_specs=[
            rows_of(L, FF), lead((L, D)), rows_of(L, D), lead((D, L)), lead((heads, L)),
            pl.BlockSpec((8, D), lambda i: (0, 0)), pl.BlockSpec((8, FF), lambda i: (0, 0)),
        ],
        out_shape=[
            shape_of((T, FF), BF16), shape_of((R, L, D), BF16), shape_of((T, D), BF16),
            shape_of((R, D, L), BF16), shape_of((R, heads, L), F32), shape_of((8, D), F32),
            shape_of((8, FF), F32),
        ],
        compiler_params=params(),
        cost_estimate=cost(4 * T * D * FF * 1.5, 4 * T * FF + 4 * D * FF),
        name="ffn_back",
    )(g, slope, wu, wd, wo, n1, s1, ga, att, il)


def up_grad_kernel(x_ref, g_ref, o_ref):
    o_ref[...] = mm(x_ref[...], g_ref[...], TN).astype(BF16)


def up_grad(x, g, tile):
    T, D = x.shape
    FF = g.shape[1]
    return pl.pallas_call(
        up_grad_kernel,
        grid=(FF // tile,),
        in_specs=[whole((T, D)), pl.BlockSpec((T, tile), lambda i: (0, i))],
        out_specs=pl.BlockSpec((D, tile), lambda i: (0, i)),
        out_shape=shape_of((D, FF), BF16),
        compiler_params=params(),
        cost_estimate=cost(2 * T * D * FF * 1.3, 2 * T * FF + 2 * D * FF),
        name="up_grad",
    )(x, g)


def out_grad_kernel(att_ref, g_ref, o_ref):
    total = mm(att_ref[0], g_ref[0])
    for r in range(1, att_ref.shape[0]):
        total = total + mm(att_ref[r], g_ref[r])
    o_ref[...] = total.astype(BF16)


def out_grad(att, g):
    R, D, L = att.shape
    tile = D // 3
    return pl.pallas_call(
        out_grad_kernel,
        grid=(3,),
        in_specs=[pl.BlockSpec((R, tile, L), lambda i: (0, i, 0)), whole((R, L, D))],
        out_specs=rows_of(tile, D),
        out_shape=shape_of((D, D), BF16),
        compiler_params=params(),
        cost_estimate=cost(2 * R * L * D * D * 1.3, 4 * R * L * D),
        name="out_grad",
    )(att, g)


def attend_back_kernel(
    qkv_ref, p_ref, do_ref, de_ref, gone_ref, wt_ref, g_ref, gin_ref, sums_ref, *, heads, hs, scale
):
    D = heads * hs
    for h in range(heads):
        q = qkv_ref[0, h * hs : (h + 1) * hs, :]
        k = qkv_ref[0, D + h * hs : D + (h + 1) * hs, :]
        v = qkv_ref[0, 2 * D + h * hs : 2 * D + (h + 1) * hs, :]
        do = do_ref[0, h * hs : (h + 1) * hs, :]
        p = p_ref[0, h]
        dp = mm(v, do, TN)
        ds = (p.astype(F32) * (dp - de_ref[0, h : h + 1, :])).astype(BF16)
        g_ref[0, h * hs : (h + 1) * hs, :] = (mm(k, ds) * scale).astype(BF16)
        g_ref[0, D + h * hs : D + (h + 1) * hs, :] = mm(q, ds, NT).astype(BF16)
        g_ref[0, 2 * D + h * hs : 2 * D + (h + 1) * hs, :] = mm(do, p, NT).astype(BF16)
    g = g_ref[0]
    gin_ref[0] = (mm(g, wt_ref[...], TN) + gone_ref[0].astype(F32)).astype(BF16)

    @pl.when(pl.program_id(0) == 0)
    def _():
        sums_ref[...] = jnp.zeros_like(sums_ref)

    ones = jnp.ones((8, g.shape[1]), BF16)
    sums_ref[...] += mm(ones, g, NT)


def attend_back(qkv, p, do, de, gone, wt, heads, hs, scale):
    R, D3, L = qkv.shape
    D = D3 // 3
    return pl.pallas_call(
        functools.partial(attend_back_kernel, heads=heads, hs=hs, scale=scale),
        grid=(R,),
        in_specs=[
            lead((D3, L)), lead((heads, L, L)), lead((D, L)), lead((heads, L)), lead((L, D)),
            whole((D3, D)),
        ],
        out_specs=[lead((D3, L)), lead((L, D)), pl.BlockSpec((8, D3), lambda i: (0, 0))],
        out_shape=[
            shape_of((R, D3, L), BF16), shape_of((R, L, D), BF16), shape_of((8, D3), F32),
        ],
        compiler_params=params(),
        cost_estimate=cost(R * (6 * L * D * D + 4 * 8 * heads * L * L * hs), R * 2 * heads * L * L),
        name="attend_back",
    )(qkv, p, do, de, gone, wt)


def qkv_grad_kernel(x_ref, g_ref, o_ref):
    total = mm(x_ref[0], g_ref[0], (((0,), (1,)), ((), ())))
    for r in range(1, x_ref.shape[0]):
        total = total + mm(x_ref[r], g_ref[r], (((0,), (1,)), ((), ())))
    o_ref[...] = total.astype(BF16)


def qkv_grad(x, g):
    R, L, D = x.shape
    D3 = g.shape[1]
    tile = 768
    return pl.pallas_call(
        qkv_grad_kernel,
        grid=(D3 // tile,),
        in_specs=[whole((R, L, D)), pl.BlockSpec((R, tile, L), lambda i: (0, i, 0))],
        out_specs=pl.BlockSpec((D, tile), lambda i: (0, i)),
        out_shape=shape_of((D, D3), BF16),
        compiler_params=params(),
        cost_estimate=cost(2 * R * L * D * D3 * 1.3, 2 * R * L * (D + D3)),
        name="qkv_grad",
    )(x, g)


def bits_of(size):
    return [b for b in range(size.bit_length() - 1)]


def flip(x, axis, size, bit):
    return lax.ppermute(x, axis, [(i, i ^ (1 << bit)) for i in range(size)])


def my_bit(axis, bit):
    return (lax.axis_index(axis) >> bit) & 1


def pick(x, index, axis):
    return lax.dynamic_index_in_dim(x, index, axis, keepdims=False)


def block_order(size):
    order = [0]
    for bit in reversed(bits_of(size)):
        order = order + [o ^ (1 << bit) for o in order]
    return order


def to_rows(x, axis, size):
    held = x
    for bit in reversed(bits_of(size)):
        mine = my_bit(axis, bit)
        split = held.reshape((2, held.shape[0] // 2) + held.shape[1:])
        other = flip(pick(split, 1 - mine, 0), axis, size, bit)
        held = jnp.concatenate([pick(split, mine, 0), other], 2)
    return held[0]


def to_blocks(x, axis, size):
    held = x[None]
    for bit in bits_of(size):
        mine = my_bit(axis, bit)
        half = held.shape[2] // 2
        own = held[:, :, :half]
        other = flip(held[:, :, half:], axis, size, bit)
        low = jnp.where(mine == 0, own, other)
        high = jnp.where(mine == 0, other, own)
        held = jnp.concatenate([low, high], 0)
    return held


def reduce_rows(x, sizes, order):
    (dp, seq) = sizes
    names = [("dp", b) for b in reversed(bits_of(dp))] + [("seq", b) for b in reversed(bits_of(seq))]
    held = x.reshape((2,) * len(names) + (x.shape[0] // (dp * seq),) + x.shape[1:])
    left = list(names)
    for name, bit in order:
        axis = left.index((name, bit))
        mine = my_bit(name, bit)
        size = dp if name == "dp" else seq
        other = flip(pick(held, 1 - mine, axis), name, size, bit)
        held = (pick(held, mine, axis).astype(F32) + other.astype(F32)).astype(BF16)
        left.pop(axis)
    return held


def shards(
    dp, seq, hidden_in, segment_ids, cluster_perm, w_qkv, bias_qv, w_out, bias_out, gain_attn,
    shift_attn, w_up, bias_up, w_down, bias_down, gain_ffn, shift_ffn, grad_out,
):
    row_count, block_len, D = hidden_in.shape
    heads = cluster_perm.shape[1]
    hs = D // heads
    L = segment_ids.shape[1]
    FF = w_up.shape[1]
    R = row_count // seq
    T = R * L
    scale = 1.0 / math.sqrt(hs)
    me = lax.axis_index("seq")

    x = to_rows(hidden_in.reshape(seq, R, block_len, D), "seq", seq)
    gout = to_rows(grad_out.reshape(seq, R, block_len, D), "seq", seq)

    perm = lax.dynamic_slice_in_dim(cluster_perm, me * R, R, 0)
    segs = lax.dynamic_slice_in_dim(segment_ids, me * R, R, 0)
    member = (jnp.arange(L, dtype=jnp.int32) // CL).astype(BF16)
    hi = (perm[:, :, None, :] // CL == jnp.arange(L // CL)[:, None]).astype(BF16) * member
    lo = (perm[:, :, None, :] % CL == jnp.arange(CL)[:, None]).astype(BF16)
    cluster = jnp.einsum("rhaj,rhbj->rhab", hi, lo, preferred_element_type=F32)
    code = cluster.reshape(R, heads, L).astype(jnp.int32) * DOCS + segs[:, None, :]
    code = code.reshape(R, heads, seq, block_len)
    code = jnp.concatenate([pick(code, me ^ o, 2) for o in block_order(seq)], -1)

    col = jnp.concatenate([jnp.full((D,), scale, F32), jnp.ones((2 * D,), F32)])
    wt = w_qkv.T
    wts = (wt.astype(F32) * col[:, None]).astype(BF16)
    bias_full = jnp.concatenate([bias_qv[:D] * scale, jnp.zeros((D,), F32), bias_qv[D:]])
    row = lambda v: v.reshape(1, -1)

    qkv, p, il, att, first, n1, s1 = attend(
        x, code, wts, bias_full.reshape(-1, 1), w_out, row(bias_out), row(gain_attn),
        row(shift_attn), heads, hs,
    )
    first = first.reshape(T, D)
    out, gffn, act, slope, sums_ffn = ffn(
        first, gout.reshape(T, D), w_up, row(bias_up), w_down, row(bias_down), row(gain_ffn),
        row(shift_ffn), L,
    )
    out_hidden = to_blocks(out.reshape(R, L, D), "seq", seq).reshape(row_count, block_len, D)
    d_down = down_grad(act, gffn, 512)
    gpre, gone, gbr, do, de, sums_attn, sums_up = ffn_back(
        gffn, slope, w_up, w_down, w_out, n1, s1, row(gain_attn), att, il, heads, hs
    )
    d_up = up_grad(first, gpre, 512)
    d_out = out_grad(att, gbr.reshape(R, L, D))
    g, gin, sums_qkv = attend_back(qkv, p, do, de, gone, wt, heads, hs, scale)
    grad_in = to_blocks(gin, "seq", seq).reshape(row_count, block_len, D)
    d_qkv = qkv_grad(x, g)

    n = dp * seq
    small = [
        sums_qkv[0, :D], sums_qkv[0, 2 * D :], sums_attn[0], sums_attn[1], sums_attn[2],
        sums_up[0], sums_ffn[0], sums_ffn[1], sums_ffn[2],
    ]
    small = [jnp.concatenate(small[:2])] + small[2:]
    per = [v.size // n for v in small]
    packed = jnp.concatenate([v.reshape(n, -1) for v in small], -1)
    pad = 8 * D - packed.shape[1] if packed.shape[1] <= 8 * D else 0
    packed = jnp.pad(packed, ((0, 0), (0, pad))).reshape(n * 8, D).astype(BF16)

    bits = lambda name, size: [(name, b) for b in bits_of(size)]
    order = [("seq", 0)] + bits("dp", dp) + bits("seq", seq)[1:]
    reduce = lambda v: reduce_rows(v, (dp, seq), order)
    r_down = reduce(d_down).astype(F32)
    r_up = reduce(d_up).astype(F32)
    r_out = reduce(jnp.concatenate([d_out.reshape(n, -1, D), packed.reshape(n, 8, D)], 1).reshape(-1, D))
    r_out = r_out.astype(F32)
    r_qkv = reduce(d_qkv).astype(F32)
    vec = r_out[D // n :].reshape(-1)
    cuts, at = [], 0
    for width in per:
        cuts.append(vec[at : at + width])
        at += width
    b_qv, b_out, g_attn, s_attn, b_up, b_down, g_ffn, s_ffn = cuts
    return (
        out_hidden, grad_in, r_qkv, b_qv, r_out[: D // n], b_out, g_attn, s_attn, r_up, b_up,
        r_down, b_down, g_ffn, s_ffn,
    )


def solution(mesh):
    tok = P("dp", "seq", None)
    both = ("dp", "seq")
    return jax.shard_map(
        functools.partial(shards, mesh.shape["dp"], mesh.shape["seq"]),
        mesh=mesh,
        in_specs=(tok, P("dp", None), P("dp", None, None)) + (P(),) * 12 + (tok,),
        out_specs=(
            tok, tok, P(both, None), P(both), P(both, None), P(both), P(both), P(both),
            P(both, None), P(both), P(both, None), P(both), P(both), P(both),
        ),
        check_vma=False,
    )
```

```python
import functools
import math

import jax
import jax.numpy as jnp
from jax import lax
from jax.experimental import pallas as pl
from jax.experimental.pallas import tpu as pltpu
from jax.sharding import PartitionSpec as P

CL = 128
DOCS = 3
CODES = 16
NORM_EPS = 1e-05
BIG = 2.0**50
F32 = jnp.float32
BF16 = jnp.bfloat16
NN = (((1,), (0,)), ((), ()))
NT = (((1,), (1,)), ((), ()))
TN = (((0,), (0,)), ((), ()))
MIB = 2**20
VMEM = 48 * MIB
ATTEND_VMEM = 40 * MIB
FFN_VMEM = 48 * MIB
BACK_VMEM = 48 * MIB
ATTEND_BACK_VMEM = 40 * MIB
WHOLE = pl.BlockSpec(memory_space=pltpu.VMEM)
TICK = jax.ShapeDtypeStruct((1, 1), jnp.float32)
TICK1 = pl.BlockSpec((1, 1), lambda i: (0, 0))
TICK2 = pl.BlockSpec((1, 1), lambda i, g: (0, 0))
TICK3 = pl.BlockSpec((1, 1), lambda i, g, me: (0, 0))
ANY = pl.BlockSpec(memory_space=pl.ANY)


def mm(a, b, dims=NN):
    return lax.dot_general(a, b, dims, preferred_element_type=F32)


def whole(shape):
    return pl.BlockSpec(shape, lambda i: (0,) * len(shape), pipeline_mode=pl.Buffered(1))


def lead(shape):
    return pl.BlockSpec((1,) + shape, lambda i: (i,) + (0,) * len(shape))


def rows_of(tile, width):
    return pl.BlockSpec((tile, width), lambda i: (i, 0))


def shape_of(shape, dtype):
    return jax.ShapeDtypeStruct(shape, dtype)


def params(limit=VMEM):
    return pltpu.CompilerParams(vmem_limit_bytes=limit)


def cost(flops, nbytes):
    return pl.CostEstimate(flops=int(flops), bytes_accessed=int(nbytes), transcendentals=0)


def part_specs(parts, R, at, block_len, D):
    own = pl.BlockSpec((1, block_len, D), lambda i, g, me: (me[0] * R + at + i, 0, 0))
    specs = [own]
    for bit, (part, base) in enumerate(parts[1:]):
        shape = (1, 1) + part.shape[2:]
        place = lambda bit, base, i, g, me: (me[0] >> (bit + 1), at + i - base, 0, 0)
        specs.append(pl.BlockSpec(shape, functools.partial(place, bit, base)))
    return specs


def arrays_of(parts):
    return [parts[0]] + [part for part, _ in parts[1:]]


def merge(refs):
    return jnp.concatenate([refs[0][0]] + [ref[0, 0] for ref in refs[1:]], 0)


def attend_kernel(me_ref, *refs, nparts, heads, hs, group, scale, nio):
    parts, (code_ref, wt_ref, bt_ref, wo_ref, vec_ref) = refs[:nparts], refs[nparts : nparts + 5]
    x_ref, qkv_ref, p_ref, il_ref, att_ref, first_ref, n_ref, s_ref, tick_ref = refs[nparts + 5 + nio :]
    tick_ref[...] = jnp.zeros_like(tick_ref)
    D = heads * hs
    L = x_ref.shape[1]
    step = pl.program_id(1)

    @pl.when(step == 0)
    def _():
        x_ref[0] = merge(parts)
        f = mm(wt_ref[...], x_ref[0], NT) + bt_ref[:, 0:1]
        qkv_ref[0, :D, :] = (f[:D].astype(BF16).astype(F32) * scale).astype(BF16)
        qkv_ref[0, D:, :] = f[D:].astype(BF16)

    it = lax.broadcasted_iota(jnp.int32, (CODES, L), 0)
    for i in range(group):
        at = pl.multiple_of((step * group + i) * hs, hs)
        q = qkv_ref[0, pl.ds(at, hs), :]
        k = qkv_ref[0, pl.ds(D + at, hs), :]
        v = qkv_ref[0, pl.ds(2 * D + at, hs), :]
        same = it == code_ref[0, 0, i : i + 1, :]
        qa = jnp.concatenate([q, jnp.where(same, BIG, 0.0).astype(BF16)], 0)
        ka = jnp.concatenate([k, jnp.where(same, 0.0, -BIG).astype(BF16)], 0)
        s = mm(ka, qa, TN)
        e = jnp.exp(s - jnp.max(s, axis=0, keepdims=True))
        il = 1.0 / jnp.sum(e, axis=0, keepdims=True)
        p = e.astype(BF16)
        p_ref[0, i] = p
        il_ref[0, 0, i : i + 1, :] = il
        att_ref[0, pl.ds(at, hs), :] = (mm(v, p) * il).astype(BF16)

    @pl.when(step == heads // group - 1)
    def _():
        v1 = x_ref[0].astype(F32) + mm(att_ref[0], wo_ref[...], TN) + vec_ref[0:1, :]
        c = v1 - jnp.mean(v1, -1, keepdims=True)
        s1 = lax.rsqrt(jnp.mean(c * c, -1, keepdims=True) + NORM_EPS)
        n1 = c * s1
        first_ref[0] = (n1 * vec_ref[1:2, :] + vec_ref[2:3, :]).astype(BF16)
        n_ref[0] = n1.astype(BF16)
        s_ref[0] = jnp.broadcast_to(s1, (L, 128))


def attend(me, parts, at, r, R, code, wt, bt, wo, vec, heads, hs, scale, group, deps, held):
    D = wo.shape[0]
    L = code.shape[-1]
    here = lambda shape: pl.BlockSpec((1,) + shape, lambda i, g, me: (at + i,) + (0,) * len(shape))
    grouped = lambda shape: pl.BlockSpec((1, 1) + shape, lambda i, g, me: (at + i, g, 0, 0))
    shapes = [
        shape_of((R, L, D), BF16),
        shape_of((R, 3 * D, L), BF16), shape_of((R, heads, L, L), BF16),
        shape_of((R, heads // group, group, L), F32), shape_of((R, D, L), BF16),
        shape_of((R, L, D), BF16), shape_of((R, L, D), BF16), shape_of((R, L, 128), F32),
        TICK,
    ]
    nio = len(held) + len(deps)
    np_ = len(parts)
    return pl.pallas_call(
        functools.partial(
            attend_kernel, nparts=np_, heads=heads, hs=hs, group=group, scale=scale, nio=nio
        ),
        grid_spec=pltpu.PrefetchScalarGridSpec(
            num_scalar_prefetch=1,
            grid=(r, heads // group),
            in_specs=part_specs(parts, R, at, parts[0].shape[1], D) + [
                grouped((group, L)), WHOLE, WHOLE, WHOLE, WHOLE,
            ] + [ANY] * nio,
            out_specs=[
                here((L, D)),
                here((3 * D, L)), pl.BlockSpec((1, group, L, L), lambda i, g, me: (at + i, g, 0, 0)),
                grouped((group, L)), here((D, L)), here((L, D)), here((L, D)), here((L, 128)),
                TICK3,
            ],
        ),
        out_shape=shapes,
        input_output_aliases={1 + np_ + 5 + len(deps) + i: i for i in range(len(held))},
        compiler_params=params(ATTEND_VMEM),
        cost_estimate=cost(r * (8 * L * D * D + 4 * 4 * heads * L * L * hs), r * 2 * heads * L * L),
        name="attend",
    )(me, *arrays_of(parts), code, wt, bt, wo, vec, *deps, *held)


def prepare_kernel(me_ref, w_ref, b_ref, perm_ref, seg_ref, *rest, seq):
    wt_ref, bt_ref, code_ref = rest[-3:]
    wt_ref[...] = w_ref[...].T
    bt_ref[...] = b_ref[...].T
    R, heads, L = perm_ref.shape
    group = code_ref.shape[2]
    me = me_ref[0]
    block = L // seq
    high = lax.broadcasted_iota(jnp.int32, (8, L), 0)
    low = lax.broadcasted_iota(jnp.int32, (128, L), 0)
    member = (lax.broadcasted_iota(jnp.int32, (8, L), 1) // CL).astype(F32)
    for r in range(R):
        seg = seg_ref[pl.ds(me * R + r, 1), :]
        for bit in bits_of(seq):
            blocks = [seg[:, i * block : (i + 1) * block] for i in range(seq)]
            turned = jnp.concatenate([blocks[i ^ (1 << bit)] for i in range(seq)], 1)
            seg = jnp.where(((me >> bit) & 1) == 1, turned, seg)
        for h in range(heads):
            place = perm_ref[r, h : h + 1, :] ^ (me * block)
            a = jnp.where((place >> 7) == high, member, 0.0).astype(BF16)
            b = ((place & 127) == low).astype(BF16)
            table = mm(a, b, NT)
            row = jnp.concatenate([table[i : i + 1, :] for i in range(L // 128)], 1)
            code_ref[r, h // group, h % group : h % group + 1, :] = row.astype(jnp.int32) * DOCS + seg


def prepare(me, seq, w, b, perm, segs, group, deps):
    rows, heads, L = perm.shape
    R = rows // seq
    D, D3 = w.shape
    full = lambda shape: pl.BlockSpec(shape, lambda i, me: (0,) * len(shape))
    codes = (R, heads // group, group, L)
    return pl.pallas_call(
        functools.partial(prepare_kernel, seq=seq),
        grid_spec=pltpu.PrefetchScalarGridSpec(
            num_scalar_prefetch=1,
            grid=(1,),
            in_specs=[
                full((D, D3)), full((8, D3)), pl.BlockSpec((R, heads, L), lambda i, me: (me[0], 0, 0)),
                full(segs.shape),
            ] + [ANY] * len(deps),
            out_specs=[full((D3, D)), full((D3, 8)), full(codes)],
        ),
        out_shape=[shape_of((D3, D), BF16), shape_of((D3, 8), F32), shape_of(codes, jnp.int32)],
        compiler_params=params(32 * MIB),
        cost_estimate=cost(4e9, 8e6),
        name="prepare",
    )(me, w, b, perm, segs, *deps)


def join_kernel(*refs):
    refs[-1][...] = jnp.zeros_like(refs[-1])


def join(*after):
    return pl.pallas_call(
        join_kernel,
        in_specs=[ANY] * len(after),
        out_specs=WHOLE,
        out_shape=TICK,
        compiler_params=params(4 * MIB),
        cost_estimate=cost(1, 1),
        name="join",
    )(*after)


def ffn_kernel(me_ref, *refs, nparts, nio):
    parts, (first_ref, wu_ref, bu_ref, wd_ref, vec_ref) = refs[:nparts], refs[nparts : nparts + 5]
    lo_ref, hi_ref, gffn_ref, act_ref, slope_ref, sums_ref, tick_ref = refs[nparts + 5 + nio :]
    tick_ref[...] = jnp.zeros_like(tick_ref)
    first = first_ref[...]
    u = mm(first, wu_ref[...]) + bu_ref[...]
    half = 0.5 * (1.0 + lax.erf(u * 0.7071067811865476))
    act = (u * half).astype(BF16)
    act_ref[...] = act
    slope_ref[...] = (half + u * jnp.exp(-0.5 * u * u) * 0.3989422804014327).astype(BF16)
    y = first.astype(F32) + mm(act, wd_ref[...]) + vec_ref[3:4, :]
    c = y - jnp.mean(y, -1, keepdims=True)
    s2 = lax.rsqrt(jnp.mean(c * c, -1, keepdims=True) + NORM_EPS)
    n2 = c * s2
    out = (n2 * vec_ref[4:5, :] + vec_ref[5:6, :]).astype(BF16)
    half_len = out.shape[0] // 2
    lo_ref[0] = out[:half_len]
    hi_ref[0] = out[half_len:]
    go = merge(parts).astype(F32)
    e = go * vec_ref[4:5, :]
    g2 = s2 * (e - jnp.mean(e, -1, keepdims=True) - n2 * jnp.mean(e * n2, -1, keepdims=True))
    gl = g2.astype(BF16)
    gffn_ref[...] = gl

    @pl.when(pl.program_id(0) == 0)
    def _():
        sums_ref[...] = jnp.zeros_like(sums_ref)

    sums_ref[0:1, :] += jnp.sum(gl.astype(F32), 0, keepdims=True)
    sums_ref[1:2, :] += jnp.sum(go * n2, 0, keepdims=True)
    sums_ref[2:3, :] += jnp.sum(go, 0, keepdims=True)


def ffn(me, first, parts, at, r, R, wu, bu, wd, vec, deps, held):
    T, D = first.shape
    L = T // R
    FF = wu.shape[1]
    here = lambda width: pl.BlockSpec((L, width), lambda i, g, me: (at + i, 0))
    nio = len(held) + len(deps)
    np_ = len(parts)
    half = pl.BlockSpec((1, L // 2, D), lambda i, g, me: (i, 0, 0))
    return pl.pallas_call(
        functools.partial(ffn_kernel, nparts=np_, nio=nio),
        grid_spec=pltpu.PrefetchScalarGridSpec(
            num_scalar_prefetch=1,
            grid=(r, 1),
            in_specs=part_specs(parts, R, at, parts[0].shape[1], D) + [
                here(D), WHOLE, WHOLE, WHOLE, WHOLE,
            ] + [ANY] * nio,
            out_specs=[
                half, half, here(D), here(FF), here(FF),
                pl.BlockSpec((8, D), lambda i, g, me: (0, 0)), TICK3,
            ],
        ),
        out_shape=[
            shape_of((r, L // 2, D), BF16), shape_of((r, L // 2, D), BF16), shape_of((T, D), BF16),
            shape_of((T, FF), BF16), shape_of((T, FF), BF16), shape_of((8, D), F32),
            TICK,
        ],
        input_output_aliases={1 + np_ + 5 + len(deps) + i: 2 + i for i in range(len(held))},
        compiler_params=params(FFN_VMEM),
        cost_estimate=cost(4 * r * L * D * FF * 1.3, 4 * r * L * FF + 4 * D * FF),
        name="ffn",
    )(me, *arrays_of(parts), first, wu, bu, wd, vec, *deps, *held)


def down_grad_kernel(act_ref, g_ref, o_ref):
    o_ref[...] = mm(act_ref[...], g_ref[...], TN).astype(BF16)


def down_grad(act, g, tile):
    T, FF = act.shape
    D = g.shape[1]
    return pl.pallas_call(
        down_grad_kernel,
        grid=(FF // tile,),
        in_specs=[pl.BlockSpec((T, tile), lambda i: (0, i)), whole((T, D))],
        out_specs=rows_of(tile, D),
        out_shape=shape_of((FF, D), BF16),
        compiler_params=params(),
        cost_estimate=cost(2 * T * D * FF * 1.3, 2 * T * FF + 2 * D * FF),
        name="down_grad",
    )(act, g)


def ffn_back_kernel(
    g_ref, slope_ref, wu_ref, wd_ref, wo_ref, n_ref, s_ref, vec_ref, att_ref, il_ref, *rest,
    heads, hs,
):
    gpre_ref, gbr_ref, do_ref, de_ref, sums_ref, bsum_ref, tick_ref = rest[-7:]
    tick_ref[...] = jnp.zeros_like(tick_ref)
    g = g_ref[...]
    gp = (mm(g, wd_ref[...], NT) * slope_ref[...].astype(F32)).astype(BF16)
    gpre_ref[...] = gp
    gfirst = mm(gp, wu_ref[...], NT) + g.astype(F32)
    n1 = n_ref[0].astype(F32)
    e = gfirst * vec_ref[1:2, :]
    g1 = s_ref[0, :, 0:1] * (
        e - jnp.mean(e, -1, keepdims=True) - n1 * jnp.mean(e * n1, -1, keepdims=True)
    )
    gl = g1.astype(BF16)
    gbr_ref[0] = gl
    da = mm(wo_ref[...], gl, NT)
    for h in range(heads):
        il = il_ref[0, h : h + 1, :]
        piece = da[h * hs : (h + 1) * hs, :] * il
        do_ref[0, h * hs : (h + 1) * hs, :] = piece.astype(BF16)
        att = att_ref[0, h * hs : (h + 1) * hs, :].astype(F32)
        de_ref[0, h : h + 1, :] = jnp.sum(piece * att, axis=0, keepdims=True)

    @pl.when(pl.program_id(0) == 0)
    def _():
        sums_ref[...] = jnp.zeros_like(sums_ref)
        bsum_ref[...] = jnp.zeros_like(bsum_ref)

    sums_ref[0:1, :] += jnp.sum(gl.astype(F32), 0, keepdims=True)
    sums_ref[1:2, :] += jnp.sum(gfirst * n1, 0, keepdims=True)
    sums_ref[2:3, :] += jnp.sum(gfirst, 0, keepdims=True)
    bsum_ref[0:1, :] += jnp.sum(gp.astype(F32), 0, keepdims=True)


def ffn_back(at, r, g, slope, wu, wd, wo, n1, s1, vec, att, il, heads, hs, deps, held):
    T, D = g.shape
    FF = wu.shape[1]
    R, L = n1.shape[:2]
    flat = lambda width: pl.BlockSpec((L, width), lambda i: (at + i, 0))
    here = lambda shape: pl.BlockSpec((1,) + shape, lambda i: (at + i,) + (0,) * len(shape))
    extra = list(deps) + list(held)
    return pl.pallas_call(
        functools.partial(ffn_back_kernel, heads=heads, hs=hs),
        grid=(r,),
        in_specs=[
            flat(D), flat(FF), WHOLE, WHOLE, WHOLE, here((L, D)), here((L, 128)), WHOLE,
            here((D, L)), here((heads, L)),
        ] + [ANY] * len(extra),
        out_specs=[
            flat(FF), here((L, D)), here((D, L)), here((heads, L)),
            pl.BlockSpec((8, D), lambda i: (0, 0)), pl.BlockSpec((8, FF), lambda i: (0, 0)),
            TICK1,
        ],
        out_shape=[
            shape_of((T, FF), BF16), shape_of((R, L, D), BF16), shape_of((R, D, L), BF16),
            shape_of((R, heads, L), F32), shape_of((8, D), F32), shape_of((8, FF), F32),
            TICK,
        ],
        input_output_aliases={10 + len(deps) + i: i for i in range(len(held))},
        compiler_params=params(BACK_VMEM),
        cost_estimate=cost(4 * r * L * D * FF * 1.5, 4 * r * L * FF + 4 * D * FF),
        name="ffn_back",
    )(g, slope, wu, wd, wo, n1, s1, vec, att, il, *extra)


def up_grad_kernel(x_ref, g_ref, *rest):
    o_ref, tick_ref = rest[-2:]
    tick_ref[...] = jnp.zeros_like(tick_ref)
    o_ref[...] = mm(x_ref[...], g_ref[...], TN).astype(BF16)


def up_grad(x, g, tile, deps):
    T, D = x.shape
    FF = g.shape[1]
    return pl.pallas_call(
        up_grad_kernel,
        grid=(FF // tile,),
        in_specs=[whole((T, D)), pl.BlockSpec((T, tile), lambda i: (0, i))] + [ANY] * len(deps),
        out_specs=[pl.BlockSpec((D, tile), lambda i: (0, i)), TICK1],
        out_shape=[shape_of((D, FF + D), BF16), TICK],
        compiler_params=params(),
        cost_estimate=cost(2 * T * D * FF * 1.3, 2 * T * FF + 2 * D * FF),
        name="up_grad",
    )(x, g, *deps)


def out_grad_kernel(att_ref, g_ref, *rest):
    o_ref, tick_ref = rest[-2:]
    tick_ref[...] = jnp.zeros_like(tick_ref)
    total = mm(att_ref[0], g_ref[0])
    for r in range(1, att_ref.shape[0]):
        total = total + mm(att_ref[r], g_ref[r])
    o_ref[...] = total.astype(BF16)


def out_grad(att, g, deps, held):
    R, D, L = att.shape
    tile = D // 3
    last = held.shape[1] // D - 1
    return pl.pallas_call(
        out_grad_kernel,
        grid=(3,),
        in_specs=[pl.BlockSpec((R, tile, L), lambda i: (0, i, 0)), whole((R, L, D))]
        + [ANY] * (len(deps) + 1),
        out_specs=[pl.BlockSpec((tile, D), lambda i: (i, last)), TICK1],
        out_shape=[shape_of(held.shape, BF16), TICK],
        input_output_aliases={2 + len(deps): 0},
        compiler_params=params(),
        cost_estimate=cost(2 * R * L * D * D * 1.3, 4 * R * L * D),
        name="out_grad",
    )(att, g, *deps, held)


def attend_back_kernel(
    qkv_ref, p_ref, do_ref, de_ref, gone_ref, wt_ref, *rest, heads, hs, scale, group
):
    g_ref, lo_ref, hi_ref, sums_ref, tick_ref = rest[-5:]
    tick_ref[...] = jnp.zeros_like(tick_ref)
    D = heads * hs
    step = pl.program_id(1)
    for i in range(group):
        at = pl.multiple_of((step * group + i) * hs, hs)
        q = qkv_ref[0, pl.ds(at, hs), :]
        k = qkv_ref[0, pl.ds(D + at, hs), :]
        v = qkv_ref[0, pl.ds(2 * D + at, hs), :]
        do = do_ref[0, pl.ds(at, hs), :]
        p = p_ref[0, i]
        dp = mm(v, do, TN)
        ds = (p.astype(F32) * (dp - de_ref[0, 0, i : i + 1, :])).astype(BF16)
        g_ref[0, pl.ds(at, hs), :] = (mm(k, ds) * scale).astype(BF16)
        g_ref[0, pl.ds(D + at, hs), :] = mm(q, ds, NT).astype(BF16)
        g_ref[0, pl.ds(2 * D + at, hs), :] = mm(do, p, NT).astype(BF16)

    @pl.when(step == heads // group - 1)
    def _():
        g = g_ref[0]
        gin = (mm(g, wt_ref[...], TN) + gone_ref[0].astype(F32)).astype(BF16)
        half_len = gin.shape[0] // 2
        lo_ref[0] = gin[:half_len]
        hi_ref[0] = gin[half_len:]

        @pl.when(pl.program_id(0) == 0)
        def _():
            sums_ref[...] = jnp.zeros_like(sums_ref)

        ones = jnp.ones((8, g.shape[1]), BF16)
        sums_ref[...] += mm(ones, g, NT)


def attend_back(at, r, of, place, qkv, p, do, de, gone, wt, heads, hs, scale, group, deps, held):
    R, D3, L = qkv.shape
    D = D3 // 3
    here = lambda shape: pl.BlockSpec((1,) + shape, lambda i, g: (at + i,) + (0,) * len(shape))
    extra = list(deps) + [v for v in held if v is not None]
    aliases = {}
    for i, v in enumerate(held):
        if v is not None:
            aliases[6 + len(deps) + len(aliases)] = i
    half = pl.BlockSpec((1, L // 2, D), lambda i, g: (place + i, 0, 0))
    return pl.pallas_call(
        functools.partial(attend_back_kernel, heads=heads, hs=hs, scale=scale, group=group),
        grid=(r, heads // group),
        in_specs=[
            here((D3, L)), pl.BlockSpec((1, group, L, L), lambda i, g: (at + i, g, 0, 0)),
            here((D, L)), pl.BlockSpec((1, 1, group, L), lambda i, g: (at + i, g, 0, 0)),
            here((L, D)), WHOLE,
        ] + [ANY] * len(extra),
        out_specs=[
            here((D3, L)), half, half, pl.BlockSpec((8, D3), lambda i, g: (0, 0)),
            TICK2,
        ],
        out_shape=[
            shape_of((R, D3, L), BF16), shape_of((of, L // 2, D), BF16),
            shape_of((of, L // 2, D), BF16), shape_of((8, D3), F32), TICK,
        ],
        input_output_aliases=aliases,
        compiler_params=params(ATTEND_BACK_VMEM),
        cost_estimate=cost(r * (6 * L * D * D + 4 * 8 * heads * L * L * hs), r * 2 * heads * L * L),
        name="attend_back",
    )(qkv, p, do, de, gone, wt, *extra)


def qkv_grad_kernel(x_ref, g_ref, *rest):
    o_refs, tick_ref = rest[-3:-1], rest[-1]
    tick_ref[...] = jnp.zeros_like(tick_ref)
    total = mm(x_ref[0], g_ref[0], (((0,), (1,)), ((), ())))
    for r in range(1, x_ref.shape[0]):
        total = total + mm(x_ref[r], g_ref[r], (((0,), (1,)), ((), ())))
    half = pl.num_programs(0) // 2

    @pl.when(pl.program_id(0) < half)
    def _():
        o_refs[0][...] = total.astype(BF16)

    @pl.when(pl.program_id(0) >= half)
    def _():
        o_refs[1][...] = total.astype(BF16)


def qkv_grad(x, g, deps):
    R, L, D = x.shape
    D3 = g.shape[1]
    tile = 384
    half = D3 // 2 // tile
    return pl.pallas_call(
        qkv_grad_kernel,
        grid=(2 * half,),
        in_specs=[whole((R, L, D)), pl.BlockSpec((R, tile, L), lambda i: (0, i, 0))] + [ANY] * len(deps),
        out_specs=[
            pl.BlockSpec((D, tile), lambda i: (0, jnp.minimum(i, half - 1))),
            pl.BlockSpec((D, tile), lambda i: (0, jnp.maximum(i - half, 0))), TICK1,
        ],
        out_shape=[shape_of((D, D3 // 2), BF16), shape_of((D, D3 // 2), BF16), TICK],
        compiler_params=params(),
        cost_estimate=cost(2 * R * L * D * D3 * 1.3, 2 * R * L * (D + D3)),
        name="qkv_grad",
    )(x, g, *deps)


def bits_of(size):
    return [b for b in range(size.bit_length() - 1)]


def flip(x, axis, size, bit):
    return lax.ppermute(x, axis, [(i, i ^ (1 << bit)) for i in range(size)])


def my_bit(axis, bit):
    return (lax.axis_index(axis) >> bit) & 1


def pick(x, index, axis):
    return lax.dynamic_index_in_dim(x, index, axis, keepdims=False)


def late(x, tick):
    return x if tick is None else x + tick.reshape(()).astype(x.dtype)


class Rows:
    def __init__(self, x, axis, size):
        self.x, self.axis, self.size = x, axis, size
        self.bits = bits_of(size)
        self.R = x.shape[0] // size
        self.came = [[] for _ in self.bits]
        self.sent = []

    def own(self, bit, start, stop):
        cut = self.x.reshape((2,) * len(self.bits) + (self.R,) + self.x.shape[1:])[..., start:stop, :, :]
        held = [cut]
        for done in range(bit):
            mine = my_bit(self.axis, done)
            held = [pick(v, mine, v.ndim - 4) for v in held]
            got, base = self.find(done, start)
            held.append(got[..., start - base : stop - base, :, :])
        return held

    def find(self, bit, start):
        return [(v, base) for v, base in self.came[bit] if base <= start][-1]

    def come(self, bit, start, stop):
        held = self.own(bit, start, stop)
        mine = my_bit(self.axis, bit)
        send = [pick(v, 1 - mine, v.ndim - 4) for v in held]
        send = send[0] if len(send) == 1 else jnp.concatenate(send, -2)
        self.came[bit].append((flip(send, self.axis, self.size, bit), start))
        return send

    def all_high(self, start, stop):
        return [self.come(bit, start, stop) for bit in self.bits[1:]]

    def parts(self, start):
        out = [self.x]
        for bit in self.bits:
            got, base = self.find(bit, start)
            out.append((got.reshape((-1,) + got.shape[-3:]), base))
        return out


class Blocks:
    def __init__(self, axis, size):
        self.axis, self.size, self.chunks = axis, size, []

    def send(self, lo, hi):
        self.chunks.append((lo, flip(hi, self.axis, self.size, bits_of(self.size)[-1])))

    def result(self, tick=None):
        bits = bits_of(self.size)
        axis, size = self.axis, self.size
        join = lambda vs: jnp.concatenate(vs, 0) if len(vs) > 1 else vs[0]
        pieces = {0: join([lo for lo, _ in self.chunks]), 1 << bits[-1]: late(join([hi for _, hi in self.chunks]), tick)}
        for bit in reversed(bits[:-1]):
            names = list(pieces)
            half = pieces[0].shape[1] // 2
            came = flip(jnp.stack([pieces[name][:, half:] for name in names], 0), axis, size, bit)
            for i, name in enumerate(names):
                pieces[name | (1 << bit)] = came[i]
                pieces[name] = pieces[name][:, :half]
        R, B, D = pieces[0].shape
        me = lax.axis_index(axis)
        out = jnp.zeros((size * R, B, D), BF16)
        for name, piece in pieces.items():
            out = lax.dynamic_update_slice_in_dim(out, piece, (me ^ name) * R, 0)
        return out


class Sum:
    def __init__(self, x, dp, seq, order):
        self.sizes = {"dp": dp, "seq": seq}
        self.left = [("dp", b) for b in reversed(bits_of(dp))] + [("seq", b) for b in reversed(bits_of(seq))]
        self.order = list(order)
        self.terms = [x.reshape((2,) * len(self.left) + (x.shape[0] // (dp * seq),) + x.shape[1:])]
        self.came = []

    def total(self, terms, tick):
        if len(terms) == 1:
            return terms[0]
        sum_ = terms[0].astype(F32) + terms[1].astype(F32)
        return (sum_ if tick is None else sum_ + tick.reshape(())).astype(BF16)

    def step(self, tick=None, split=1):
        name, bit = self.order.pop(0)
        axis = self.left.index((name, bit))
        self.left.pop(axis)
        mine = my_bit(name, bit)
        terms = self.terms
        if self.came:
            terms = terms + [self.came[0] if len(self.came) == 1 else jnp.concatenate(self.came, -1)]
        send = self.total([pick(term, 1 - mine, axis) for term in terms], tick)
        self.terms = [self.total([pick(term, mine, axis) for term in terms], tick)]
        width = send.shape[-1] // split
        sends = [send[..., i * width : (i + 1) * width] for i in range(split)] if split > 1 else [send]
        self.came = [flip(v, name, self.sizes[name], bit) for v in sends]
        return sends

    def result(self, tick=None):
        while self.order:
            self.step(tick)
        out = self.terms[0].astype(F32) + self.came[0].astype(F32)
        return out if tick is None else out + tick.reshape(())


def chunks_of(count, sizes):
    out, at = [], 0
    for size in sizes:
        stop = min(count, at + size)
        if stop > at:
            out.append((at, stop))
        at = stop
    return out + ([(at, count)] if at < count else [])


def shards(
    dp, seq, hidden_in, segment_ids, cluster_perm, w_qkv, bias_qv, w_out, bias_out, gain_attn,
    shift_attn, w_up, bias_up, w_down, bias_down, gain_ffn, shift_ffn, grad_out,
):
    row_count, block_len, D = hidden_in.shape
    heads = cluster_perm.shape[1]
    hs = D // heads
    L = segment_ids.shape[1]
    FF = w_up.shape[1]
    R = row_count // seq
    T = R * L
    group = 4
    scale = 1.0 / math.sqrt(hs)
    mine = lax.axis_index("seq")
    me = mine.reshape(1).astype(jnp.int32)

    hidden, gout = Rows(hidden_in, "seq", seq), Rows(grad_out, "seq", seq)
    halves = chunks_of(R, (R // 2,))
    hidden.come(0, 0, R)
    sent = [hidden.all_high(row, row + 1) for row in range(R)]
    gout_core = gout.come(0, 0, R)
    gout_sent = [gout.all_high(*half) for half in halves]

    bias = jnp.concatenate([bias_qv[:D], jnp.zeros((D,), F32), bias_qv[D:]])
    bias = jnp.broadcast_to(bias, (8, 3 * D))
    none = jnp.zeros((D,), F32)
    vec = jnp.stack([bias_out, gain_attn, shift_attn, bias_down, gain_ffn, shift_ffn, none, none])
    wt, bt, code = prepare(me, seq, w_qkv, bias, cluster_perm, segment_ids, group, sent[0])

    held = ()
    for row in range(R):
        deps = sent[row + 1] if row + 1 < R else []
        if row == min(1, R - 1):
            deps = deps + [gout_core]
        if row >= R - 2:
            deps = deps + gout_sent[min(row - R + 2, len(halves) - 1)]
        *held, tick = attend(
            me, hidden.parts(row), row, 1, R, code, wt, bt, w_out, vec, heads, hs, scale, group, deps, held
        )
    x, qkv, p, il, att, first, n1, s1 = held
    il = il.reshape(R, heads, L)
    first = first.reshape(T, D)

    held, out_blocks, sums_ffn = (), Blocks("seq", seq), []
    for start, stop in halves:
        lo, hi, *held, sums, tick = ffn(
            me, first, gout.parts(start), start, stop - start, R, w_up, bias_up.reshape(1, -1), w_down,
            vec, [], held,
        )
        out_blocks.send(lo, hi)
        sums_ffn.append(sums)
    gffn, act, slope = held

    low = [("dp", b) for b in bits_of(dp)]
    high = [("seq", b) for b in bits_of(seq)[1:]]
    core = [("seq", 0)]
    turned = low[1:2] + low[:1] + high + low[2:]

    d_down = down_grad(act, gffn, 512)
    down = Sum(d_down, dp, seq, core + low + high)
    tick, held, sums_attn, sums_up = None, (), [], []
    for i, (start, stop) in enumerate(halves):
        deps = down.step(tick)
        *held, sums1, sums2, tick = ffn_back(
            start, stop - start, gffn, slope, w_up, w_down, w_out, n1, s1, vec, att, il, heads, hs,
            deps, held,
        )
        tick = join(tick, *down.came)
        sums_attn.append(sums1)
        sums_up.append(sums2)
    gpre, gbr, do, de = held
    deps = down.step(tick)
    d_up, tick = up_grad(first, gpre, 512, deps)
    d_up, tick = out_grad(att, gbr, [], d_up)
    up = Sum(d_up, dp, seq, core + low + high)
    tick = join(tick, *down.came)
    deps = down.step(tick) + up.step()
    de = de.reshape(R, heads // group, group, L)
    g, in_blocks, sums_qkv = None, Blocks("seq", seq), []
    for start, stop in halves:
        lo = hi = None
        for row in range(start, stop):
            if row == 1:
                tick = join(tick, *down.came, *up.came)
                last = down.step(tick) if len(down.order) == 1 else []
                sends = up.step(tick, 2)
                deps = last + sends[:1]
            elif row == 2:
                tick = join(tick, *down.came, up.came[0])
                deps = sends[1:]
            elif row == 3:
                tick = join(tick, *up.came)
                deps = up.step(tick)
            elif row:
                deps = []
            g, lo, hi, sums, tick = attend_back(
                row, 1, stop - start, row - start, qkv, p, do, de, gbr, wt, heads, hs, scale, group,
                deps, (g, lo, hi),
            )
            sums_qkv.append(sums)
        in_blocks.send(lo, hi)
    if R > 3:
        tick = join(tick, *up.came, *[came for _, came in in_blocks.chunks[:1]])
    d_qkv0, d_qkv1, tick = qkv_grad(x, g, up.step(tick))
    qkv0 = Sum(d_qkv0, dp, seq, core + low + high)

    n = dp * seq
    add = lambda vs: late(functools.reduce(jnp.add, vs), tick)
    sums_qkv, sums_attn, sums_up, sums_ffn = add(sums_qkv), add(sums_attn), add(sums_up), add(sums_ffn)
    small = [
        jnp.concatenate([sums_qkv[0, :D], sums_qkv[0, 2 * D :]]),
        sums_attn[0], sums_attn[1], sums_attn[2], sums_up[0], sums_ffn[0], sums_ffn[1], sums_ffn[2],
    ]
    per = [v.size // n for v in small]
    packed = jnp.concatenate([v.reshape(n, -1) for v in small], -1)
    lanes = 128 * -(-packed.shape[1] // (128 * (D // n)))
    packed = jnp.pad(packed, ((0, 0), (0, lanes * (D // n) - packed.shape[1])))
    packed = packed.reshape(D, lanes).astype(BF16)

    qkv1 = Sum(jnp.concatenate([d_qkv1, packed], 1), dp, seq, core + turned)
    while qkv0.order or qkv1.order or up.order:
        for s in (qkv0, qkv1, up):
            if s.order:
                s.step()
    grad_in = in_blocks.result(tick)
    out_hidden = out_blocks.result(tick)
    r_down, r_up, r_qkv0, r_qkv1 = down.result(tick), up.result(tick), qkv0.result(), qkv1.result()
    vec = r_qkv1[:, 3 * D // 2 :].reshape(-1)
    cuts, at = [], 0
    for width in per:
        cuts.append(vec[at : at + width])
        at += width
    b_qv, b_out, g_attn, s_attn, b_up, b_down, g_ffn, s_ffn = cuts
    return (
        out_hidden, grad_in, jnp.concatenate([r_qkv0, r_qkv1[:, : 3 * D // 2]], 1), b_qv,
        r_up[:, FF:], b_out, g_attn, s_attn, r_up[:, :FF], b_up, r_down, b_down, g_ffn, s_ffn,
    )


def solution(mesh):
    tok = P("dp", "seq", None)
    both = ("dp", "seq")
    return jax.shard_map(
        functools.partial(shards, mesh.shape["dp"], mesh.shape["seq"]),
        mesh=mesh,
        in_specs=(tok, P("dp", None), P("dp", None, None)) + (P(),) * 12 + (tok,),
        out_specs=(
            tok, tok, P(both, None), P(both), P(both, None), P(both), P(both), P(both),
            P(both, None), P(both), P(both, None), P(both), P(both), P(both),
        ),
        check_vma=False,
    )
```

```python
import functools
import math

import jax
import jax.numpy as jnp
from jax import lax
from jax.experimental import pallas as pl
from jax.experimental.pallas import tpu as pltpu
from jax.sharding import PartitionSpec as P

CL = 128
DOCS = 3
CODES = 16
NORM_EPS = 1e-05
BIG = 2.0**50
F32 = jnp.float32
BF16 = jnp.bfloat16
NN = (((1,), (0,)), ((), ()))
NT = (((1,), (1,)), ((), ()))
TN = (((0,), (0,)), ((), ()))
MIB = 2**20
VMEM = 32 * MIB
ATTEND_VMEM = 32 * MIB
FFN_VMEM = 44 * MIB
BACK_VMEM = 44 * MIB
ATTEND_BACK_VMEM = 32 * MIB
WHOLE = pl.BlockSpec(memory_space=pltpu.VMEM)
TICK = jax.ShapeDtypeStruct((1, 1), jnp.float32)
TICK1 = pl.BlockSpec((1, 1), lambda i: (0, 0))
TICK2 = pl.BlockSpec((1, 1), lambda i, g: (0, 0))
TICK3 = pl.BlockSpec((1, 1), lambda i, g, me: (0, 0))
ANY = pl.BlockSpec(memory_space=pl.ANY)


def mm(a, b, dims=NN):
    return lax.dot_general(a, b, dims, preferred_element_type=F32)


def far(*arrays):
    return [pltpu.with_memory_space_constraint(v, pltpu.HBM) for v in arrays]


def whole(shape):
    return pl.BlockSpec(shape, lambda i: (0,) * len(shape), pipeline_mode=pl.Buffered(1))


def lead(shape):
    return pl.BlockSpec((1,) + shape, lambda i: (i,) + (0,) * len(shape))


def rows_of(tile, width):
    return pl.BlockSpec((tile, width), lambda i: (i, 0))


def shape_of(shape, dtype):
    return pltpu.HBM(shape, dtype)


def params(limit=VMEM):
    return pltpu.CompilerParams(vmem_limit_bytes=limit)


def cost(flops, nbytes):
    return pl.CostEstimate(flops=int(flops), bytes_accessed=int(nbytes), transcendentals=0)


def part_specs(parts, R, at, block_len, D):
    own = pl.BlockSpec((1, block_len, D), lambda i, g, me: (me[0] * R + at + i, 0, 0))
    specs = [own]
    for bit, (part, base) in enumerate(parts[1:]):
        shape = (1, 1) + part.shape[2:]
        place = lambda bit, base, i, g, me: (me[0] >> (bit + 1), at + i - base, 0, 0)
        specs.append(pl.BlockSpec(shape, functools.partial(place, bit, base)))
    return specs


def arrays_of(parts):
    return [parts[0]] + [part for part, _ in parts[1:]]


def merge(refs):
    return jnp.concatenate([refs[0][0]] + [ref[0, 0] for ref in refs[1:]], 0)


def attend_kernel(me_ref, *refs, nparts, heads, hs, group, scale, nio):
    parts, (code_ref, wt_ref, bt_ref, wo_ref, vec_ref) = refs[:nparts], refs[nparts : nparts + 5]
    x_ref, qkv_ref, p_ref, il_ref, att_ref, first_ref, n_ref, s_ref, tick_ref = refs[nparts + 5 + nio :]
    tick_ref[...] = jnp.zeros_like(tick_ref)
    D = heads * hs
    L = x_ref.shape[1]
    step = pl.program_id(1)

    @pl.when(step == 0)
    def _():
        x_ref[0] = merge(parts)
        f = mm(wt_ref[...], x_ref[0], NT) + bt_ref[:, 0:1]
        qkv_ref[0, :D, :] = (f[:D].astype(BF16).astype(F32) * scale).astype(BF16)
        qkv_ref[0, D:, :] = f[D:].astype(BF16)

    it = lax.broadcasted_iota(jnp.int32, (CODES, L), 0)
    for i in range(group):
        at = pl.multiple_of((step * group + i) * hs, hs)
        q = qkv_ref[0, pl.ds(at, hs), :]
        k = qkv_ref[0, pl.ds(D + at, hs), :]
        v = qkv_ref[0, pl.ds(2 * D + at, hs), :]
        same = it == code_ref[0, 0, i : i + 1, :]
        qa = jnp.concatenate([q, jnp.where(same, BIG, 0.0).astype(BF16)], 0)
        ka = jnp.concatenate([k, jnp.where(same, 0.0, -BIG).astype(BF16)], 0)
        s = mm(ka, qa, TN)
        e = jnp.exp(s - jnp.max(s, axis=0, keepdims=True))
        il = 1.0 / jnp.sum(e, axis=0, keepdims=True)
        p = e.astype(BF16)
        p_ref[0, i] = p
        il_ref[0, 0, i : i + 1, :] = il
        att_ref[0, pl.ds(at, hs), :] = (mm(v, p) * il).astype(BF16)

    @pl.when(step == heads // group - 1)
    def _():
        v1 = x_ref[0].astype(F32) + mm(att_ref[0], wo_ref[...], TN) + vec_ref[0:1, :]
        c = v1 - jnp.mean(v1, -1, keepdims=True)
        s1 = lax.rsqrt(jnp.mean(c * c, -1, keepdims=True) + NORM_EPS)
        n1 = c * s1
        first_ref[0] = (n1 * vec_ref[1:2, :] + vec_ref[2:3, :]).astype(BF16)
        n_ref[0] = n1.astype(BF16)
        s_ref[0] = jnp.broadcast_to(s1, (L, 128))


def attend(me, parts, at, r, R, code, wt, bt, wo, vec, heads, hs, scale, group, deps, held):
    D = wo.shape[0]
    L = code.shape[-1]
    here = lambda shape: pl.BlockSpec((1,) + shape, lambda i, g, me: (at + i,) + (0,) * len(shape))
    grouped = lambda shape: pl.BlockSpec((1, 1) + shape, lambda i, g, me: (at + i, g, 0, 0))
    shapes = [
        shape_of((R, L, D), BF16),
        shape_of((R, 3 * D, L), BF16), shape_of((R, heads, L, L), BF16),
        shape_of((R, heads // group, group, L), F32), shape_of((R, D, L), BF16),
        shape_of((R, L, D), BF16), shape_of((R, L, D), BF16), shape_of((R, L, 128), F32),
        TICK,
    ]
    nio = len(held) + len(deps)
    np_ = len(parts)
    return pl.pallas_call(
        functools.partial(
            attend_kernel, nparts=np_, heads=heads, hs=hs, group=group, scale=scale, nio=nio
        ),
        grid_spec=pltpu.PrefetchScalarGridSpec(
            num_scalar_prefetch=1,
            grid=(r, heads // group),
            in_specs=part_specs(parts, R, at, parts[0].shape[1], D) + [
                grouped((group, L)), WHOLE, WHOLE, WHOLE, WHOLE,
            ] + [ANY] * nio,
            out_specs=[
                here((L, D)),
                here((3 * D, L)), pl.BlockSpec((1, group, L, L), lambda i, g, me: (at + i, g, 0, 0)),
                grouped((group, L)), here((D, L)), here((L, D)), here((L, D)), here((L, 128)),
                TICK3,
            ],
        ),
        out_shape=shapes,
        input_output_aliases={1 + np_ + 5 + len(deps) + i: i for i in range(len(held))},
        compiler_params=params(ATTEND_VMEM),
        cost_estimate=cost(r * (8 * L * D * D + 4 * 4 * heads * L * L * hs), r * 2 * heads * L * L),
        name="attend",
    )(me, *arrays_of(parts), code, wt, bt, wo, vec, *deps, *held)


def prepare_kernel(me_ref, w_ref, b_ref, perm_ref, seg_ref, *rest, seq):
    wt_ref, bt_ref, code_ref = rest[-3:]
    wt_ref[...] = w_ref[...].T
    bt_ref[...] = b_ref[...].T
    heads, _, L = perm_ref.shape
    R, _, group = code_ref.shape[:3]
    me = me_ref[0]
    block = L // seq
    high = lax.broadcasted_iota(jnp.int32, (8, L), 0)
    low = lax.broadcasted_iota(jnp.int32, (128, L), 0)
    member = (lax.broadcasted_iota(jnp.int32, (8, L), 1) // CL).astype(F32)
    for r in range(R):
        seg = seg_ref[pl.ds(me * R + r, 1), :]
        for bit in bits_of(seq):
            blocks = [seg[:, i * block : (i + 1) * block] for i in range(seq)]
            turned = jnp.concatenate([blocks[i ^ (1 << bit)] for i in range(seq)], 1)
            seg = jnp.where(((me >> bit) & 1) == 1, turned, seg)
        for h in range(heads):
            place = perm_ref[h, pl.ds(me * R + r, 1), :] ^ (me * block)
            a = jnp.where((place >> 7) == high, member, 0.0).astype(BF16)
            b = ((place & 127) == low).astype(BF16)
            table = mm(a, b, NT)
            row = jnp.concatenate([table[i : i + 1, :] for i in range(L // 128)], 1)
            code_ref[r, h // group, h % group : h % group + 1, :] = row.astype(jnp.int32) * DOCS + seg


def prepare(me, seq, w, b, perm, segs, group, deps):
    heads, rows, L = perm.shape
    R = rows // seq
    D, D3 = w.shape
    full = lambda shape: pl.BlockSpec(shape, lambda i, me: (0,) * len(shape))
    codes = (R, heads // group, group, L)
    return pl.pallas_call(
        functools.partial(prepare_kernel, seq=seq),
        grid_spec=pltpu.PrefetchScalarGridSpec(
            num_scalar_prefetch=1,
            grid=(1,),
            in_specs=[
                full((D, D3)), full((8, D3)), full(perm.shape),
                full(segs.shape),
            ] + [ANY] * len(deps),
            out_specs=[full((D3, D)), full((D3, 8)), full(codes)],
        ),
        out_shape=[
            jax.ShapeDtypeStruct((D3, D), BF16), jax.ShapeDtypeStruct((D3, 8), F32),
            jax.ShapeDtypeStruct(codes, jnp.int32),
        ],
        compiler_params=params(32 * MIB),
        cost_estimate=cost(4e9, 8e6),
        name="prepare",
    )(me, w, b, perm, segs, *deps)


def ffn_kernel(me_ref, *refs, nparts, nio):
    parts, (first_ref, wu_ref, bu_ref, wd_ref, vec_ref) = refs[:nparts], refs[nparts : nparts + 5]
    lo_ref, hi_ref, gffn_ref, act_ref, slope_ref, sums_ref, tick_ref = refs[nparts + 5 + nio :]
    tick_ref[...] = jnp.zeros_like(tick_ref)
    first = first_ref[...]
    u = mm(first, wu_ref[...]) + bu_ref[...]
    half = 0.5 * (1.0 + lax.erf(u * 0.7071067811865476))
    act = (u * half).astype(BF16)
    act_ref[...] = act
    slope_ref[...] = (half + u * jnp.exp(-0.5 * u * u) * 0.3989422804014327).astype(BF16)
    y = first.astype(F32) + mm(act, wd_ref[...]) + vec_ref[3:4, :]
    c = y - jnp.mean(y, -1, keepdims=True)
    s2 = lax.rsqrt(jnp.mean(c * c, -1, keepdims=True) + NORM_EPS)
    n2 = c * s2
    out = (n2 * vec_ref[4:5, :] + vec_ref[5:6, :]).astype(BF16)
    half_len = out.shape[0] // 2
    lo_ref[0] = out[:half_len]
    hi_ref[0] = out[half_len:]
    go = merge(parts).astype(F32)
    e = go * vec_ref[4:5, :]
    g2 = s2 * (e - jnp.mean(e, -1, keepdims=True) - n2 * jnp.mean(e * n2, -1, keepdims=True))
    gl = g2.astype(BF16)
    gffn_ref[...] = gl

    @pl.when(pl.program_id(0) == 0)
    def _():
        sums_ref[...] = jnp.zeros_like(sums_ref)

    sums_ref[0:1, :] += jnp.sum(gl.astype(F32), 0, keepdims=True)
    sums_ref[1:2, :] += jnp.sum(go * n2, 0, keepdims=True)
    sums_ref[2:3, :] += jnp.sum(go, 0, keepdims=True)


def ffn(me, first, parts, at, r, R, wu, bu, wd, vec, deps, held):
    T, D = first.shape
    L = T // R
    FF = wu.shape[1]
    here = lambda width: pl.BlockSpec((L, width), lambda i, g, me: (at + i, 0))
    nio = len(held) + len(deps)
    np_ = len(parts)
    half = pl.BlockSpec((1, L // 2, D), lambda i, g, me: (i, 0, 0))
    return pl.pallas_call(
        functools.partial(ffn_kernel, nparts=np_, nio=nio),
        grid_spec=pltpu.PrefetchScalarGridSpec(
            num_scalar_prefetch=1,
            grid=(r, 1),
            in_specs=part_specs(parts, R, at, parts[0].shape[1], D) + [
                here(D), WHOLE, WHOLE, WHOLE, WHOLE,
            ] + [ANY] * nio,
            out_specs=[
                half, half, here(D), here(FF), here(FF),
                pl.BlockSpec((8, D), lambda i, g, me: (0, 0)), TICK3,
            ],
        ),
        out_shape=[
            shape_of((r, L // 2, D), BF16), shape_of((r, L // 2, D), BF16), shape_of((T, D), BF16),
            shape_of((T, FF), BF16), shape_of((T, FF), BF16), shape_of((8, D), F32),
            TICK,
        ],
        input_output_aliases={1 + np_ + 5 + len(deps) + i: 2 + i for i in range(len(held))},
        compiler_params=params(FFN_VMEM),
        cost_estimate=cost(4 * r * L * D * FF * 1.3, 4 * r * L * FF + 4 * D * FF),
        name="ffn",
    )(me, *arrays_of(parts), *far(first), wu, bu, wd, vec, *deps, *held)


def by_core(total, place):
    rows, width = total.shape
    bits = len(place) + 1
    cube = total.reshape((2,) * bits + (rows >> bits, width))
    cube = cube.transpose((bits - 1,) + tuple(place) + (bits, bits + 1))
    return cube[0].reshape(rows // 2, width), cube[1].reshape(rows // 2, width)


def put_halves(me_ref, total, place, send_ref, keep_ref):
    even, odd = by_core(total, place)
    mine = me_ref[0] % 2 == 0
    send_ref[...] = jnp.where(mine, odd, even).astype(BF16)
    keep_ref[...] = jnp.where(mine, even, odd).astype(BF16)


def halves_of(me, total, place):
    even, odd = by_core(total, place)
    mine = me[0] % 2 == 0
    return jnp.where(mine, odd, even), jnp.where(mine, even, odd)


def places(dp, seq, order):
    names = [("dp", b) for b in reversed(bits_of(dp))] + [("seq", b) for b in reversed(bits_of(seq))]
    return [names.index(item) for item in order]


def splits(rows, n):
    return (rows // n) % 8 == 0


def down_grad_kernel(me_ref, act_ref, g_ref, *rest, place, ndep):
    outs = rest[ndep:]
    total = mm(act_ref[...], g_ref[...], TN)
    if len(outs) == 2:
        put_halves(me_ref, total, place, *outs)
    else:
        outs[0][...] = total.astype(BF16)


def down_grad(me, dp, seq, order, act, g, deps):
    T, FF = act.shape
    D = g.shape[1]
    n = dp * seq
    inside = splits(FF, n) and FF // dp % 128 == 0
    steps = dp if inside else 8
    tile = FF // steps
    place = places(dp, seq, order)
    inner = [p - len(bits_of(dp)) for p in place if p >= len(bits_of(dp))]
    turns = [bit for name, bit in order if name == "dp"]

    def at(i):
        where = 0
        for bit in turns:
            where = 2 * where + ((i >> bit) & 1)
        return (where, 0)

    res = pl.pallas_call(
        functools.partial(down_grad_kernel, place=inner, ndep=len(deps)),
        grid=(steps,),
        in_specs=[
            pl.BlockSpec(memory_space=pltpu.SMEM), pl.BlockSpec((T, tile), lambda i: (0, i)), whole((T, D)),
        ] + [ANY] * len(deps),
        out_specs=[pl.BlockSpec((tile // 2, D), at)] * 2 if inside else [rows_of(tile, D)],
        out_shape=[jax.ShapeDtypeStruct((FF // 2, D), BF16)] * 2 if inside else [shape_of((FF, D), BF16)],
        compiler_params=params(),
        cost_estimate=cost(2 * T * D * FF * 1.3, 2 * T * FF + 2 * D * FF),
        name="down_grad",
    )(me, *far(act, g), *deps)
    return res if inside else halves_of(me, res[0], place)


def ffn_back_kernel(
    g_ref, slope_ref, wu_ref, wd_ref, wo_ref, n_ref, s_ref, vec_ref, att_ref, il_ref, *rest,
    heads, hs,
):
    gpre_ref, gbr_ref, do_ref, de_ref, sums_ref, bsum_ref, tick_ref = rest[-7:]
    tick_ref[...] = jnp.zeros_like(tick_ref)
    g = g_ref[...]
    gp = (mm(g, wd_ref[...], NT) * slope_ref[...].astype(F32)).astype(BF16)
    gpre_ref[...] = gp
    gfirst = mm(gp, wu_ref[...], NT) + g.astype(F32)
    n1 = n_ref[0].astype(F32)
    e = gfirst * vec_ref[1:2, :]
    g1 = s_ref[0, :, 0:1] * (
        e - jnp.mean(e, -1, keepdims=True) - n1 * jnp.mean(e * n1, -1, keepdims=True)
    )
    gl = g1.astype(BF16)
    gbr_ref[0] = gl
    da = mm(wo_ref[...], gl, NT)
    for h in range(heads):
        group = il_ref.shape[2]
        i, j = h // group, h % group
        il = il_ref[0, i, j : j + 1, :]
        piece = da[h * hs : (h + 1) * hs, :] * il
        do_ref[0, h * hs : (h + 1) * hs, :] = piece.astype(BF16)
        att = att_ref[0, h * hs : (h + 1) * hs, :].astype(F32)
        de_ref[0, i, j : j + 1, :] = jnp.sum(piece * att, axis=0, keepdims=True)

    @pl.when(pl.program_id(0) == 0)
    def _():
        sums_ref[...] = jnp.zeros_like(sums_ref)
        bsum_ref[...] = jnp.zeros_like(bsum_ref)

    sums_ref[0:1, :] += jnp.sum(gl.astype(F32), 0, keepdims=True)
    sums_ref[1:2, :] += jnp.sum(gfirst * n1, 0, keepdims=True)
    sums_ref[2:3, :] += jnp.sum(gfirst, 0, keepdims=True)
    bsum_ref[0:1, :] += jnp.sum(gp.astype(F32), 0, keepdims=True)


def ffn_back(at, r, g, slope, wu, wd, wo, n1, s1, vec, att, il, heads, hs, deps, held):
    T, D = g.shape
    FF = wu.shape[1]
    R, L = n1.shape[:2]
    flat = lambda width: pl.BlockSpec((L, width), lambda i: (at + i, 0))
    here = lambda shape: pl.BlockSpec((1,) + shape, lambda i: (at + i,) + (0,) * len(shape))
    extra = list(deps) + list(held)
    return pl.pallas_call(
        functools.partial(ffn_back_kernel, heads=heads, hs=hs),
        grid=(r,),
        in_specs=[
            flat(D), flat(FF), WHOLE, WHOLE, WHOLE, here((L, D)), here((L, 128)), WHOLE,
            here((D, L)), here(il.shape[1:]),
        ] + [ANY] * len(extra),
        out_specs=[
            flat(FF), here((L, D)), here((D, L)), here(il.shape[1:]),
            pl.BlockSpec((8, D), lambda i: (0, 0)), pl.BlockSpec((8, FF), lambda i: (0, 0)),
            TICK1,
        ],
        out_shape=[
            shape_of((T, FF), BF16), shape_of((R, L, D), BF16), shape_of((R, D, L), BF16),
            shape_of(il.shape, F32), shape_of((8, D), F32), shape_of((8, FF), F32),
            TICK,
        ],
        input_output_aliases={10 + len(deps) + i: i for i in range(len(held))},
        compiler_params=params(BACK_VMEM),
        cost_estimate=cost(4 * r * L * D * FF * 1.5, 4 * r * L * FF + 4 * D * FF),
        name="ffn_back",
    )(*far(g, slope), wu, wd, wo, *far(n1, s1), vec, *far(att, il), *extra)


def up_out_grad_kernel(me_ref, x_ref, g_ref, att_ref, gbr_ref, *rest, place, ndep):
    outs, tick_ref = rest[ndep:-1], rest[-1]
    tick_ref[...] = jnp.zeros_like(tick_ref)
    last = pl.num_programs(0) - 1

    def put(total):
        if len(outs) == 2:
            put_halves(me_ref, total, place, *outs)
        else:
            outs[0][...] = total.astype(BF16)

    @pl.when(pl.program_id(0) < last)
    def _():
        put(mm(x_ref[...], g_ref[...], TN))

    @pl.when(pl.program_id(0) == last)
    def _():
        total = mm(att_ref[0], gbr_ref[0])
        for r in range(1, att_ref.shape[0]):
            total = total + mm(att_ref[r], gbr_ref[r])
        put(total)


def up_out_grad(me, dp, seq, order, x, g, att, gbr, deps):
    T, D = x.shape
    FF = g.shape[1]
    R, _, L = att.shape
    place = places(dp, seq, order)
    inside = splits(D, dp * seq)
    rows, count = (D // 2, 2) if inside else (D, 1)
    steps = FF // D
    *res, tick = pl.pallas_call(
        functools.partial(up_out_grad_kernel, place=place, ndep=len(deps)),
        grid=(steps + 1,),
        in_specs=[
            pl.BlockSpec(memory_space=pltpu.SMEM), whole((T, D)),
            pl.BlockSpec((T, D), lambda i: (0, jnp.minimum(i, steps - 1))), whole((R, D, L)),
            whole((R, L, D)),
        ] + [ANY] * len(deps),
        out_specs=[pl.BlockSpec((rows, D), lambda i: (0, i))] * count + [TICK1],
        out_shape=[jax.ShapeDtypeStruct((rows, FF + D), BF16)] * count + [TICK],
        compiler_params=params(),
        cost_estimate=cost(2 * T * D * (FF + D) * 1.3, 2 * T * FF + 2 * D * FF),
        name="up_out_grad",
    )(me, *far(x, g, att, gbr), *deps)
    return (res if inside else halves_of(me, res[0], place)), tick


def attend_back_kernel(
    qkv_ref, p_ref, do_ref, de_ref, gone_ref, wt_ref, *rest, heads, hs, scale, group
):
    g_ref, lo_ref, hi_ref, sums_ref, tick_ref = rest[-5:]
    tick_ref[...] = jnp.zeros_like(tick_ref)
    D = heads * hs
    step = pl.program_id(1)
    for i in range(group):
        at = pl.multiple_of((step * group + i) * hs, hs)
        q = qkv_ref[0, pl.ds(at, hs), :]
        k = qkv_ref[0, pl.ds(D + at, hs), :]
        v = qkv_ref[0, pl.ds(2 * D + at, hs), :]
        do = do_ref[0, pl.ds(at, hs), :]
        p = p_ref[0, i]
        dp = mm(v, do, TN)
        ds = (p.astype(F32) * (dp - de_ref[0, 0, i : i + 1, :])).astype(BF16)
        g_ref[0, pl.ds(at, hs), :] = (mm(k, ds) * scale).astype(BF16)
        g_ref[0, pl.ds(D + at, hs), :] = mm(q, ds, NT).astype(BF16)
        g_ref[0, pl.ds(2 * D + at, hs), :] = mm(do, p, NT).astype(BF16)

    @pl.when(step == heads // group - 1)
    def _():
        g = g_ref[0]
        gin = (mm(g, wt_ref[...], TN) + gone_ref[0].astype(F32)).astype(BF16)
        half_len = gin.shape[0] // 2
        lo_ref[0] = gin[:half_len]
        hi_ref[0] = gin[half_len:]

        @pl.when(pl.program_id(0) == 0)
        def _():
            sums_ref[...] = jnp.zeros_like(sums_ref)

        ones = jnp.ones((8, g.shape[1]), BF16)
        sums_ref[...] += mm(ones, g, NT)


def attend_back(at, r, of, place, qkv, p, do, de, gone, wt, heads, hs, scale, group, deps, held):
    R, D3, L = qkv.shape
    D = D3 // 3
    here = lambda shape: pl.BlockSpec((1,) + shape, lambda i, g: (at + i,) + (0,) * len(shape))
    extra = list(deps) + [v for v in held if v is not None]
    aliases = {}
    for i, v in enumerate(held):
        if v is not None:
            aliases[6 + len(deps) + len(aliases)] = i
    half = pl.BlockSpec((1, L // 2, D), lambda i, g: (place + i, 0, 0))
    return pl.pallas_call(
        functools.partial(attend_back_kernel, heads=heads, hs=hs, scale=scale, group=group),
        grid=(r, heads // group),
        in_specs=[
            here((D3, L)), pl.BlockSpec((1, group, L, L), lambda i, g: (at + i, g, 0, 0)),
            here((D, L)), pl.BlockSpec((1, 1, group, L), lambda i, g: (at + i, g, 0, 0)),
            here((L, D)), WHOLE,
        ] + [ANY] * len(extra),
        out_specs=[
            here((D3, L)), half, half, pl.BlockSpec((8, D3), lambda i, g: (0, 0)),
            TICK2,
        ],
        out_shape=[
            shape_of((R, D3, L), BF16), shape_of((of, L // 2, D), BF16),
            shape_of((of, L // 2, D), BF16), shape_of((8, D3), F32), TICK,
        ],
        input_output_aliases=aliases,
        compiler_params=params(ATTEND_BACK_VMEM),
        cost_estimate=cost(r * (6 * L * D * D + 4 * 8 * heads * L * L * hs), r * 2 * heads * L * L),
        name="attend_back",
    )(*far(qkv, p, do, de, gone), wt, *extra)


def pack(sums, n, lanes):
    total, at = jnp.zeros((n, lanes), F32), 0
    for terms in sums:
        v = functools.reduce(jnp.add, terms)
        W = v.shape[1]
        width = W // n
        owner = lax.broadcasted_iota(jnp.int32, (n, W), 0)
        place = lax.broadcasted_iota(jnp.int32, (n, W), 1)
        a = jnp.where((place >= owner * width) & (place < (owner + 1) * width), v, 0.0).astype(BF16)
        index = lax.broadcasted_iota(jnp.int32, (W, lanes), 0)
        start = ((index.astype(F32) + 0.5) * (1.0 / width)).astype(jnp.int32) * width
        b = (lax.broadcasted_iota(jnp.int32, (W, lanes), 1) == index - start + at).astype(BF16)
        total = total + mm(a, b)
        at += width
    return total


def qkv_grad_kernel(me_ref, x_ref, g_ref, *rest, spans, nsum, ndep, n, count, first, place):
    sums_refs, outs, pack_ref = rest[:nsum], rest[nsum + ndep : -2], rest[-1]
    rest[-2][...] = jnp.zeros_like(rest[-2])
    step, steps = pl.program_id(0), pl.num_programs(0)

    def put(total, which):
        refs = outs[which * count : (which + 1) * count]
        if count == 2:
            put_halves(me_ref, total, place[which], *refs)
        else:
            refs[0][...] = total.astype(BF16)

    @pl.when(step == 0)
    def _():
        sums = [
            [jnp.concatenate([sums_refs[i][row : row + 1, lo:hi] for lo, hi in cols], 1) for i in terms]
            for terms, row, cols in spans
        ]
        pack_ref[...] = pack(sums, n, pack_ref.shape[1])

    @pl.when(step < steps - 1)
    def _():
        total = mm(x_ref[0], g_ref[0], (((0,), (1,)), ((), ())))
        for r in range(1, x_ref.shape[0]):
            total = total + mm(x_ref[r], g_ref[r], (((0,), (1,)), ((), ())))

        @pl.when(step < first)
        def _():
            put(total, 0)

        @pl.when(step >= first)
        def _():
            put(total, 1)

    @pl.when(step == steps - 1)
    def _():
        D = x_ref.shape[2]
        lanes = pack_ref.shape[1]
        row = lax.broadcasted_iota(jnp.int32, (n, D // n, lanes), 1)
        total = jnp.where(row == 0, pack_ref[...][:, None, :], 0.0)
        put(total.reshape(D, lanes), 1)


def qkv_grad(me, dp, seq, orders, x, g, sums, spans, deps):
    R, L, D = x.shape
    D3 = g.shape[1]
    n = dp * seq
    place = [places(dp, seq, order) for order in orders]
    tile = D // 2
    real = D3 // tile
    first = (real + 2) // 2
    inside = splits(D, n)
    rows, count = (D // 2, 2) if inside else (D, 1)
    widths = (first * tile, (real + 1 - first) * tile)
    *res, tick = pl.pallas_call(
        functools.partial(
            qkv_grad_kernel, spans=spans, nsum=len(sums), ndep=len(deps), n=n, count=count,
            first=first, place=place,
        ),
        grid=(real + 1,),
        in_specs=[
            pl.BlockSpec(memory_space=pltpu.SMEM), whole((R, L, D)),
            pl.BlockSpec((R, tile, L), lambda i: (0, jnp.minimum(i, real - 1), 0)),
        ] + [whole(v.shape) for v in sums] + [ANY] * len(deps),
        out_specs=[pl.BlockSpec((rows, tile), lambda i: (0, jnp.minimum(i, first - 1)))] * count
        + [pl.BlockSpec((rows, tile), lambda i: (0, jnp.maximum(i - first, 0)))] * count + [TICK1],
        out_shape=[
            jax.ShapeDtypeStruct((rows, width), BF16) for width in widths for _ in range(count)
        ] + [TICK],
        scratch_shapes=[pltpu.VMEM((n, tile), F32)],
        compiler_params=params(),
        cost_estimate=cost(2 * R * L * D * D3 * 1.3, 2 * R * L * (D + D3)),
        name="qkv_grad",
    )(me, *far(x, g), *sums, *deps)
    pieces = [res[:count], res[count:]]
    return [piece if inside else halves_of(me, piece[0], at) for piece, at in zip(pieces, place)], tick


def bits_of(size):
    return [b for b in range(size.bit_length() - 1)]


def flip(x, axis, size, bit):
    return lax.ppermute(x, axis, [(i, i ^ (1 << bit)) for i in range(size)])


def my_bit(axis, bit):
    return (lax.axis_index(axis) >> bit) & 1


def pick(x, index, axis):
    return lax.dynamic_index_in_dim(x, index, axis, keepdims=False)


def late(x, tick):
    return x if tick is None else x + tick.reshape(()).astype(x.dtype)


def move_kernel(me_ref, *refs, count, ndep, copies):
    srcs, outs, sems = refs[:count], refs[count + ndep : -1], refs[-1]
    me = me_ref[0]
    started = []
    for i, (src, at, out, to) in enumerate(copies):
        copy = pltpu.make_async_copy(srcs[src].at[at(me)], outs[out].at[to(me)], sems.at[i])
        copy.start()
        started.append(copy)
    for copy in started:
        copy.wait()


def move(me, srcs, shapes, copies, deps=()):
    return pl.pallas_call(
        functools.partial(move_kernel, count=len(srcs), ndep=len(deps), copies=copies),
        in_specs=[pl.BlockSpec(memory_space=pltpu.SMEM)] + [ANY] * (len(srcs) + len(deps)),
        out_specs=[ANY] * len(shapes),
        out_shape=[jax.ShapeDtypeStruct(shape, BF16) for shape in shapes],
        scratch_shapes=[pltpu.SemaphoreType.DMA((len(copies),))],
        compiler_params=params(4 * MIB),
        cost_estimate=cost(1, 1),
        name="move",
    )(me, *srcs, *deps)


class Rows:
    def __init__(self, x, axis, size):
        self.x, self.axis, self.size = x, axis, size
        self.bits = bits_of(size)
        self.R, self.B, self.D = x.shape[0] // size, x.shape[1], x.shape[2]
        self.came = [[] for _ in self.bits]

    def find(self, bit, start):
        return [(v, base) for v, base in self.came[bit] if base <= start][-1]

    def plan(self, bit, start, stop, srcs, copies, out):
        r, B, R = stop - start, self.B, self.R
        lead = 1 << (len(self.bits) - 1 - bit)
        for high in range(lead):
            def owner(me, high=high):
                return (high << (bit + 1)) + (me ^ (1 << bit)) % (1 << (bit + 1))

            def own(me, owner=owner):
                return (pl.ds(owner(me) * R + start, r),)

            def place(lo, hi, high=high):
                return lambda me: (high, slice(None), pl.ds(lo, hi - lo))

            copies.append((len(srcs), own, out, place(0, B)))
            for done in range(bit):
                got, base = self.find(done, start)

                def theirs(me, owner=owner, done=done, base=base):
                    return (owner(me) >> (done + 1), pl.ds(start - base, r))

                copies.append((len(srcs) + 1 + done, theirs, out, place(B << done, B << (done + 1))))
        srcs.append(self.x)
        srcs.extend(self.find(done, start)[0] for done in range(bit))
        return (lead, r, B << bit, self.D)

    def send(self, bit, start, send):
        self.came[bit].append((flip(send, self.axis, self.size, bit), start))

    def parts(self, start):
        return [self.x] + [self.find(bit, start) for bit in self.bits]


def exchange(me, jobs, deps=()):
    srcs, copies, shapes = [], [], []
    for out, (rows, bit, start, stop) in enumerate(jobs):
        shapes.append(rows.plan(bit, start, stop, srcs, copies, out))
    sends = move(me, srcs, shapes, copies, deps)
    for (rows, bit, start, stop), send in zip(jobs, sends):
        rows.send(bit, start, send)
    return sends


class Blocks:
    def __init__(self, axis, size):
        self.axis, self.size, self.chunks = axis, size, []

    def send(self, lo, hi):
        self.chunks.append((lo, flip(hi, self.axis, self.size, bits_of(self.size)[-1])))

    def turn(self, me, tick):
        bits, axis, size = bits_of(self.size), self.axis, self.size
        half, D = self.chunks[0][0].shape[1:]
        self.R = R = sum(lo.shape[0] for lo, _ in self.chunks)
        self.pieces = pieces = {0: [], 1 << bits[-1]: []}
        at = 0
        for chunk in self.chunks:
            for name, v in zip(pieces, chunk):
                pieces[name].append((v, (), at, v.shape[0], 0))
            at += chunk[0].shape[0]
        for bit in reversed(bits[:-1]):
            half //= 2
            names = list(pieces)
            join = lambda vs: vs[0] if len(vs) == 1 else jnp.concatenate(vs, 0)
            send = jnp.stack([
                join([v[front + (slice(None), slice(token + half, token + 2 * half))] for v, front, _, _, token in pieces[name]])
                for name in names
            ], 0)
            send = late(send, tick)
            self.came = flip(send, axis, size, bit)
            for i, name in enumerate(names):
                pieces[name | (1 << bit)] = [(self.came, (i,), 0, R, 0)]
        self.shape = (size * R, half, D)

    def result(self, tick):
        half = self.shape[1]
        me = lax.axis_index(self.axis)
        out = jnp.zeros(self.shape, BF16)
        for name, sources in self.pieces.items():
            for v, front, row, rows, token in sources:
                piece = v[front + (slice(None), slice(token, token + half))]
                out = lax.dynamic_update_slice_in_dim(out, late(piece, tick), (me ^ name) * self.R + row, 0)
        return out


class Sum:
    def __init__(self, halves, dp, seq, order):
        self.sizes = {"dp": dp, "seq": seq}
        self.order = list(order)
        self.send, self.keep = halves

    def begin(self, send=None):
        self.go("seq", 0, [self.send if send is None else send])

    def go(self, name, bit, sends):
        self.came = [flip(v, name, self.sizes[name], bit) for v in sends]

    def result(self, tick=None):
        came = self.came[0] if len(self.came) == 1 else jnp.concatenate(self.came, -1)
        return late(self.keep.astype(F32) + came.astype(F32), tick)


def fold_kernel(me_ref, *refs, shapes, ndep, nthrough):
    nin = sum(2 + 2 * took for took, _ in shapes)
    ins, outs = refs[:nin], refs[nin + ndep + nthrough : len(refs) - nthrough]
    outs[-1][...] = jnp.zeros_like(outs[-1])
    for took, gave in shapes:
        keep, came, ins = ins[:2], (ins[2 : 2 + took], ins[2 + took : 2 + 2 * took]), ins[2 + 2 * took :]
        send_refs, keep_ref, outs = outs[:gave], outs[gave], outs[gave + 1 :]
        sums = []
        for base, parts in zip(keep, came):
            part = jnp.concatenate([ref[0] for ref in parts], 1) if took > 1 else parts[0][0]
            sums.append((base[0].astype(F32) + part.astype(F32)).astype(BF16))
        width = sums[0].shape[1] // gave
        for i, ref in enumerate(send_refs):
            ref[...] = sums[0][:, i * width : (i + 1) * width]
        keep_ref[...] = sums[1]


def fold(me, chains, deps=(), split=1, through=()):
    items = [chain.order.pop(0) for chain in chains]
    rows = [chain.keep.shape[0] // 2 for chain in chains]
    steps = max(s for s in (4, 2, 1) if s == 1 or all(r % (16 * s) == 0 for r in rows))
    ins, in_specs, out_specs, out_shape, shapes = [], [], [], [], []
    for chain, (name, bit), r in zip(chains, items, rows):
        tile, width = r // steps, chain.keep.shape[1]
        row = 0 if name == "dp" else 1
        gave = split if chain is chains[-1] else 1

        def half(other, width, row=row, bit=bit, tile=tile):
            return pl.BlockSpec(
                (1, tile, width), lambda i, me: (((me[row] >> bit) & 1) ^ other, i, 0)
            )

        view = lambda v, r=r: v.reshape(2, r, v.shape[1])
        ins += [view(chain.keep)] * 2 + [view(v) for v in chain.came] * 2
        in_specs += [half(1, width), half(0, width)]
        in_specs += [half(other, v.shape[1]) for other in (1, 0) for v in chain.came]
        out_specs += [pl.BlockSpec((tile, width // gave), lambda i, me: (i, 0))] * gave
        out_specs += [pl.BlockSpec((tile, width), lambda i, me: (i, 0))]
        out_shape += [jax.ShapeDtypeStruct((r, width // gave), BF16)] * gave
        out_shape += [jax.ShapeDtypeStruct((r, width), BF16)]
        shapes.append((len(chain.came), gave))
    res = pl.pallas_call(
        functools.partial(fold_kernel, shapes=shapes, ndep=len(deps), nthrough=len(through)),
        grid_spec=pltpu.PrefetchScalarGridSpec(
            num_scalar_prefetch=1,
            grid=(steps,),
            in_specs=in_specs + [ANY] * (len(deps) + len(through)),
            out_specs=out_specs + [pl.BlockSpec((1, 1), lambda i, me: (0, 0))] + [ANY] * len(through),
        ),
        out_shape=out_shape + [TICK] + [jax.ShapeDtypeStruct(v.shape, v.dtype) for v in through],
        input_output_aliases={
            1 + len(ins) + len(deps) + i: len(out_shape) + 1 + i for i in range(len(through))
        },
        compiler_params=params(16 * MIB),
        cost_estimate=cost(1, 1),
        name="fold",
    )(me, *ins, *deps, *through)
    tick, on = res[len(out_shape)], res[len(out_shape) + 1 :]
    sends = []
    for chain, (name, bit), (_, gave) in zip(chains, items, shapes):
        chain.go(name, bit, res[:gave])
        chain.keep = res[gave]
        sends += res[:gave]
        res = res[gave + 1 :]
    return (sends, tick, on) if through else (sends, tick)


def chunks_of(count, sizes):
    out, at = [], 0
    for size in sizes:
        stop = min(count, at + size)
        if stop > at:
            out.append((at, stop))
        at = stop
    return out + ([(at, count)] if at < count else [])


def shards(
    dp, seq, hidden_in, segment_ids, cluster_perm, w_qkv, bias_qv, w_out, bias_out, gain_attn,
    shift_attn, w_up, bias_up, w_down, bias_down, gain_ffn, shift_ffn, grad_out,
):
    row_count, block_len, D = hidden_in.shape
    heads = cluster_perm.shape[1]
    hs = D // heads
    L = segment_ids.shape[1]
    FF = w_up.shape[1]
    R = row_count // seq
    T = R * L
    group = 4
    scale = 1.0 / math.sqrt(hs)
    mine = lax.axis_index("seq")
    me = mine.reshape(1).astype(jnp.int32)
    both = jnp.stack([lax.axis_index("dp"), mine]).astype(jnp.int32)

    hidden, gout = Rows(hidden_in, "seq", seq), Rows(grad_out, "seq", seq)
    halves = chunks_of(R, (R // 2,))
    bits = bits_of(seq)
    exchange(me, [(hidden, 0, 0, 1)])
    for bit in bits[1:]:
        first_sent = exchange(me, [(hidden, bit, 0, 1)])
    rest = [(hidden, 0, 1, R)] if R > 1 else []
    exchange(me, rest + [(gout, 0, 0, R)], first_sent)

    bias = jnp.concatenate([bias_qv[:D], jnp.zeros((D,), F32), bias_qv[D:]])
    bias = jnp.broadcast_to(bias, (8, 3 * D))
    none = jnp.zeros((D,), F32)
    vec = jnp.stack([bias_out, gain_attn, shift_attn, bias_down, gain_ffn, shift_ffn, none, none])
    wt, bt, code = prepare(me, seq, w_qkv, bias, cluster_perm.transpose(1, 0, 2), segment_ids, group, first_sent)

    held, tick = (), None
    for row in range(R):
        jobs = [(hidden, row + 1, row + 2)] if row + 1 < R else [(gout, *halves[0])]
        deps = first_sent if tick is None else [tick]
        for bit in bits[1:]:
            deps = exchange(me, [(rows, bit, start, stop) for rows, start, stop in jobs], deps)
        *held, tick = attend(
            me, hidden.parts(row), row, 1, R, code, wt, bt, w_out, vec, heads, hs, scale, group, deps, held
        )
    x, qkv, p, il, att, first, n1, s1 = held
    first = first.reshape(T, D)

    held, out_blocks, sums_ffn = (), Blocks("seq", seq), []
    for i, (start, stop) in enumerate(halves):
        deps = [tick]
        for bit in bits[1:] if i + 1 < len(halves) else []:
            deps = exchange(me, [(gout, bit, *halves[i + 1])], deps)
        lo, hi, *held, sums, tick = ffn(
            me, first, gout.parts(start), start, stop - start, R, w_up, bias_up.reshape(1, -1), w_down,
            vec, deps, held,
        )
        out_blocks.send(lo, hi)
        sums_ffn.append(sums)
    gffn, act, slope = held

    low = [("dp", b) for b in bits_of(dp)]
    high = [("seq", b) for b in bits_of(seq)[1:]]
    turned = low[1:2] + low[:1] + high + low[2:]

    n = dp * seq
    came_out = [v for _, v in out_blocks.chunks]
    down = Sum(down_grad(me, dp, seq, low + high, act, gffn, came_out[:1]), dp, seq, low + high)
    down.begin()
    held, sums_attn, sums_up, deps = (), [], [], []
    for i, (start, stop) in enumerate(halves):
        *held, sums1, sums2, tick = ffn_back(
            start, stop - start, gffn, slope, w_up, w_down, w_out, n1, s1, vec, att, il, heads, hs,
            deps, held,
        )
        sums_attn.append(sums1)
        sums_up.append(sums2)
        deps, _ = fold(both, [down], [tick] + (came_out[1:] if i == 0 else []))
    gpre, gbr, do, de = held
    d_up, tick = up_out_grad(me, dp, seq, low + high, first, gpre, att, gbr, deps)
    up = Sum(d_up, dp, seq, low + high)
    deps, _, (send,) = fold(both, [down], [tick], 1, [up.send])
    up.begin(send)
    g, in_blocks, sums_qkv = None, Blocks("seq", seq), []
    for start, stop in halves:
        lo = hi = None
        for row in range(start, stop):
            if row == 1:
                sends, _ = fold(both, [down, up] if down.order else [up], [tick], 2)
                deps = sends[:-1]
            elif row == 2:
                deps = [sends[-1], up.came[0]]
            elif row == 3:
                deps, _ = fold(both, [up], [tick])
            elif row:
                deps = []
            g, lo, hi, sums, tick = attend_back(
                row, 1, stop - start, row - start, qkv, p, do, de, gbr, wt, heads, hs, scale, group,
                deps, (g, lo, hi),
            )
            sums_qkv.append(sums)
        in_blocks.send(lo, hi)
    deps, _ = fold(both, [up], [tick, in_blocks.chunks[0][1]])

    sums = sums_qkv + sums_attn + sums_up + sums_ffn
    kinds = [sums_qkv, sums_attn, sums_up, sums_ffn]
    firsts = [sum(len(v) for v in kinds[:i]) for i in range(4)]
    span = lambda kind, row, *cols: (range(firsts[kind], firsts[kind] + len(kinds[kind])), row, cols)
    spans = [
        span(0, 0, (0, D), (2 * D, 3 * D)), span(1, 0, (0, D)), span(1, 1, (0, D)), span(1, 2, (0, D)),
        span(2, 0, (0, FF)), span(3, 0, (0, D)), span(3, 1, (0, D)), span(3, 2, (0, D)),
    ]
    per = [sum(hi - lo for lo, hi in cols) // n for _, _, cols in spans]
    (d_qkv0, d_qkv1), tick = qkv_grad(me, dp, seq, [low + high, turned], x, g, sums, spans, deps)
    qkv0 = Sum(d_qkv0, dp, seq, low + high)
    qkv1 = Sum(d_qkv1, dp, seq, turned)
    while len(up.order) > 1:
        _, tick = fold(both, [up], [tick])
    _, tick, sends = fold(both, [up], [tick], 1, [qkv0.send, qkv1.send])
    qkv0.begin(sends[0])
    qkv1.begin(sends[1])
    while down.order:
        _, tick = fold(both, [down], [tick])
    out_blocks.turn(me, tick)
    stage = 0
    while qkv0.order:
        _, tick = fold(both, [qkv0, qkv1], [tick])
        if stage == 0:
            in_blocks.turn(me, tick)
            out_hidden = out_blocks.result(tick)
            r_down = down.result(tick)
        if stage == 1:
            grad_in = in_blocks.result(tick)
            r_up = up.result(tick)
        stage += 1
    r_qkv0, r_qkv1 = qkv0.result(), qkv1.result()
    split = 3 * D - r_qkv0.shape[1]
    vec = r_qkv1[0, split:]
    cuts, at = [], 0
    for width in per:
        cuts.append(vec[at : at + width])
        at += width
    b_qv, b_out, g_attn, s_attn, b_up, b_down, g_ffn, s_ffn = cuts
    return (
        out_hidden, grad_in, jnp.concatenate([r_qkv0, r_qkv1[:, :split]], 1), b_qv,
        r_up[:, FF:], b_out, g_attn, s_attn, r_up[:, :FF], b_up, r_down, b_down, g_ffn, s_ffn,
    )


def solution(mesh):
    tok = P("dp", "seq", None)
    both = ("dp", "seq")
    return jax.shard_map(
        functools.partial(shards, mesh.shape["dp"], mesh.shape["seq"]),
        mesh=mesh,
        in_specs=(tok, P("dp", None), P("dp", None, None)) + (P(),) * 12 + (tok,),
        out_specs=(
            tok, tok, P(both, None), P(both), P(both, None), P(both), P(both), P(both),
            P(both, None), P(both), P(both, None), P(both), P(both), P(both),
        ),
        check_vma=False,
    )
```

```python
import functools
import math

import jax
import jax.numpy as jnp
from jax import lax
from jax.experimental import pallas as pl
from jax.experimental.pallas import tpu as pltpu
from jax.sharding import PartitionSpec as P

CL = 128
DOCS = 3
CODES = 16
NORM_EPS = 1e-05
BIG = 2.0**50
NO_SHIFT = 40.0
F32 = jnp.float32
BF16 = jnp.bfloat16
NN = (((1,), (0,)), ((), ()))
NT = (((1,), (1,)), ((), ()))
TN = (((0,), (0,)), ((), ()))
MIB = 2**20
FFN_CUT = 2
BACK_CUT = 1
VMEM = 32 * MIB
ATTEND_VMEM = 28 * MIB
FFN_VMEM = 36 * MIB
BACK_VMEM = 28 * MIB
ATTEND_BACK_VMEM = 24 * MIB
WHOLE = pl.BlockSpec(memory_space=pltpu.VMEM)
TICK = jax.ShapeDtypeStruct((1, 1), jnp.float32)
TICK1 = pl.BlockSpec((1, 1), lambda i: (0, 0))
TICK2 = pl.BlockSpec((1, 1), lambda i, g: (0, 0))
TICK3 = pl.BlockSpec((1, 1), lambda i, g, me: (0, 0))
ANY = pl.BlockSpec(memory_space=pl.ANY)


def mm(a, b, dims=NN):
    return lax.dot_general(a, b, dims, preferred_element_type=F32)


def far(*arrays):
    return [pltpu.with_memory_space_constraint(v, pltpu.HBM) for v in arrays]


def whole(shape):
    return pl.BlockSpec(shape, lambda i: (0,) * len(shape), pipeline_mode=pl.Buffered(1))


def lead(shape):
    return pl.BlockSpec((1,) + shape, lambda i: (i,) + (0,) * len(shape))


def rows_of(tile, width):
    return pl.BlockSpec((tile, width), lambda i: (i, 0))


def shape_of(shape, dtype):
    return pltpu.HBM(shape, dtype)


def params(limit=VMEM):
    return pltpu.CompilerParams(vmem_limit_bytes=limit)


def cost(flops, nbytes):
    return pl.CostEstimate(flops=int(flops), bytes_accessed=int(nbytes), transcendentals=0)


def part_specs(parts, R, at, block_len, D):
    own = pl.BlockSpec((1, block_len, D), lambda i, g, me: (me[0] * R + at + i, 0, 0))
    specs = [own]
    for bit, (part, base) in enumerate(parts[1:]):
        shape = (1, 1) + part.shape[2:]
        place = lambda bit, base, i, g, me: (me[0] >> (bit + 1), at + i - base, 0, 0)
        specs.append(pl.BlockSpec(shape, functools.partial(place, bit, base)))
    return specs


def arrays_of(parts):
    return [parts[0]] + [part for part, _ in parts[1:]]


def merge(refs):
    return jnp.concatenate([refs[0][0]] + [ref[0, 0] for ref in refs[1:]], 0)


def attend_kernel(me_ref, *refs, nparts, heads, hs, group, scale, nio, row, ncarry):
    carried, refs = refs[:ncarry], refs[ncarry:]
    parts, (code_ref, wt_ref, bt_ref, wo_ref, vec_ref) = refs[:nparts], refs[nparts : nparts + 5]
    outs = refs[nparts + 5 + nio :]
    x_far, qkv_far, p_ref, il_ref, att_ref, first_ref, n_ref, s_ref, tick_ref = outs[:9]
    kept, (x_ref, qkv_ref, sems) = outs[9:-3], outs[-3:]
    tick_ref[...] = jnp.zeros_like(tick_ref)
    D = heads * hs
    L = x_ref.shape[1]
    step = pl.program_id(1)
    copies = [
        pltpu.make_async_copy(x_ref, x_far.at[pl.ds(row, 1)], sems.at[0]),
        pltpu.make_async_copy(qkv_ref, qkv_far.at[pl.ds(row, 1)], sems.at[1]),
    ] + [pltpu.make_async_copy(a, b, sems.at[2 + i]) for i, (a, b) in enumerate(zip(carried, kept))]

    @pl.when(step == 0)
    def _():
        x_ref[0] = merge(parts)
        f = mm(wt_ref[...], x_ref[0], NT) + bt_ref[:, 0:1]
        qkv_ref[0, :D, :] = (f[:D].astype(BF16).astype(F32) * scale).astype(BF16)
        qkv_ref[0, D:, :] = f[D:].astype(BF16)
        for copy in copies:
            copy.start()

    it = lax.broadcasted_iota(jnp.int32, (CODES, L), 0)

    def head(i):
        at = pl.multiple_of((step * group + i) * hs, hs)
        return [qkv_ref[0, pl.ds(j * D + at, hs), :] for j in range(3)]

    bound = jnp.zeros((1, 1), F32)
    for i in range(group):
        q, k, _ = head(i)
        norms = [
            jnp.max(jnp.sum(v.astype(F32) * v.astype(F32), axis=0, keepdims=True), axis=1, keepdims=True)
            for v in (q, k)
        ]
        bound = jnp.maximum(bound, norms[0] * norms[1])
    small = bound[0, 0] <= NO_SHIFT * NO_SHIFT

    def attend_group(shifted):
        for i in range(group):
            at = pl.multiple_of((step * group + i) * hs, hs)
            q, k, v = head(i)
            same = it == code_ref[0, 0, i : i + 1, :]
            qa = jnp.concatenate([q, jnp.where(same, BIG, 0.0).astype(BF16)], 0)
            ka = jnp.concatenate([k, jnp.where(same, 0.0, -BIG).astype(BF16)], 0)
            s = mm(ka, qa, TN)
            if shifted:
                s = s - jnp.max(s, axis=0, keepdims=True)
            p = jnp.exp(s).astype(BF16)
            p_ref[0, i] = p
            o = mm(jnp.concatenate([v, jnp.ones((16, L), BF16)], 0), p)
            il = 1.0 / o[hs : hs + 1]
            il_ref[0, 0, i : i + 1, :] = il
            att_ref[0, pl.ds(at, hs), :] = (o[:hs] * il).astype(BF16)

    @pl.when(small)
    def _():
        attend_group(False)

    @pl.when(jnp.logical_not(small))
    def _():
        attend_group(True)

    @pl.when(step == heads // group - 1)
    def _():
        v1 = x_ref[0].astype(F32) + mm(att_ref[0], wo_ref[...], TN) + vec_ref[0:1, :]
        c = v1 - jnp.mean(v1, -1, keepdims=True)
        s1 = lax.rsqrt(jnp.mean(c * c, -1, keepdims=True) + NORM_EPS)
        n1 = c * s1
        first_ref[0] = (n1 * vec_ref[1:2, :] + vec_ref[2:3, :]).astype(BF16)
        n_ref[0] = n1.astype(BF16)
        s_ref[0] = jnp.broadcast_to(s1, (L, 128))
        for copy in copies:
            copy.wait()


def attend(me, parts, at, R, code, wt, bt, wo, vec, heads, hs, scale, group, deps, held, carry=()):
    r = 1
    D = wo.shape[0]
    L = code.shape[-1]
    here = lambda shape: pl.BlockSpec((1,) + shape, lambda i, g, me: (at + i,) + (0,) * len(shape))
    grouped = lambda shape: pl.BlockSpec((1, 1) + shape, lambda i, g, me: (at + i, g, 0, 0))
    shapes = [
        shape_of((R, L, D), BF16),
        shape_of((R, 3 * D, L), BF16), shape_of((R, heads, L, L), BF16),
        shape_of((R, heads // group, group, L), F32), shape_of((R, D, L), BF16),
        shape_of((R, L, D), BF16), shape_of((R, L, D), BF16), shape_of((R, L, 128), F32),
        TICK,
    ]
    nio = len(held) + len(deps)
    np_ = len(parts)
    return pl.pallas_call(
        functools.partial(
            attend_kernel, nparts=np_, heads=heads, hs=hs, group=group, scale=scale, nio=nio,
            row=at, ncarry=len(carry),
        ),
        grid_spec=pltpu.PrefetchScalarGridSpec(
            num_scalar_prefetch=1,
            grid=(r, heads // group),
            in_specs=[ANY] * len(carry) + part_specs(parts, R, at, parts[0].shape[1], D) + [
                grouped((group, L)), WHOLE, WHOLE, WHOLE, WHOLE,
            ] + [ANY] * nio,
            out_specs=[
                ANY, ANY, pl.BlockSpec((1, group, L, L), lambda i, g, me: (at + i, g, 0, 0)),
                grouped((group, L)), here((D, L)), here((L, D)), here((L, D)), here((L, 128)),
                TICK3,
            ] + [WHOLE] * len(carry),
            scratch_shapes=[
                pltpu.VMEM((1, L, D), BF16), pltpu.VMEM((1, 3 * D, L), BF16),
                pltpu.SemaphoreType.DMA((2 + len(carry),)),
            ],
        ),
        out_shape=shapes + [pltpu.VMEM(v.shape, v.dtype) for v in carry],
        input_output_aliases={1 + len(carry) + np_ + 5 + len(deps) + i: i for i in range(len(held))},
        compiler_params=params(ATTEND_VMEM),
        cost_estimate=cost(r * (8 * L * D * D + 4 * 4 * heads * L * L * hs), r * 2 * heads * L * L),
        name="attend",
    )(me, *carry, *arrays_of(parts), code, wt, bt, wo, vec, *deps, *held)


def prepare_kernel(me_ref, w_ref, b_ref, perm_ref, seg_ref, *rest, seq):
    wt_ref, bt_ref, code_ref = rest[-3:]
    wt_ref[...] = w_ref[...].T
    bt_ref[...] = b_ref[...].T
    heads, _, L = perm_ref.shape
    R, _, group = code_ref.shape[:3]
    me = me_ref[0]
    block = L // seq
    high = lax.broadcasted_iota(jnp.int32, (8, L), 0)
    low = lax.broadcasted_iota(jnp.int32, (128, L), 0)
    member = (lax.broadcasted_iota(jnp.int32, (8, L), 1) // CL).astype(F32)
    for r in range(R):
        seg = seg_ref[pl.ds(me * R + r, 1), :]
        for bit in bits_of(seq):
            blocks = [seg[:, i * block : (i + 1) * block] for i in range(seq)]
            turned = jnp.concatenate([blocks[i ^ (1 << bit)] for i in range(seq)], 1)
            seg = jnp.where(((me >> bit) & 1) == 1, turned, seg)
        for h in range(heads):
            place = perm_ref[h, pl.ds(me * R + r, 1), :] ^ (me * block)
            a = jnp.where((place >> 7) == high, member, 0.0).astype(BF16)
            b = ((place & 127) == low).astype(BF16)
            table = mm(a, b, NT)
            row = jnp.concatenate([table[i : i + 1, :] for i in range(L // 128)], 1)
            code_ref[r, h // group, h % group : h % group + 1, :] = row.astype(jnp.int32) * DOCS + seg


def prepare(me, seq, w, b, perm, segs, group, deps):
    heads, rows, L = perm.shape
    R = rows // seq
    D, D3 = w.shape
    full = lambda shape: pl.BlockSpec(shape, lambda i, me: (0,) * len(shape))
    codes = (R, heads // group, group, L)
    return pl.pallas_call(
        functools.partial(prepare_kernel, seq=seq),
        grid_spec=pltpu.PrefetchScalarGridSpec(
            num_scalar_prefetch=1,
            grid=(1,),
            in_specs=[
                full((D, D3)), full((8, D3)), full(perm.shape),
                full(segs.shape),
            ] + [ANY] * len(deps),
            out_specs=[full((D3, D)), full((D3, 8)), full(codes)],
        ),
        out_shape=[
            jax.ShapeDtypeStruct((D3, D), BF16), jax.ShapeDtypeStruct((D3, 8), F32),
            jax.ShapeDtypeStruct(codes, jnp.int32),
        ],
        compiler_params=params(32 * MIB),
        cost_estimate=cost(4e9, 8e6),
        name="prepare",
    )(me, w, b, perm, segs, *deps)


def ffn_kernel(me_ref, *refs, nparts, nio):
    parts, (first_ref, wu_ref, bu_ref, wd_ref, vec_ref) = refs[:nparts], refs[nparts : nparts + 5]
    lo_ref, hi_ref, gffn_ref, act_ref, slope_ref, sums_ref, tick_ref = refs[nparts + 5 + nio :]
    tick_ref[...] = jnp.zeros_like(tick_ref)
    @pl.when(pl.program_id(0) == 0)
    def _():
        sums_ref[...] = jnp.zeros_like(sums_ref)

    go_all = merge(parts)
    tile = first_ref.shape[0]
    sub = tile // FFN_CUT
    for cut in range(FFN_CUT):
        here = slice(cut * sub, (cut + 1) * sub)
        first = first_ref[here, :]
        u = mm(first, wu_ref[...]) + bu_ref[...]
        half = 0.5 * (1.0 + lax.erf(u * 0.7071067811865476))
        act = (u * half).astype(BF16)
        act_ref[here, :] = act
        slope_ref[here, :] = (half + u * jnp.exp(-0.5 * u * u) * 0.3989422804014327).astype(BF16)
        y = first.astype(F32) + mm(act, wd_ref[...]) + vec_ref[3:4, :]
        c = y - jnp.mean(y, -1, keepdims=True)
        s2 = lax.rsqrt(jnp.mean(c * c, -1, keepdims=True) + NORM_EPS)
        n2 = c * s2
        out = (n2 * vec_ref[4:5, :] + vec_ref[5:6, :]).astype(BF16)
        if cut < FFN_CUT // 2:
            lo_ref[0, here, :] = out
        elif FFN_CUT > 1:
            hi_ref[0, cut * sub - tile // 2 : (cut + 1) * sub - tile // 2, :] = out
        else:
            lo_ref[0] = out[: tile // 2]
            hi_ref[0] = out[tile // 2 :]
        go = go_all[here].astype(F32)
        e = go * vec_ref[4:5, :]
        g2 = s2 * (e - jnp.mean(e, -1, keepdims=True) - n2 * jnp.mean(e * n2, -1, keepdims=True))
        gl = g2.astype(BF16)
        gffn_ref[here, :] = gl
        sums_ref[0:1, :] += jnp.sum(gl.astype(F32), 0, keepdims=True)
        sums_ref[1:2, :] += jnp.sum(go * n2, 0, keepdims=True)
        sums_ref[2:3, :] += jnp.sum(go, 0, keepdims=True)


def ffn(me, first, parts, at, r, R, wu, bu, wd, vec, deps, held):
    T, D = first.shape
    L = T // R
    FF = wu.shape[1]
    here = lambda width: pl.BlockSpec((L, width), lambda i, g, me: (at + i, 0))
    nio = len(held) + len(deps)
    np_ = len(parts)
    half = pl.BlockSpec((1, L // 2, D), lambda i, g, me: (i, 0, 0))
    return pl.pallas_call(
        functools.partial(ffn_kernel, nparts=np_, nio=nio),
        grid_spec=pltpu.PrefetchScalarGridSpec(
            num_scalar_prefetch=1,
            grid=(r, 1),
            in_specs=part_specs(parts, R, at, parts[0].shape[1], D) + [
                here(D), WHOLE, WHOLE, WHOLE, WHOLE,
            ] + [ANY] * nio,
            out_specs=[
                half, half, here(D), here(FF), here(FF),
                pl.BlockSpec((8, D), lambda i, g, me: (0, 0)), TICK3,
            ],
        ),
        out_shape=[
            shape_of((r, L // 2, D), BF16), shape_of((r, L // 2, D), BF16), shape_of((T, D), BF16),
            shape_of((T, FF), BF16), shape_of((T, FF), BF16), shape_of((8, D), F32),
            TICK,
        ],
        input_output_aliases={1 + np_ + 5 + len(deps) + i: 2 + i for i in range(len(held))},
        compiler_params=params(FFN_VMEM),
        cost_estimate=cost(4 * r * L * D * FF * 1.3, 4 * r * L * FF + 4 * D * FF),
        name="ffn",
    )(me, *arrays_of(parts), *far(first), wu, bu, wd, vec, *deps, *held)


def by_core(total, place):
    rows, width = total.shape
    bits = len(place) + 1
    cube = total.reshape((2,) * bits + (rows >> bits, width))
    cube = cube.transpose((bits - 1,) + tuple(place) + (bits, bits + 1))
    return cube[0].reshape(rows // 2, width), cube[1].reshape(rows // 2, width)


def put_halves(me_ref, total, place, send_ref, keep_ref):
    even, odd = by_core(total, place)
    mine = me_ref[0] % 2 == 0
    send_ref[...] = jnp.where(mine, odd, even).astype(BF16)
    keep_ref[...] = jnp.where(mine, even, odd).astype(BF16)


def halves_of(me, total, place):
    even, odd = by_core(total, place)
    mine = me[0] % 2 == 0
    return jnp.where(mine, odd, even), jnp.where(mine, even, odd)


def places(dp, seq, order):
    names = [("dp", b) for b in reversed(bits_of(dp))] + [("seq", b) for b in reversed(bits_of(seq))]
    return [names.index(item) for item in order]


def splits(rows, n):
    return (rows // n) % 8 == 0


def down_grad_kernel(me_ref, act_ref, g_ref, *rest, place, ndep):
    outs = rest[ndep:]
    total = mm(act_ref[...], g_ref[...], TN)
    if len(outs) == 2:
        put_halves(me_ref, total, place, *outs)
    else:
        outs[0][...] = total.astype(BF16)


def down_grad(me, dp, seq, order, act, g, deps):
    T, FF = act.shape
    D = g.shape[1]
    n = dp * seq
    inside = splits(FF, n) and FF // dp % 128 == 0
    steps = dp if inside else 8
    tile = FF // steps
    place = places(dp, seq, order)
    inner = [p - len(bits_of(dp)) for p in place if p >= len(bits_of(dp))]
    turns = [bit for name, bit in order if name == "dp"]

    def at(i):
        where = 0
        for bit in turns:
            where = 2 * where + ((i >> bit) & 1)
        return (where, 0)

    res = pl.pallas_call(
        functools.partial(down_grad_kernel, place=inner, ndep=len(deps)),
        grid=(steps,),
        in_specs=[
            pl.BlockSpec(memory_space=pltpu.SMEM), pl.BlockSpec((T, tile), lambda i: (0, i)), whole((T, D)),
        ] + [ANY] * len(deps),
        out_specs=[pl.BlockSpec((tile // 2, D), at)] * 2 if inside else [rows_of(tile, D)],
        out_shape=[shape_of((FF // 2, D), BF16), jax.ShapeDtypeStruct((FF // 2, D), BF16)] if inside else [shape_of((FF, D), BF16)],
        compiler_params=params(18 * MIB),
        cost_estimate=cost(2 * T * D * FF * 1.3, 2 * T * FF + 2 * D * FF),
        name="down_grad",
    )(me, *far(act, g), *deps)
    return res if inside else halves_of(me, res[0], place)


def ffn_back_kernel(
    g_ref, slope_ref, wu_ref, wd_ref, wo_ref, n_ref, s_ref, vec_ref, att_ref, il_ref, *rest,
    heads, hs,
):
    gpre_ref, gbr_ref, do_ref, de_ref, sums_ref, bsum_ref, tick_ref = rest[-7:]
    tick_ref[...] = jnp.zeros_like(tick_ref)
    @pl.when((pl.program_id(0) == 0) & (pl.program_id(1) == 0))
    def _():
        sums_ref[...] = jnp.zeros_like(sums_ref)
        bsum_ref[...] = jnp.zeros_like(bsum_ref)

    sub = g_ref.shape[0] // BACK_CUT
    for cut in range(BACK_CUT):
        here = slice(cut * sub, (cut + 1) * sub)
        g = g_ref[here, :]
        gp = (mm(g, wd_ref[...], NT) * slope_ref[here, :].astype(F32)).astype(BF16)
        gpre_ref[here, :] = gp
        gfirst = mm(gp, wu_ref[...], NT) + g.astype(F32)
        n1 = n_ref[0, here, :].astype(F32)
        e = gfirst * vec_ref[1:2, :]
        g1 = s_ref[0, here, 0:1] * (
            e - jnp.mean(e, -1, keepdims=True) - n1 * jnp.mean(e * n1, -1, keepdims=True)
        )
        gl = g1.astype(BF16)
        gbr_ref[0, here, :] = gl
        da = mm(wo_ref[...], gl, NT)
        group = il_ref.shape[2]
        for h in range(heads):
            i, j = h // group, h % group
            il = il_ref[0, i, j : j + 1, here]
            piece = da[h * hs : (h + 1) * hs, :] * il
            do_ref[0, h * hs : (h + 1) * hs, here] = piece.astype(BF16)
            att = att_ref[0, h * hs : (h + 1) * hs, here].astype(F32)
            de_ref[0, i, j : j + 1, here] = jnp.sum(piece * att, axis=0, keepdims=True)
        sums_ref[0:1, :] += jnp.sum(gl.astype(F32), 0, keepdims=True)
        sums_ref[1:2, :] += jnp.sum(gfirst * n1, 0, keepdims=True)
        sums_ref[2:3, :] += jnp.sum(gfirst, 0, keepdims=True)
        bsum_ref[0:1, :] += jnp.sum(gp.astype(F32), 0, keepdims=True)


def ffn_back(at, r, g, slope, wu, wd, wo, n1, s1, vec, att, il, heads, hs, deps, held):
    T, D = g.shape
    FF = wu.shape[1]
    R, L = n1.shape[:2]
    half = L // 2
    flat = lambda width: pl.BlockSpec((half, width), lambda i, g: (2 * (at + i) + g, 0))
    tokens = lambda width: pl.BlockSpec((1, half, width), lambda i, g: (at + i, g, 0))
    columns = lambda *lead: pl.BlockSpec(
        (1,) + lead + (half,), lambda i, g: (at + i,) + (0,) * len(lead) + (g,)
    )
    extra = list(deps) + list(held)
    return pl.pallas_call(
        functools.partial(ffn_back_kernel, heads=heads, hs=hs),
        grid=(r, 2),
        in_specs=[
            flat(D), flat(FF), WHOLE, WHOLE, WHOLE, tokens(D), tokens(128), WHOLE,
            columns(D), columns(*il.shape[1:3]),
        ] + [ANY] * len(extra),
        out_specs=[
            flat(FF), tokens(D), columns(D), columns(*il.shape[1:3]),
            pl.BlockSpec((8, D), lambda i, g: (0, 0)), pl.BlockSpec((8, FF), lambda i, g: (0, 0)),
            TICK2,
        ],
        out_shape=[
            shape_of((T, FF), BF16), shape_of((R, L, D), BF16), shape_of((R, D, L), BF16),
            shape_of(il.shape, F32), shape_of((8, D), F32), shape_of((8, FF), F32),
            TICK,
        ],
        input_output_aliases={10 + len(deps) + i: i for i in range(len(held))},
        compiler_params=params(BACK_VMEM),
        cost_estimate=cost(4 * r * L * D * FF * 1.5, 4 * r * L * FF + 4 * D * FF),
        name="ffn_back",
    )(*far(g, slope), wu, wd, wo, *far(n1, s1), vec, *far(att, il), *extra)


def up_out_grad_kernel(me_ref, x_ref, g_ref, att_far, gbr_far, *rest, place, ndep):
    outs, tick_ref, att_ref, gbr_ref, sems = rest[ndep:-4], rest[-4], rest[-3], rest[-2], rest[-1]
    tick_ref[...] = jnp.zeros_like(tick_ref)
    last = pl.num_programs(0) - 1

    def put(total):
        if len(outs) == 2:
            put_halves(me_ref, total, place, *outs)
        else:
            outs[0][...] = total.astype(BF16)

    copies = [
        pltpu.make_async_copy(att_far, att_ref, sems.at[0]),
        pltpu.make_async_copy(gbr_far, gbr_ref, sems.at[1]),
    ]

    @pl.when(pl.program_id(0) == 0)
    def _():
        for copy in copies:
            copy.start()

    @pl.when(pl.program_id(0) < last)
    def _():
        put(mm(x_ref[...], g_ref[...], TN))

    @pl.when(pl.program_id(0) == last)
    def _():
        for copy in copies:
            copy.wait()
        total = mm(att_ref[0], gbr_ref[0])
        for r in range(1, att_ref.shape[0]):
            total = total + mm(att_ref[r], gbr_ref[r])
        put(total)


def up_out_grad(me, dp, seq, order, x, g, att, gbr, deps):
    T, D = x.shape
    FF = g.shape[1]
    R, _, L = att.shape
    place = places(dp, seq, order)
    inside = splits(D, dp * seq)
    rows, count = (D // 2, 2) if inside else (D, 1)
    steps = FF // D
    *res, tick = pl.pallas_call(
        functools.partial(up_out_grad_kernel, place=place, ndep=len(deps)),
        grid=(steps + 1,),
        in_specs=[
            pl.BlockSpec(memory_space=pltpu.SMEM), whole((T, D)),
            pl.BlockSpec((T, D), lambda i: (0, jnp.minimum(i, steps - 1))), ANY, ANY,
        ] + [ANY] * len(deps),
        out_specs=[pl.BlockSpec((rows, D), lambda i: (0, i))] * count + [TICK1],
        out_shape=[jax.ShapeDtypeStruct((rows, FF + D), BF16)] * count + [TICK],
        scratch_shapes=[
            pltpu.VMEM((R, D, L), BF16), pltpu.VMEM((R, L, D), BF16), pltpu.SemaphoreType.DMA((2,)),
        ],
        compiler_params=params(),
        cost_estimate=cost(1, 1),
        name="up_out_grad",
    )(me, *far(x, g, att, gbr), *deps)
    return (res if inside else halves_of(me, res[0], place)), tick


def attend_back_kernel(
    qkv_ref, p_ref, do_ref, de_ref, gone_ref, wt_ref, *rest, heads, hs, scale, group
):
    g_out, lo_ref, hi_ref, sums_ref, tick_ref, g_ref = rest[-6:]
    tick_ref[...] = jnp.zeros_like(tick_ref)
    step = pl.program_id(1)
    for i in range(group):
        here = slice(i * hs, (i + 1) * hs)
        q, k, v = [qkv_ref[0, j, here, :] for j in range(3)]
        do = do_ref[0, here, :]
        p = p_ref[0, i]
        dp = mm(v, do, TN)
        ds = (p.astype(F32) * (dp - de_ref[0, 0, i : i + 1, :])).astype(BF16)
        grads = [mm(k, ds) * scale, mm(q, ds, NT), mm(do, p, NT)]
        for j in range(3):
            part = grads[j].astype(BF16)
            g_out[0, j, here, :] = part
            g_ref[j, step, here, :] = part

    @pl.when(step == heads // group - 1)
    def _():
        g = g_ref[...].reshape(3 * heads * hs, g_ref.shape[-1])
        gin = (mm(g, wt_ref[...], TN) + gone_ref[0].astype(F32)).astype(BF16)
        half_len = gin.shape[0] // 2
        lo_ref[0] = gin[:half_len]
        hi_ref[0] = gin[half_len:]

        @pl.when(pl.program_id(0) == 0)
        def _():
            sums_ref[...] = jnp.zeros_like(sums_ref)

        ones = jnp.ones((8, g.shape[1]), BF16)
        sums_ref[...] += mm(ones, g, NT)


def attend_back(at, r, of, place, qkv, p, do, de, gone, wt, heads, hs, scale, group, deps, held):
    R, D3, L = qkv.shape
    D = D3 // 3
    here = lambda shape: pl.BlockSpec((1,) + shape, lambda i, g: (at + i,) + (0,) * len(shape))
    extra = list(deps) + [v for v in held if v is not None]
    aliases = {}
    for i, v in enumerate(held):
        if v is not None:
            aliases[6 + len(deps) + len(aliases)] = i
    half = pl.BlockSpec((1, L // 2, D), lambda i, g: (place + i, 0, 0))
    heads_of = pl.BlockSpec((1, 3, group * hs, L), lambda i, g: (at + i, 0, g, 0))
    g, *rest = pl.pallas_call(
        functools.partial(attend_back_kernel, heads=heads, hs=hs, scale=scale, group=group),
        grid=(r, heads // group),
        in_specs=[
            heads_of, pl.BlockSpec((1, group, L, L), lambda i, g: (at + i, g, 0, 0)),
            pl.BlockSpec((1, group * hs, L), lambda i, g: (at + i, g, 0)),
            pl.BlockSpec((1, 1, group, L), lambda i, g: (at + i, g, 0, 0)),
            here((L, D)), WHOLE,
        ] + [ANY] * len(extra),
        out_specs=[heads_of, half, half, pl.BlockSpec((8, D3), lambda i, g: (0, 0)), TICK2],
        out_shape=[
            shape_of((R, 3, D, L), BF16), shape_of((of, L // 2, D), BF16),
            shape_of((of, L // 2, D), BF16), shape_of((8, D3), F32), TICK,
        ],
        scratch_shapes=[pltpu.VMEM((3, heads // group, group * hs, L), BF16)],
        input_output_aliases=aliases,
        compiler_params=params(ATTEND_BACK_VMEM),
        cost_estimate=cost(r * (6 * L * D * D + 4 * 8 * heads * L * L * hs), r * 2 * heads * L * L),
        name="attend_back",
    )(*far(qkv.reshape(R, 3, D, L), p, do, de, gone), wt, *extra)
    return [g, *rest]


def spots(widths):
    out, at = [], 0
    for width in widths:
        if at % 128 + width > 128:
            at = 128 * -(-at // 128)
        out.append(at)
        at += width
    return out


def pack(sums, n, lanes):
    widths = [terms[0].shape[1] // n for terms in sums]
    pieces = [jnp.zeros((n, 128), F32) for _ in range(lanes // 128)]
    for terms, width, at in zip(sums, widths, spots(widths)):
        v = functools.reduce(jnp.add, terms)
        W = v.shape[1]
        owner = lax.broadcasted_iota(jnp.int32, (n, W), 0)
        place = lax.broadcasted_iota(jnp.int32, (n, W), 1)
        a = jnp.where((place >= owner * width) & (place < (owner + 1) * width), v, 0.0).astype(BF16)
        index = lax.broadcasted_iota(jnp.int32, (W, 128), 0)
        start = ((index.astype(F32) + 0.5) * (1.0 / width)).astype(jnp.int32) * width
        b = (lax.broadcasted_iota(jnp.int32, (W, 128), 1) == index - start + at % 128).astype(BF16)
        pieces[at // 128] += mm(a, b)
    return jnp.concatenate(pieces, 1)


def qkv_grad_kernel(me_ref, x_ref, g_ref, *rest, spans, nsum, ndep, n, count, place):
    sums_refs, outs, pack_ref, xt_ref = rest[:nsum], rest[nsum + ndep : -3], rest[-2], rest[-1]
    rest[-3][...] = jnp.zeros_like(rest[-3])
    step, steps = pl.program_id(0), pl.num_programs(0)
    D = x_ref.shape[2]

    def put(total, which):
        refs = outs[which * count : (which + 1) * count]
        if count == 2:
            put_halves(me_ref, total, place[which], *refs)
        else:
            refs[0][...] = total.astype(BF16)

    @pl.when(step == 0)
    def _():
        for r in range(x_ref.shape[0]):
            xt_ref[r] = x_ref[r].T
        sums = [
            [jnp.concatenate([sums_refs[i][row : row + 1, lo:hi] for lo, hi in cols], 1) for i in terms]
            for terms, row, cols in spans
        ]
        pack_ref[...] = pack(sums, n, pack_ref.shape[1])

    total = mm(xt_ref[0], g_ref[0], NT)
    for r in range(1, x_ref.shape[0]):
        total = total + mm(xt_ref[r], g_ref[r], NT)

    @pl.when(step < steps - 1)
    def _():
        put(total, 0)

    @pl.when(step == steps - 1)
    def _():
        lanes = pack_ref.shape[1]
        row = lax.broadcasted_iota(jnp.int32, (n, D // n, lanes), 1)
        packed = jnp.where(row == 0, pack_ref[...][:, None, :], 0.0).reshape(D, lanes)
        put(jnp.concatenate([total, packed], 1), 1)


def qkv_grad(me, dp, seq, orders, x, g, sums, spans, deps):
    R, L, D = x.shape
    D3 = g.shape[1]
    n = dp * seq
    place = [places(dp, seq, order) for order in orders]
    real = D3 // D
    inside = splits(D, n)
    rows, count = (D // 2, 2) if inside else (D, 1)
    widths = ((real - 1) * D, D + D // 2)
    *res, tick = pl.pallas_call(
        functools.partial(
            qkv_grad_kernel, spans=spans, nsum=len(sums), ndep=len(deps), n=n, count=count, place=place
        ),
        grid=(real,),
        in_specs=[
            pl.BlockSpec(memory_space=pltpu.SMEM), whole((R, L, D)),
            pl.BlockSpec((R, D, L), lambda i: (0, i, 0)),
        ] + [whole(v.shape) for v in sums] + [ANY] * len(deps),
        out_specs=[pl.BlockSpec((rows, D), lambda i: (0, jnp.minimum(i, real - 2)))] * count
        + [pl.BlockSpec((rows, widths[1]), lambda i: (0, 0))] * count + [TICK1],
        out_shape=[
            jax.ShapeDtypeStruct((rows, width), BF16) for width in widths for _ in range(count)
        ] + [TICK],
        scratch_shapes=[pltpu.VMEM((n, D // 2), F32), pltpu.VMEM((R, D, L), BF16)],
        compiler_params=params(),
        cost_estimate=cost(2 * R * L * D * D3 * 1.3, 2 * R * L * (D + D3)),
        name="qkv_grad",
    )(me, *far(x, g), *sums, *deps)
    pieces = [res[:count], res[count:]]
    return [piece if inside else halves_of(me, piece[0], at) for piece, at in zip(pieces, place)], tick


def bits_of(size):
    return [b for b in range(size.bit_length() - 1)]


def flip(x, axis, size, bit):
    return lax.ppermute(x, axis, [(i, i ^ (1 << bit)) for i in range(size)])


def my_bit(axis, bit):
    return (lax.axis_index(axis) >> bit) & 1


def pick(x, index, axis):
    return lax.dynamic_index_in_dim(x, index, axis, keepdims=False)


def late(x, tick):
    return x if tick is None else x + tick.reshape(()).astype(x.dtype)


def move_kernel(me_ref, *refs, count, ndep, copies):
    srcs, outs, sems = refs[:count], refs[count + ndep : -1], refs[-1]
    me = me_ref[0]
    started = []
    for i, (src, at, out, to) in enumerate(copies):
        copy = pltpu.make_async_copy(srcs[src].at[at(me)], outs[out].at[to(me)], sems.at[i])
        copy.start()
        started.append(copy)
    for copy in started:
        copy.wait()


def move(me, srcs, shapes, copies, deps=()):
    return pl.pallas_call(
        functools.partial(move_kernel, count=len(srcs), ndep=len(deps), copies=copies),
        in_specs=[pl.BlockSpec(memory_space=pltpu.SMEM)] + [ANY] * (len(srcs) + len(deps)),
        out_specs=[ANY] * len(shapes),
        out_shape=[jax.ShapeDtypeStruct(shape, BF16) for shape in shapes],
        scratch_shapes=[pltpu.SemaphoreType.DMA((len(copies),))],
        compiler_params=params(4 * MIB),
        cost_estimate=cost(1, 1),
        name="move",
    )(me, *srcs, *deps)


def pass_on(arrays, after):
    return pl.pallas_call(
        lambda *refs: None,
        in_specs=[ANY] * (len(arrays) + len(after)),
        out_specs=[ANY] * len(arrays),
        out_shape=[jax.ShapeDtypeStruct(v.shape, v.dtype) for v in arrays],
        input_output_aliases={i: i for i in range(len(arrays))},
        compiler_params=params(4 * MIB),
        cost_estimate=cost(1, 1),
        name="pass_on",
    )(*arrays, *after)


class Rows:
    def __init__(self, x, axis, size):
        self.x, self.axis, self.size = x, axis, size
        self.bits = bits_of(size)
        self.R, self.B, self.D = x.shape[0] // size, x.shape[1], x.shape[2]
        self.came = [[] for _ in self.bits]

    def find(self, bit, start):
        return [(v, base) for v, base in self.came[bit] if base <= start][-1]

    def plan(self, bit, start, stop, srcs, copies, out):
        r, B, R = stop - start, self.B, self.R
        lead = 1 << (len(self.bits) - 1 - bit)
        for high in range(lead):
            def owner(me, high=high):
                return (high << (bit + 1)) + (me ^ (1 << bit)) % (1 << (bit + 1))

            def own(me, owner=owner):
                return (pl.ds(owner(me) * R + start, r),)

            def place(lo, hi, high=high):
                return lambda me: (high, slice(None), pl.ds(lo, hi - lo))

            copies.append((len(srcs), own, out, place(0, B)))
            for done in range(bit):
                got, base = self.find(done, start)

                def theirs(me, owner=owner, done=done, base=base):
                    return (owner(me) >> (done + 1), pl.ds(start - base, r))

                copies.append((len(srcs) + 1 + done, theirs, out, place(B << done, B << (done + 1))))
        srcs.append(self.x)
        srcs.extend(self.find(done, start)[0] for done in range(bit))
        return (lead, r, B << bit, self.D)

    def send(self, bit, start, send):
        self.came[bit].append((flip(send, self.axis, self.size, bit), start))

    def parts(self, start):
        return [self.x] + [self.find(bit, start) for bit in self.bits]


def gather(me, jobs, deps=()):
    srcs, copies, shapes = [], [], []
    for out, (rows, bit, start, stop) in enumerate(jobs):
        shapes.append(rows.plan(bit, start, stop, srcs, copies, out))
    return move(me, srcs, shapes, copies, deps)


def exchange(me, jobs, deps=()):
    sends = gather(me, jobs, deps)
    for (rows, bit, start, stop), send in zip(jobs, sends):
        rows.send(bit, start, send)
    return sends


class Blocks:
    def __init__(self, axis, size):
        self.axis, self.size, self.chunks = axis, size, []

    def send(self, lo, hi):
        self.chunks.append((lo, flip(hi, self.axis, self.size, bits_of(self.size)[-1])))

    def turn(self, me, tick):
        bits, axis, size = bits_of(self.size), self.axis, self.size
        half, D = self.chunks[0][0].shape[1:]
        self.R = R = sum(lo.shape[0] for lo, _ in self.chunks)
        self.pieces = pieces = {0: [], 1 << bits[-1]: []}
        at = 0
        for chunk in self.chunks:
            for name, v in zip(pieces, chunk):
                pieces[name].append((v, (), at, v.shape[0], 0))
            at += chunk[0].shape[0]
        for bit in reversed(bits[:-1]):
            half //= 2
            names = list(pieces)
            join = lambda vs: vs[0] if len(vs) == 1 else jnp.concatenate(vs, 0)
            send = jnp.stack([
                join([v[front + (slice(None), slice(token + half, token + 2 * half))] for v, front, _, _, token in pieces[name]])
                for name in names
            ], 0)
            send = late(send, tick)
            self.came = flip(send, axis, size, bit)
            for i, name in enumerate(names):
                pieces[name | (1 << bit)] = [(self.came, (i,), 0, R, 0)]
        self.shape = (size * R, half, D)

    def result(self, me, tick):
        half, D = self.shape[1:]
        entries = [(name,) + source for name, sources in self.pieces.items() for source in sources]
        block = functools.reduce(math.gcd, [rows for _, _, _, _, rows, _ in entries])
        starts = [sum(e[4] // block for e in entries[:i]) for i in range(len(entries) + 1)]
        R = self.R

        def source_spec(e, start, stop):
            _, v, front, _, _, _ = e
            lead = (1,) * len(front)

            def at(i, me):
                return front + (jnp.clip(i, start, stop - 1) - start, 0, 0)

            return pl.BlockSpec(lead + (block, half, D), at)

        def target(i, me):
            where = 0
            for (name, _, _, row, _, _), start, stop in zip(entries, starts, starts[1:]):
                here = ((me[0] ^ name) * R + row) // block + i - start
                where = jnp.where((i >= start) & (i < stop), here, where)
            return (where, 0, 0)

        def kernel(me_ref, *refs):
            i, out = pl.program_id(0), refs[-1]
            for ref, start, stop in zip(refs, starts, starts[1:]):
                @pl.when((i >= start) & (i < stop))
                def _(ref=ref):
                    out[...] = ref[...].reshape(out.shape)

        return pl.pallas_call(
            kernel,
            grid_spec=pltpu.PrefetchScalarGridSpec(
                num_scalar_prefetch=1,
                grid=(starts[-1],),
                in_specs=[source_spec(e, a, b) for e, a, b in zip(entries, starts, starts[1:])] + [ANY],
                out_specs=pl.BlockSpec((block, half, D), target),
            ),
            out_shape=shape_of(self.shape, BF16),
            compiler_params=params(16 * MIB),
            cost_estimate=cost(1, 1),
            name="place",
        )(me, *[e[1] for e in entries], tick)


class Sum:
    def __init__(self, halves, dp, seq, order):
        self.sizes = {"dp": dp, "seq": seq}
        self.order = list(order)
        self.send, self.keep = halves

    def begin(self, send=None):
        self.go("seq", 0, [self.send if send is None else send])

    def go(self, name, bit, sends):
        self.came = [flip(v, name, self.sizes[name], bit) for v in sends]

    def result(self, tick=None):
        came = self.came[0] if len(self.came) == 1 else jnp.concatenate(self.came, -1)
        return late(self.keep.astype(F32) + came.astype(F32), tick)


def fold_kernel(me_ref, *refs, shapes, ndep, nthrough):
    nin = sum(2 + 2 * took for took, _ in shapes)
    ins, outs = refs[:nin], refs[nin + ndep + nthrough : len(refs) - nthrough]
    outs[-1][...] = jnp.zeros_like(outs[-1])
    for took, gave in shapes:
        keep, came, ins = ins[:2], (ins[2 : 2 + took], ins[2 + took : 2 + 2 * took]), ins[2 + 2 * took :]
        send_refs, keep_ref, outs = outs[:gave], outs[gave], outs[gave + 1 :]
        sums = []
        for base, parts in zip(keep, came):
            part = jnp.concatenate([ref[0] for ref in parts], 1) if took > 1 else parts[0][0]
            sums.append((base[0].astype(F32) + part.astype(F32)).astype(BF16))
        width = sums[0].shape[1] // gave
        for i, ref in enumerate(send_refs):
            ref[...] = sums[0][:, i * width : (i + 1) * width]
        keep_ref[...] = sums[1]


def fold(me, chains, deps=(), split=1, through=()):
    items = [chain.order.pop(0) for chain in chains]
    rows = [chain.keep.shape[0] // 2 for chain in chains]
    steps = max(s for s in (4, 2, 1) if s == 1 or all(r % (16 * s) == 0 for r in rows))
    ins, in_specs, out_specs, out_shape, shapes = [], [], [], [], []
    for chain, (name, bit), r in zip(chains, items, rows):
        tile, width = r // steps, chain.keep.shape[1]
        row = 0 if name == "dp" else 1
        gave = split if chain is chains[-1] else 1

        def half(other, width, row=row, bit=bit, tile=tile):
            return pl.BlockSpec(
                (1, tile, width), lambda i, me: (((me[row] >> bit) & 1) ^ other, i, 0)
            )

        view = lambda v, r=r: v.reshape(2, r, v.shape[1])
        ins += [view(chain.keep)] * 2 + [view(v) for v in chain.came] * 2
        in_specs += [half(1, width), half(0, width)]
        in_specs += [half(other, v.shape[1]) for other in (1, 0) for v in chain.came]
        out_specs += [pl.BlockSpec((tile, width // gave), lambda i, me: (i, 0))] * gave
        out_specs += [pl.BlockSpec((tile, width), lambda i, me: (i, 0))]
        out_shape += [shape_of((r, width // gave), BF16)] * gave
        out_shape += [jax.ShapeDtypeStruct((r, width), BF16)]
        shapes.append((len(chain.came), gave))
    res = pl.pallas_call(
        functools.partial(fold_kernel, shapes=shapes, ndep=len(deps), nthrough=len(through)),
        grid_spec=pltpu.PrefetchScalarGridSpec(
            num_scalar_prefetch=1,
            grid=(steps,),
            in_specs=in_specs + [ANY] * (len(deps) + len(through)),
            out_specs=out_specs + [pl.BlockSpec((1, 1), lambda i, me: (0, 0))] + [ANY] * len(through),
        ),
        out_shape=out_shape + [TICK] + [jax.ShapeDtypeStruct(v.shape, v.dtype) for v in through],
        input_output_aliases={
            1 + len(ins) + len(deps) + i: len(out_shape) + 1 + i for i in range(len(through))
        },
        compiler_params=params(16 * MIB),
        cost_estimate=cost(1, 1),
        name="fold",
    )(me, *ins, *deps, *through)
    tick, on = res[len(out_shape)], res[len(out_shape) + 1 :]
    sends = []
    for chain, (name, bit), (_, gave) in zip(chains, items, shapes):
        chain.go(name, bit, res[:gave])
        chain.keep = res[gave]
        sends += res[:gave]
        res = res[gave + 1 :]
    return (sends, tick, on) if through else (sends, tick)


def chunks_of(count, sizes):
    out, at = [], 0
    for size in sizes:
        stop = min(count, at + size)
        if stop > at:
            out.append((at, stop))
        at = stop
    return out + ([(at, count)] if at < count else [])


def shards(
    dp, seq, hidden_in, segment_ids, cluster_perm, w_qkv, bias_qv, w_out, bias_out, gain_attn,
    shift_attn, w_up, bias_up, w_down, bias_down, gain_ffn, shift_ffn, grad_out,
):
    row_count, block_len, D = hidden_in.shape
    heads = cluster_perm.shape[1]
    hs = D // heads
    L = segment_ids.shape[1]
    FF = w_up.shape[1]
    R = row_count // seq
    T = R * L
    group = 4
    scale = 1.0 / math.sqrt(hs)
    mine = lax.axis_index("seq")
    me = mine.reshape(1).astype(jnp.int32)
    both = jnp.stack([lax.axis_index("dp"), mine]).astype(jnp.int32)

    hidden, gout = Rows(hidden_in, "seq", seq), Rows(grad_out, "seq", seq)
    halves = chunks_of(R, (R // 2,))
    bits = bits_of(seq)
    exchange(me, [(hidden, 0, 0, 1)])
    for bit in bits[1:]:
        first_sent = exchange(me, [(hidden, bit, 0, 1)])
    rest = [(hidden, 0, 1, R)] if R > 1 else []
    exchange(me, rest + [(gout, 0, 0, R)], first_sent)

    bias = jnp.concatenate([bias_qv[:D], jnp.zeros((D,), F32), bias_qv[D:]])
    bias = jnp.broadcast_to(bias, (8, 3 * D))
    none = jnp.zeros((D,), F32)
    vec = jnp.stack([bias_out, gain_attn, shift_attn, bias_down, gain_ffn, shift_ffn, none, none])
    wt, bt, code = prepare(me, seq, w_qkv, bias, cluster_perm.transpose(1, 0, 2), segment_ids, group, first_sent)

    jobs = [(hidden, row, row + 1) for row in range(1, R)] + [(gout, *half) for half in halves]
    early = len(bits) == 2
    if early:
        queue = list(zip(jobs, gather(me, [(rows, bits[-1], a, b) for rows, a, b in jobs], first_sent)))
    else:
        queue = [(job, None) for job in jobs]

    def launch(after):
        if not queue:
            return after
        (rows, start, stop), send = queue.pop(0)
        if early:
            (send,) = pass_on([send], after)
            rows.send(bits[-1], start, send)
            return [send]
        for bit in bits[1:]:
            after = exchange(me, [(rows, bit, start, stop)], after)
        return after

    held, tick = (), None
    for row in range(R):
        deps = launch(first_sent if tick is None else [tick])
        res = attend(
            me, hidden.parts(row), row, R, code, wt, bt, w_out, vec, heads, hs, scale, group, deps, held,
        )
        held, tick = res[:8], res[8]
    x, qkv, p, il, att, first, n1, s1 = held
    first = first.reshape(T, D)

    held, out_blocks, sums_ffn = (), Blocks("seq", seq), []
    for i, (start, stop) in enumerate(halves):
        deps = launch([tick])
        lo, hi, *held, sums, tick = ffn(
            me, first, gout.parts(start), start, stop - start, R, w_up, bias_up.reshape(1, -1), w_down,
            vec, deps, held,
        )
        out_blocks.send(lo, hi)
        sums_ffn.append(sums)
    gffn, act, slope = held

    low = [("dp", b) for b in bits_of(dp)]
    high = [("seq", b) for b in bits_of(seq)[1:]]
    turned = low[1:2] + low[:1] + high + low[2:]

    n = dp * seq
    came_out = [v for _, v in out_blocks.chunks]
    down = Sum(down_grad(me, dp, seq, low + high, act, gffn, came_out[:1]), dp, seq, low + high)
    down.begin()
    held, sums_attn, sums_up, deps = (), [], [], []
    for i, (start, stop) in enumerate(halves):
        *held, sums1, sums2, tick = ffn_back(
            start, stop - start, gffn, slope, w_up, w_down, w_out, n1, s1, vec, att, il, heads, hs,
            deps, held,
        )
        sums_attn.append(sums1)
        sums_up.append(sums2)
        deps = []
        if i == 0:
            deps, _ = fold(both, [down], [tick] + came_out[1:])
    gpre, gbr, do, de = held
    d_up, tick = up_out_grad(me, dp, seq, low + high, first, gpre, att, gbr, deps)
    up = Sum(d_up, dp, seq, low + high)
    deps, _, (send,) = fold(both, [down], [tick], 1, [up.send])
    up.begin(send)
    g, in_blocks, sums_qkv = None, Blocks("seq", seq), []
    for start, stop in halves:
        lo = hi = None
        for row in range(start, stop):
            if row == 1:
                sends, _ = fold(both, [down, up] if down.order else [up], [tick], 2)
                deps = sends[:-1]
            elif row == 2:
                deps = [sends[-1], up.came[0]]
                if down.order:
                    more, _ = fold(both, [down], [tick])
                    deps = deps + more
            elif row == 3:
                deps, _ = fold(both, [up], [tick])
            elif row:
                deps = []
            g, lo, hi, sums, tick = attend_back(
                row, 1, stop - start, row - start, qkv, p, do, de, gbr, wt, heads, hs, scale, group,
                deps, (g, lo, hi),
            )
            sums_qkv.append(sums)
        in_blocks.send(lo, hi)
    g = g.reshape(R, 3 * D, L)
    deps, _ = fold(both, [up], [tick, in_blocks.chunks[0][1]])

    sums = sums_qkv + sums_attn + sums_up + sums_ffn
    kinds = [sums_qkv, sums_attn, sums_up, sums_ffn]
    firsts = [sum(len(v) for v in kinds[:i]) for i in range(4)]
    span = lambda kind, row, *cols: (range(firsts[kind], firsts[kind] + len(kinds[kind])), row, cols)
    spans = [
        span(0, 0, (0, D), (2 * D, 3 * D)), span(1, 0, (0, D)), span(1, 1, (0, D)), span(1, 2, (0, D)),
        span(2, 0, (0, FF)), span(3, 0, (0, D)), span(3, 1, (0, D)), span(3, 2, (0, D)),
    ]
    per = [sum(hi - lo for lo, hi in cols) // n for _, _, cols in spans]
    (d_qkv0, d_qkv1), tick = qkv_grad(me, dp, seq, [low + high, turned], x, g, sums, spans, deps)
    qkv0 = Sum(d_qkv0, dp, seq, low + high)
    qkv1 = Sum(d_qkv1, dp, seq, turned)
    while len(up.order) > 1:
        _, tick = fold(both, [up], [tick])
    _, tick, sends = fold(both, [up], [tick] + [v for _, v in in_blocks.chunks[1:]], 1, [qkv0.send, qkv1.send])
    qkv0.begin(sends[0])
    qkv1.begin(sends[1])
    while down.order:
        _, tick = fold(both, [down], [tick])
    out_blocks.turn(me, tick)
    in_blocks.turn(me, tick)
    stage, done = 0, []
    while qkv0.order:
        _, tick = fold(both, [qkv0, qkv1], [tick] + done)
        done = []
        if stage == 0:
            out_hidden = out_blocks.result(me, tick)
            grad_in = in_blocks.result(me, tick)
            done = [out_hidden, grad_in]
        if stage == 1:
            r_down, r_up = down.result(tick), up.result(tick)
            done = [r_down, r_up]
        stage += 1
    r_qkv0, r_qkv1 = qkv0.result(), qkv1.result()
    split = 3 * D - r_qkv0.shape[1]
    vec = r_qkv1[0, split:]
    cuts = [vec[at : at + width] for at, width in zip(spots(per), per)]
    b_qv, b_out, g_attn, s_attn, b_up, b_down, g_ffn, s_ffn = cuts
    return (
        out_hidden, grad_in, jnp.concatenate([r_qkv0, r_qkv1[:, :split]], 1), b_qv,
        r_up[:, FF:], b_out, g_attn, s_attn, r_up[:, :FF], b_up, r_down, b_down, g_ffn, s_ffn,
    )


def solution(mesh):
    tok = P("dp", "seq", None)
    both = ("dp", "seq")
    return jax.shard_map(
        functools.partial(shards, mesh.shape["dp"], mesh.shape["seq"]),
        mesh=mesh,
        in_specs=(tok, P("dp", None), P("dp", None, None)) + (P(),) * 12 + (tok,),
        out_specs=(
            tok, tok, P(both, None), P(both), P(both, None), P(both), P(both), P(both),
            P(both, None), P(both), P(both, None), P(both), P(both), P(both),
        ),
        check_vma=False,
    )
```

```python
import functools
import math

import jax
import jax.numpy as jnp
from jax import lax
from jax.experimental import pallas as pl
from jax.experimental.pallas import tpu as pltpu
from jax.sharding import PartitionSpec as P

CL = 128
DOCS = 3
CODES = 16
NORM_EPS = 1e-05
BIG = 2.0**50
NO_SHIFT = 40.0
F32 = jnp.float32
BF16 = jnp.bfloat16
NN = (((1,), (0,)), ((), ()))
NT = (((1,), (1,)), ((), ()))
TN = (((0,), (0,)), ((), ()))
MIB = 2**20
FFN_CUT = 2
BACK_CUT = 1
VMEM = 32 * MIB
ATTEND_VMEM = 28 * MIB
FFN_VMEM = 36 * MIB
BACK_VMEM = 28 * MIB
ATTEND_BACK_VMEM = 24 * MIB
WHOLE = pl.BlockSpec(memory_space=pltpu.VMEM)
TICK = jax.ShapeDtypeStruct((1, 1), jnp.float32)
TICK1 = pl.BlockSpec((1, 1), lambda i: (0, 0))
TICK2 = pl.BlockSpec((1, 1), lambda i, g: (0, 0))
TICK3 = pl.BlockSpec((1, 1), lambda i, g, me: (0, 0))
ANY = pl.BlockSpec(memory_space=pl.ANY)


def mm(a, b, dims=NN):
    return lax.dot_general(a, b, dims, preferred_element_type=F32)


def far(*arrays):
    return [pltpu.with_memory_space_constraint(v, pltpu.HBM) for v in arrays]


def whole(shape):
    return pl.BlockSpec(shape, lambda i: (0,) * len(shape), pipeline_mode=pl.Buffered(1))


def lead(shape):
    return pl.BlockSpec((1,) + shape, lambda i: (i,) + (0,) * len(shape))


def rows_of(tile, width):
    return pl.BlockSpec((tile, width), lambda i: (i, 0))


def shape_of(shape, dtype):
    return pltpu.HBM(shape, dtype)


def params(limit=VMEM):
    return pltpu.CompilerParams(vmem_limit_bytes=limit)


def cost(flops, nbytes):
    return pl.CostEstimate(flops=int(flops), bytes_accessed=int(nbytes), transcendentals=0)


def part_specs(parts, R, at, block_len, D):
    own = pl.BlockSpec((1, block_len, D), lambda i, g, me: (me[0] * R + at + i, 0, 0))
    specs = [own]
    for bit, (part, base) in enumerate(parts[1:]):
        shape = (1, 1) + part.shape[2:]
        place = lambda bit, base, i, g, me: (me[0] >> (bit + 1), at + i - base, 0, 0)
        specs.append(pl.BlockSpec(shape, functools.partial(place, bit, base)))
    return specs


def arrays_of(parts):
    return [parts[0]] + [part for part, _ in parts[1:]]


def merge(refs):
    return jnp.concatenate([refs[0][0]] + [ref[0, 0] for ref in refs[1:]], 0)


def attend_kernel(me_ref, *refs, nparts, heads, hs, group, scale, nio, row, ncarry):
    carried, refs = refs[:ncarry], refs[ncarry:]
    parts, (code_ref, wt_ref, bt_ref, wo_ref, vec_ref) = refs[:nparts], refs[nparts : nparts + 5]
    outs = refs[nparts + 5 + nio :]
    x_far, qkv_far, p_ref, il_ref, att_ref, first_ref, n_ref, s_ref, tick_ref = outs[:9]
    kept, (x_ref, qkv_ref, sems) = outs[9:-3], outs[-3:]
    tick_ref[...] = jnp.zeros_like(tick_ref)
    D = heads * hs
    L = x_ref.shape[1]
    step = pl.program_id(1)
    copies = [
        pltpu.make_async_copy(x_ref, x_far.at[pl.ds(row, 1)], sems.at[0]),
        pltpu.make_async_copy(qkv_ref, qkv_far.at[pl.ds(row, 1)], sems.at[1]),
    ] + [pltpu.make_async_copy(a, b, sems.at[2 + i]) for i, (a, b) in enumerate(zip(carried, kept))]

    @pl.when(step == 0)
    def _():
        x_ref[0] = merge(parts)
        f = mm(wt_ref[...], x_ref[0], NT) + bt_ref[:, 0:1]
        qkv_ref[0, :D, :] = (f[:D].astype(BF16).astype(F32) * scale).astype(BF16)
        qkv_ref[0, D:, :] = f[D:].astype(BF16)
        for copy in copies:
            copy.start()

    it = lax.broadcasted_iota(jnp.int32, (CODES, L), 0)

    def head(i):
        at = pl.multiple_of((step * group + i) * hs, hs)
        return [qkv_ref[0, pl.ds(j * D + at, hs), :] for j in range(3)]

    bound = jnp.zeros((1, 1), F32)
    for i in range(group):
        q, k, _ = head(i)
        norms = [
            jnp.max(jnp.sum(v.astype(F32) * v.astype(F32), axis=0, keepdims=True), axis=1, keepdims=True)
            for v in (q, k)
        ]
        bound = jnp.maximum(bound, norms[0] * norms[1])
    small = bound[0, 0] <= NO_SHIFT * NO_SHIFT

    def attend_group(shifted):
        for i in range(group):
            at = pl.multiple_of((step * group + i) * hs, hs)
            q, k, v = head(i)
            same = it == code_ref[0, 0, i : i + 1, :]
            qa = jnp.concatenate([q, jnp.where(same, BIG, 0.0).astype(BF16)], 0)
            ka = jnp.concatenate([k, jnp.where(same, 0.0, -BIG).astype(BF16)], 0)
            s = mm(ka, qa, TN)
            if shifted:
                s = s - jnp.max(s, axis=0, keepdims=True)
            p = jnp.exp(s).astype(BF16)
            p_ref[0, i] = p
            o = mm(jnp.concatenate([v, jnp.ones((16, L), BF16)], 0), p)
            il = 1.0 / o[hs : hs + 1]
            il_ref[0, 0, i : i + 1, :] = il
            att_ref[0, pl.ds(at, hs), :] = (o[:hs] * il).astype(BF16)

    @pl.when(small)
    def _():
        attend_group(False)

    @pl.when(jnp.logical_not(small))
    def _():
        attend_group(True)

    @pl.when(step == heads // group - 1)
    def _():
        v1 = x_ref[0].astype(F32) + mm(att_ref[0], wo_ref[...], TN) + vec_ref[0:1, :]
        c = v1 - jnp.mean(v1, -1, keepdims=True)
        s1 = lax.rsqrt(jnp.mean(c * c, -1, keepdims=True) + NORM_EPS)
        n1 = c * s1
        first_ref[0] = (n1 * vec_ref[1:2, :] + vec_ref[2:3, :]).astype(BF16)
        n_ref[0] = n1.astype(BF16)
        s_ref[0] = jnp.broadcast_to(s1, (L, 128))
        for copy in copies:
            copy.wait()


def attend(me, parts, at, R, code, wt, bt, wo, vec, heads, hs, scale, group, deps, held, carry=()):
    r = 1
    D = wo.shape[0]
    L = code.shape[-1]
    here = lambda shape: pl.BlockSpec((1,) + shape, lambda i, g, me: (at + i,) + (0,) * len(shape))
    grouped = lambda shape: pl.BlockSpec((1, 1) + shape, lambda i, g, me: (at + i, g, 0, 0))
    shapes = [
        shape_of((R, L, D), BF16),
        shape_of((R, 3 * D, L), BF16), shape_of((R, heads, L, L), BF16),
        shape_of((R, heads // group, group, L), F32), shape_of((R, D, L), BF16),
        shape_of((R, L, D), BF16), shape_of((R, L, D), BF16), shape_of((R, L, 128), F32),
        TICK,
    ]
    nio = len(held) + len(deps)
    np_ = len(parts)
    return pl.pallas_call(
        functools.partial(
            attend_kernel, nparts=np_, heads=heads, hs=hs, group=group, scale=scale, nio=nio,
            row=at, ncarry=len(carry),
        ),
        grid_spec=pltpu.PrefetchScalarGridSpec(
            num_scalar_prefetch=1,
            grid=(r, heads // group),
            in_specs=[ANY] * len(carry) + part_specs(parts, R, at, parts[0].shape[1], D) + [
                grouped((group, L)), WHOLE, WHOLE, WHOLE, WHOLE,
            ] + [ANY] * nio,
            out_specs=[
                ANY, ANY, pl.BlockSpec((1, group, L, L), lambda i, g, me: (at + i, g, 0, 0)),
                grouped((group, L)), here((D, L)), here((L, D)), here((L, D)), here((L, 128)),
                TICK3,
            ] + [WHOLE] * len(carry),
            scratch_shapes=[
                pltpu.VMEM((1, L, D), BF16), pltpu.VMEM((1, 3 * D, L), BF16),
                pltpu.SemaphoreType.DMA((2 + len(carry),)),
            ],
        ),
        out_shape=shapes + [pltpu.VMEM(v.shape, v.dtype) for v in carry],
        input_output_aliases={1 + len(carry) + np_ + 5 + len(deps) + i: i for i in range(len(held))},
        compiler_params=params(ATTEND_VMEM),
        cost_estimate=cost(r * (8 * L * D * D + 4 * 4 * heads * L * L * hs), r * 2 * heads * L * L),
        name="attend",
    )(me, *carry, *arrays_of(parts), code, wt, bt, wo, vec, *deps, *held)


def prepare_kernel(me_ref, w_ref, b_ref, perm_ref, seg_ref, *rest, seq):
    wt_ref, bt_ref, code_ref = rest[-3:]
    wt_ref[...] = w_ref[...].T
    bt_ref[...] = b_ref[...].T
    heads, _, L = perm_ref.shape
    R, _, group = code_ref.shape[:3]
    me = me_ref[0]
    block = L // seq
    high = lax.broadcasted_iota(jnp.int32, (8, L), 0)
    low = lax.broadcasted_iota(jnp.int32, (128, L), 0)
    member = (lax.broadcasted_iota(jnp.int32, (8, L), 1) // CL).astype(F32)
    for r in range(R):
        seg = seg_ref[pl.ds(me * R + r, 1), :]
        for bit in bits_of(seq):
            blocks = [seg[:, i * block : (i + 1) * block] for i in range(seq)]
            turned = jnp.concatenate([blocks[i ^ (1 << bit)] for i in range(seq)], 1)
            seg = jnp.where(((me >> bit) & 1) == 1, turned, seg)
        for h in range(heads):
            place = perm_ref[h, pl.ds(me * R + r, 1), :] ^ (me * block)
            a = jnp.where((place >> 7) == high, member, 0.0).astype(BF16)
            b = ((place & 127) == low).astype(BF16)
            table = mm(a, b, NT)
            row = jnp.concatenate([table[i : i + 1, :] for i in range(L // 128)], 1)
            code_ref[r, h // group, h % group : h % group + 1, :] = row.astype(jnp.int32) * DOCS + seg


def prepare(me, seq, w, b, perm, segs, group, deps):
    heads, rows, L = perm.shape
    R = rows // seq
    D, D3 = w.shape
    full = lambda shape: pl.BlockSpec(shape, lambda i, me: (0,) * len(shape))
    codes = (R, heads // group, group, L)
    return pl.pallas_call(
        functools.partial(prepare_kernel, seq=seq),
        grid_spec=pltpu.PrefetchScalarGridSpec(
            num_scalar_prefetch=1,
            grid=(1,),
            in_specs=[
                full((D, D3)), full((8, D3)), full(perm.shape),
                full(segs.shape),
            ] + [ANY] * len(deps),
            out_specs=[full((D3, D)), full((D3, 8)), full(codes)],
        ),
        out_shape=[
            jax.ShapeDtypeStruct((D3, D), BF16), jax.ShapeDtypeStruct((D3, 8), F32),
            jax.ShapeDtypeStruct(codes, jnp.int32),
        ],
        compiler_params=params(32 * MIB),
        cost_estimate=cost(4e9, 8e6),
        name="prepare",
    )(me, w, b, perm, segs, *deps)


def ffn_kernel(me_ref, *refs, nparts, nio):
    parts, (first_ref, wu_ref, bu_ref, wd_ref, vec_ref) = refs[:nparts], refs[nparts : nparts + 5]
    lo_ref, hi_ref, gffn_ref, act_ref, slope_ref, sums_ref, tick_ref = refs[nparts + 5 + nio :]
    tick_ref[...] = jnp.zeros_like(tick_ref)
    @pl.when(pl.program_id(0) == 0)
    def _():
        sums_ref[...] = jnp.zeros_like(sums_ref)

    go_all = merge(parts)
    tile = first_ref.shape[0]
    sub = tile // FFN_CUT
    for cut in range(FFN_CUT):
        here = slice(cut * sub, (cut + 1) * sub)
        first = first_ref[here, :]
        u = mm(first, wu_ref[...]) + bu_ref[...]
        half = 0.5 * (1.0 + lax.erf(u * 0.7071067811865476))
        act = (u * half).astype(BF16)
        act_ref[here, :] = act
        slope_ref[here, :] = (half + u * jnp.exp(-0.5 * u * u) * 0.3989422804014327).astype(BF16)
        y = first.astype(F32) + mm(act, wd_ref[...]) + vec_ref[3:4, :]
        c = y - jnp.mean(y, -1, keepdims=True)
        s2 = lax.rsqrt(jnp.mean(c * c, -1, keepdims=True) + NORM_EPS)
        n2 = c * s2
        out = (n2 * vec_ref[4:5, :] + vec_ref[5:6, :]).astype(BF16)
        if cut < FFN_CUT // 2:
            lo_ref[0, here, :] = out
        elif FFN_CUT > 1:
            hi_ref[0, cut * sub - tile // 2 : (cut + 1) * sub - tile // 2, :] = out
        else:
            lo_ref[0] = out[: tile // 2]
            hi_ref[0] = out[tile // 2 :]
        go = go_all[here].astype(F32)
        e = go * vec_ref[4:5, :]
        g2 = s2 * (e - jnp.mean(e, -1, keepdims=True) - n2 * jnp.mean(e * n2, -1, keepdims=True))
        gl = g2.astype(BF16)
        gffn_ref[here, :] = gl
        sums_ref[0:1, :] += jnp.sum(gl.astype(F32), 0, keepdims=True)
        sums_ref[1:2, :] += jnp.sum(go * n2, 0, keepdims=True)
        sums_ref[2:3, :] += jnp.sum(go, 0, keepdims=True)


def ffn(me, first, parts, at, r, R, wu, bu, wd, vec, deps, held):
    T, D = first.shape
    L = T // R
    FF = wu.shape[1]
    here = lambda width: pl.BlockSpec((L, width), lambda i, g, me: (at + i, 0))
    nio = len(held) + len(deps)
    np_ = len(parts)
    half = pl.BlockSpec((1, L // 2, D), lambda i, g, me: (i, 0, 0))
    return pl.pallas_call(
        functools.partial(ffn_kernel, nparts=np_, nio=nio),
        grid_spec=pltpu.PrefetchScalarGridSpec(
            num_scalar_prefetch=1,
            grid=(r, 1),
            in_specs=part_specs(parts, R, at, parts[0].shape[1], D) + [
                here(D), WHOLE, WHOLE, WHOLE, WHOLE,
            ] + [ANY] * nio,
            out_specs=[
                half, half, here(D), here(FF), here(FF),
                pl.BlockSpec((8, D), lambda i, g, me: (0, 0)), TICK3,
            ],
        ),
        out_shape=[
            shape_of((r, L // 2, D), BF16), shape_of((r, L // 2, D), BF16), shape_of((T, D), BF16),
            shape_of((T, FF), BF16), shape_of((T, FF), BF16), shape_of((8, D), F32),
            TICK,
        ],
        input_output_aliases={1 + np_ + 5 + len(deps) + i: 2 + i for i in range(len(held))},
        compiler_params=params(FFN_VMEM),
        cost_estimate=cost(4 * r * L * D * FF * 1.3, 4 * r * L * FF + 4 * D * FF),
        name="ffn",
    )(me, *arrays_of(parts), *far(first), wu, bu, wd, vec, *deps, *held)


def by_core(total, place):
    rows, width = total.shape
    bits = len(place) + 1
    cube = total.reshape((2,) * bits + (rows >> bits, width))
    cube = cube.transpose((bits - 1,) + tuple(place) + (bits, bits + 1))
    return cube[0].reshape(rows // 2, width), cube[1].reshape(rows // 2, width)


def put_halves(me_ref, total, place, send_ref, keep_ref):
    even, odd = by_core(total, place)
    mine = me_ref[0] % 2 == 0
    send_ref[...] = jnp.where(mine, odd, even).astype(BF16)
    keep_ref[...] = jnp.where(mine, even, odd).astype(BF16)


def halves_of(me, total, place):
    even, odd = by_core(total, place)
    mine = me[0] % 2 == 0
    return jnp.where(mine, odd, even), jnp.where(mine, even, odd)


def places(dp, seq, order):
    names = [("dp", b) for b in reversed(bits_of(dp))] + [("seq", b) for b in reversed(bits_of(seq))]
    return [names.index(item) for item in order]


def splits(rows, n):
    return (rows // n) % 8 == 0


def down_grad_kernel(me_ref, act_ref, g_ref, *rest, place, ndep):
    outs = rest[ndep:]
    total = mm(act_ref[...], g_ref[...], TN)
    if len(outs) == 2:
        put_halves(me_ref, total, place, *outs)
    else:
        outs[0][...] = total.astype(BF16)


def down_grad(me, dp, seq, order, act, g, deps):
    T, FF = act.shape
    D = g.shape[1]
    n = dp * seq
    inside = splits(FF, n) and FF // dp % 128 == 0
    steps = dp if inside else 8
    tile = FF // steps
    place = places(dp, seq, order)
    inner = [p - len(bits_of(dp)) for p in place if p >= len(bits_of(dp))]
    turns = [bit for name, bit in order if name == "dp"]

    def at(i):
        where = 0
        for bit in turns:
            where = 2 * where + ((i >> bit) & 1)
        return (where, 0)

    res = pl.pallas_call(
        functools.partial(down_grad_kernel, place=inner, ndep=len(deps)),
        grid=(steps,),
        in_specs=[
            pl.BlockSpec(memory_space=pltpu.SMEM), pl.BlockSpec((T, tile), lambda i: (0, i)), whole((T, D)),
        ] + [ANY] * len(deps),
        out_specs=[pl.BlockSpec((tile // 2, D), at)] * 2 if inside else [rows_of(tile, D)],
        out_shape=[shape_of((FF // 2, D), BF16)] * 2 if inside else [shape_of((FF, D), BF16)],
        compiler_params=params(18 * MIB),
        cost_estimate=cost(2 * T * D * FF * 1.3, 2 * T * FF + 2 * D * FF),
        name="down_grad",
    )(me, *far(act, g), *deps)
    return res if inside else halves_of(me, res[0], place)


def ffn_back_kernel(
    g_ref, slope_ref, wu_ref, wd_ref, wo_ref, n_ref, s_ref, vec_ref, att_ref, il_ref, *rest,
    heads, hs,
):
    gpre_ref, gbr_ref, do_ref, de_ref, sums_ref, bsum_ref, tick_ref = rest[-7:]
    tick_ref[...] = jnp.zeros_like(tick_ref)
    @pl.when((pl.program_id(0) == 0) & (pl.program_id(1) == 0))
    def _():
        sums_ref[...] = jnp.zeros_like(sums_ref)
        bsum_ref[...] = jnp.zeros_like(bsum_ref)

    sub = g_ref.shape[0] // BACK_CUT
    for cut in range(BACK_CUT):
        here = slice(cut * sub, (cut + 1) * sub)
        g = g_ref[here, :]
        gp = (mm(g, wd_ref[...], NT) * slope_ref[here, :].astype(F32)).astype(BF16)
        gpre_ref[here, :] = gp
        gfirst = mm(gp, wu_ref[...], NT) + g.astype(F32)
        n1 = n_ref[0, here, :].astype(F32)
        e = gfirst * vec_ref[1:2, :]
        g1 = s_ref[0, here, 0:1] * (
            e - jnp.mean(e, -1, keepdims=True) - n1 * jnp.mean(e * n1, -1, keepdims=True)
        )
        gl = g1.astype(BF16)
        gbr_ref[0, here, :] = gl
        da = mm(wo_ref[...], gl, NT)
        group = il_ref.shape[2]
        for h in range(heads):
            i, j = h // group, h % group
            il = il_ref[0, i, j : j + 1, here]
            piece = da[h * hs : (h + 1) * hs, :] * il
            do_ref[0, h * hs : (h + 1) * hs, here] = piece.astype(BF16)
            att = att_ref[0, h * hs : (h + 1) * hs, here].astype(F32)
            de_ref[0, i, j : j + 1, here] = jnp.sum(piece * att, axis=0, keepdims=True)
        sums_ref[0:1, :] += jnp.sum(gl.astype(F32), 0, keepdims=True)
        sums_ref[1:2, :] += jnp.sum(gfirst * n1, 0, keepdims=True)
        sums_ref[2:3, :] += jnp.sum(gfirst, 0, keepdims=True)
        bsum_ref[0:1, :] += jnp.sum(gp.astype(F32), 0, keepdims=True)


def ffn_back(at, r, g, slope, wu, wd, wo, n1, s1, vec, att, il, heads, hs, deps, held):
    T, D = g.shape
    FF = wu.shape[1]
    R, L = n1.shape[:2]
    half = L // 2
    flat = lambda width: pl.BlockSpec((half, width), lambda i, g: (2 * (at + i) + g, 0))
    fixed = lambda shape: pl.BlockSpec(
        shape, lambda i, g: (0,) * len(shape), pipeline_mode=pl.Buffered(1)
    )
    tokens = lambda width: pl.BlockSpec((1, half, width), lambda i, g: (at + i, g, 0))
    columns = lambda *lead: pl.BlockSpec(
        (1,) + lead + (half,), lambda i, g: (at + i,) + (0,) * len(lead) + (g,)
    )
    extra = list(deps) + list(held)
    return pl.pallas_call(
        functools.partial(ffn_back_kernel, heads=heads, hs=hs),
        grid=(r, 2),
        in_specs=[
            flat(D), flat(FF), WHOLE, WHOLE, fixed((D, D)), tokens(D), tokens(128), fixed((8, D)),
            columns(D), columns(*il.shape[1:3]),
        ] + [ANY] * len(extra),
        out_specs=[
            flat(FF), tokens(D), columns(D), columns(*il.shape[1:3]),
            pl.BlockSpec((8, D), lambda i, g: (0, 0)), pl.BlockSpec((8, FF), lambda i, g: (0, 0)),
            TICK2,
        ],
        out_shape=[
            shape_of((T, FF), BF16), shape_of((R, L, D), BF16), shape_of((R, D, L), BF16),
            shape_of(il.shape, F32), shape_of((8, D), F32), shape_of((8, FF), F32),
            TICK,
        ],
        input_output_aliases={10 + len(deps) + i: i for i in range(len(held))},
        compiler_params=params(BACK_VMEM),
        cost_estimate=cost(4 * r * L * D * FF * 1.5, 4 * r * L * FF + 4 * D * FF),
        name="ffn_back",
    )(*far(g, slope), wu, wd, *far(wo, n1, s1, vec, att, il), *extra)


def up_out_grad_kernel(me_ref, x_ref, g_ref, att_far, gbr_far, *rest, place, ndep):
    outs, tick_ref, att_ref, gbr_ref, sems = rest[ndep:-4], rest[-4], rest[-3], rest[-2], rest[-1]
    tick_ref[...] = jnp.zeros_like(tick_ref)
    last = pl.num_programs(0) - 1

    def put(total):
        if len(outs) == 2:
            put_halves(me_ref, total, place, *outs)
        else:
            outs[0][...] = total.astype(BF16)

    copies = [
        pltpu.make_async_copy(att_far, att_ref, sems.at[0]),
        pltpu.make_async_copy(gbr_far, gbr_ref, sems.at[1]),
    ]

    @pl.when(pl.program_id(0) == 0)
    def _():
        for copy in copies:
            copy.start()

    @pl.when(pl.program_id(0) < last)
    def _():
        put(mm(x_ref[...], g_ref[...], TN))

    @pl.when(pl.program_id(0) == last)
    def _():
        for copy in copies:
            copy.wait()
        total = mm(att_ref[0], gbr_ref[0])
        for r in range(1, att_ref.shape[0]):
            total = total + mm(att_ref[r], gbr_ref[r])
        put(total)


def up_out_grad(me, dp, seq, order, x, g, att, gbr, deps):
    T, D = x.shape
    FF = g.shape[1]
    R, _, L = att.shape
    place = places(dp, seq, order)
    inside = splits(D, dp * seq)
    rows, count = (D // 2, 2) if inside else (D, 1)
    steps = FF // D
    *res, tick = pl.pallas_call(
        functools.partial(up_out_grad_kernel, place=place, ndep=len(deps)),
        grid=(steps + 1,),
        in_specs=[
            pl.BlockSpec(memory_space=pltpu.SMEM), whole((T, D)),
            pl.BlockSpec((T, D), lambda i: (0, jnp.minimum(i, steps - 1))), ANY, ANY,
        ] + [ANY] * len(deps),
        out_specs=[pl.BlockSpec((rows, D), lambda i: (0, i))] * count + [TICK1],
        out_shape=[jax.ShapeDtypeStruct((rows, FF + D), BF16)] * count + [TICK],
        scratch_shapes=[
            pltpu.VMEM((R, D, L), BF16), pltpu.VMEM((R, L, D), BF16), pltpu.SemaphoreType.DMA((2,)),
        ],
        compiler_params=params(),
        cost_estimate=cost(1, 1),
        name="up_out_grad",
    )(me, *far(x, g, att, gbr), *deps)
    return (res if inside else halves_of(me, res[0], place)), tick


def attend_back_kernel(
    qkv_ref, p_ref, do_ref, de_ref, gone_ref, wt_ref, *rest, heads, hs, scale, group
):
    g_out, lo_ref, hi_ref, sums_ref, tick_ref, g_ref = rest[-6:]
    tick_ref[...] = jnp.zeros_like(tick_ref)
    step = pl.program_id(1)
    for i in range(group):
        here = slice(i * hs, (i + 1) * hs)
        q, k, v = [qkv_ref[0, j, here, :] for j in range(3)]
        do = do_ref[0, here, :]
        p = p_ref[0, i]
        dp = mm(v, do, TN)
        ds = (p.astype(F32) * (dp - de_ref[0, 0, i : i + 1, :])).astype(BF16)
        grads = [mm(k, ds) * scale, mm(q, ds, NT), mm(do, p, NT)]
        for j in range(3):
            part = grads[j].astype(BF16)
            g_out[0, j, here, :] = part
            g_ref[j, step, here, :] = part

    @pl.when(step == heads // group - 1)
    def _():
        g = g_ref[...].reshape(3 * heads * hs, g_ref.shape[-1])
        gin = (mm(g, wt_ref[...], TN) + gone_ref[0].astype(F32)).astype(BF16)
        half_len = gin.shape[0] // 2
        lo_ref[0] = gin[:half_len]
        hi_ref[0] = gin[half_len:]

        @pl.when(pl.program_id(0) == 0)
        def _():
            sums_ref[...] = jnp.zeros_like(sums_ref)

        ones = jnp.ones((8, g.shape[1]), BF16)
        sums_ref[...] += mm(ones, g, NT)


def attend_back(at, r, of, place, qkv, p, do, de, gone, wt, heads, hs, scale, group, deps, held):
    R, D3, L = qkv.shape
    D = D3 // 3
    here = lambda shape: pl.BlockSpec((1,) + shape, lambda i, g: (at + i,) + (0,) * len(shape))
    extra = list(deps) + [v for v in held if v is not None]
    aliases = {}
    for i, v in enumerate(held):
        if v is not None:
            aliases[6 + len(deps) + len(aliases)] = i
    half = pl.BlockSpec((1, L // 2, D), lambda i, g: (place + i, 0, 0))
    heads_of = pl.BlockSpec((1, 3, group * hs, L), lambda i, g: (at + i, 0, g, 0))
    g, *rest = pl.pallas_call(
        functools.partial(attend_back_kernel, heads=heads, hs=hs, scale=scale, group=group),
        grid=(r, heads // group),
        in_specs=[
            heads_of, pl.BlockSpec((1, group, L, L), lambda i, g: (at + i, g, 0, 0)),
            pl.BlockSpec((1, group * hs, L), lambda i, g: (at + i, g, 0)),
            pl.BlockSpec((1, 1, group, L), lambda i, g: (at + i, g, 0, 0)),
            here((L, D)), WHOLE,
        ] + [ANY] * len(extra),
        out_specs=[heads_of, half, half, pl.BlockSpec((8, D3), lambda i, g: (0, 0)), TICK2],
        out_shape=[
            shape_of((R, 3, D, L), BF16), shape_of((of, L // 2, D), BF16),
            shape_of((of, L // 2, D), BF16), shape_of((8, D3), F32), TICK,
        ],
        scratch_shapes=[pltpu.VMEM((3, heads // group, group * hs, L), BF16)],
        input_output_aliases=aliases,
        compiler_params=params(ATTEND_BACK_VMEM),
        cost_estimate=cost(r * (6 * L * D * D + 4 * 8 * heads * L * L * hs), r * 2 * heads * L * L),
        name="attend_back",
    )(*far(qkv.reshape(R, 3, D, L), p, do, de, gone), wt, *extra)
    return [g, *rest]


def spots(widths):
    out, at = [], 0
    for width in widths:
        if at % 128 + width > 128:
            at = 128 * -(-at // 128)
        out.append(at)
        at += width
    return out


def pack(sums, n, windows):
    widths = [terms[0].shape[1] // n for terms in sums]
    pieces = [jnp.zeros((n, 128), F32) for _ in range(windows)]
    for terms, width, at in zip(sums, widths, spots(widths)):
        v = functools.reduce(jnp.add, terms)
        W = v.shape[1]
        owner = lax.broadcasted_iota(jnp.int32, (n, W), 0)
        place = lax.broadcasted_iota(jnp.int32, (n, W), 1)
        a = jnp.where((place >= owner * width) & (place < (owner + 1) * width), v, 0.0).astype(BF16)
        index = lax.broadcasted_iota(jnp.int32, (W, 128), 0)
        start = ((index.astype(F32) + 0.5) * (1.0 / width)).astype(jnp.int32) * width
        b = (lax.broadcasted_iota(jnp.int32, (W, 128), 1) == index - start + at % 128).astype(BF16)
        pieces[at // 128] += mm(a, b)
    return pieces


def qkv_grad_kernel(me_ref, x_ref, g_ref, *rest, spans, nsum, ndep, n, count, place):
    sums_refs, outs, pack_ref, xt_ref = rest[:nsum], rest[nsum + ndep : -3], rest[-2], rest[-1]
    rest[-3][...] = jnp.zeros_like(rest[-3])
    step, steps = pl.program_id(0), len(place)
    D = x_ref.shape[2]

    def put(total, which):
        refs = outs[which * count : (which + 1) * count]
        if count == 2:
            put_halves(me_ref, total, place[which], *refs)
        else:
            refs[0][...] = total.astype(BF16)

    @pl.when(step == 0)
    def _():
        for r in range(x_ref.shape[0]):
            xt_ref[r] = x_ref[r].T
        sums = [
            [jnp.concatenate([sums_refs[i][row : row + 1, lo:hi] for lo, hi in cols], 1) for i in terms]
            for terms, row, cols in spans
        ]
        for i, piece in enumerate(pack(sums, n, pack_ref.shape[0])):
            pack_ref[i] = piece

    total = mm(xt_ref[0], g_ref[0], NT)
    for r in range(1, x_ref.shape[0]):
        total = total + mm(xt_ref[r], g_ref[r], NT)

    for which in range(steps - 1):
        @pl.when(step == which)
        def _(which=which):
            put(total, which)

    @pl.when(step == steps - 1)
    def _():
        row = lax.broadcasted_iota(jnp.int32, (n, D // n, 128), 1)
        packed = jnp.zeros((n, D // n, 128), F32)
        for i in range(pack_ref.shape[0]):
            packed = jnp.where(row == i, pack_ref[i][:, None, :], packed)
        put(jnp.concatenate([total, packed.reshape(D, 128)], 1), steps - 1)


def qkv_grad(me, dp, seq, orders, x, g, sums, spans, deps):
    R, L, D = x.shape
    n = dp * seq
    place = [places(dp, seq, order) for order in orders]
    real = len(place)
    inside = splits(D, n)
    rows, count = (D // 2, 2) if inside else (D, 1)
    widths = [D] * (real - 1) + [D + 128]
    parts = [sum(hi - lo for lo, hi in cols) // n for _, _, cols in spans]
    windows = spots(parts)[-1] // 128 + 1
    *res, tick = pl.pallas_call(
        functools.partial(
            qkv_grad_kernel, spans=spans, nsum=len(sums), ndep=len(deps), n=n, count=count, place=place
        ),
        grid=(real,),
        in_specs=[
            pl.BlockSpec(memory_space=pltpu.SMEM), whole((R, L, D)),
            pl.BlockSpec((R, D, L), lambda i: (0, i, 0)),
        ] + [whole(v.shape) for v in sums] + [ANY] * len(deps),
        out_specs=[
            pl.BlockSpec((rows, width), lambda i: (0, 0)) for width in widths for _ in range(count)
        ] + [TICK1],
        out_shape=[
            jax.ShapeDtypeStruct((rows, width), BF16) for width in widths for _ in range(count)
        ] + [TICK],
        scratch_shapes=[pltpu.VMEM((windows, n, 128), F32), pltpu.VMEM((R, D, L), BF16)],
        compiler_params=params(),
        cost_estimate=cost(6 * R * L * D * D * 1.3, 8 * R * L * D),
        name="qkv_grad",
    )(me, *far(x, g), *sums, *deps)
    pieces = [res[i * count : (i + 1) * count] for i in range(real)]
    return [piece if inside else halves_of(me, piece[0], at) for piece, at in zip(pieces, place)], tick


def bits_of(size):
    return [b for b in range(size.bit_length() - 1)]


def flip(x, axis, size, bit):
    return lax.ppermute(x, axis, [(i, i ^ (1 << bit)) for i in range(size)])


def my_bit(axis, bit):
    return (lax.axis_index(axis) >> bit) & 1


def pick(x, index, axis):
    return lax.dynamic_index_in_dim(x, index, axis, keepdims=False)


def late(x, tick):
    return x if tick is None else x + tick.reshape(()).astype(x.dtype)


def move_kernel(me_ref, *refs, count, ndep, copies):
    srcs, outs, sems = refs[:count], refs[count + ndep : -1], refs[-1]
    me = me_ref[0]
    started = []
    for i, (src, at, out, to) in enumerate(copies):
        copy = pltpu.make_async_copy(srcs[src].at[at(me)], outs[out].at[to(me)], sems.at[i])
        copy.start()
        started.append(copy)
    for copy in started:
        copy.wait()


def move(me, srcs, shapes, copies, deps=()):
    return pl.pallas_call(
        functools.partial(move_kernel, count=len(srcs), ndep=len(deps), copies=copies),
        in_specs=[pl.BlockSpec(memory_space=pltpu.SMEM)] + [ANY] * (len(srcs) + len(deps)),
        out_specs=[ANY] * len(shapes),
        out_shape=[jax.ShapeDtypeStruct(shape, BF16) for shape in shapes],
        scratch_shapes=[pltpu.SemaphoreType.DMA((len(copies),))],
        compiler_params=params(4 * MIB),
        cost_estimate=cost(1, 1),
        name="move",
    )(me, *srcs, *deps)


def pass_on(arrays, after):
    return pl.pallas_call(
        lambda *refs: None,
        in_specs=[ANY] * (len(arrays) + len(after)),
        out_specs=[ANY] * len(arrays),
        out_shape=[jax.ShapeDtypeStruct(v.shape, v.dtype) for v in arrays],
        input_output_aliases={i: i for i in range(len(arrays))},
        compiler_params=params(4 * MIB),
        cost_estimate=cost(1, 1),
        name="pass_on",
    )(*arrays, *after)


class Rows:
    def __init__(self, x, axis, size):
        self.x, self.axis, self.size = x, axis, size
        self.bits = bits_of(size)
        self.R, self.B, self.D = x.shape[0] // size, x.shape[1], x.shape[2]
        self.came = [[] for _ in self.bits]

    def find(self, bit, start):
        return [(v, base) for v, base in self.came[bit] if base <= start][-1]

    def plan(self, bit, start, stop, srcs, copies, out):
        r, B, R = stop - start, self.B, self.R
        lead = 1 << (len(self.bits) - 1 - bit)
        for high in range(lead):
            def owner(me, high=high):
                return (high << (bit + 1)) + (me ^ (1 << bit)) % (1 << (bit + 1))

            def own(me, owner=owner):
                return (pl.ds(owner(me) * R + start, r),)

            def place(lo, hi, high=high):
                return lambda me: (high, slice(None), pl.ds(lo, hi - lo))

            copies.append((len(srcs), own, out, place(0, B)))
            for done in range(bit):
                got, base = self.find(done, start)

                def theirs(me, owner=owner, done=done, base=base):
                    return (owner(me) >> (done + 1), pl.ds(start - base, r))

                copies.append((len(srcs) + 1 + done, theirs, out, place(B << done, B << (done + 1))))
        srcs.append(self.x)
        srcs.extend(self.find(done, start)[0] for done in range(bit))
        return (lead, r, B << bit, self.D)

    def send(self, bit, start, send):
        self.came[bit].append((flip(send, self.axis, self.size, bit), start))

    def parts(self, start):
        return [self.x] + [self.find(bit, start) for bit in self.bits]


def gather(me, jobs, deps=()):
    srcs, copies, shapes = [], [], []
    for out, (rows, bit, start, stop) in enumerate(jobs):
        shapes.append(rows.plan(bit, start, stop, srcs, copies, out))
    return move(me, srcs, shapes, copies, deps)


def exchange(me, jobs, deps=()):
    sends = gather(me, jobs, deps)
    for (rows, bit, start, stop), send in zip(jobs, sends):
        rows.send(bit, start, send)
    return sends


class Blocks:
    def __init__(self, axis, size):
        self.axis, self.size, self.chunks = axis, size, []

    def send(self, lo, hi):
        self.chunks.append((lo, flip(hi, self.axis, self.size, bits_of(self.size)[-1])))

    def turn(self, me, tick):
        bits, axis, size = bits_of(self.size), self.axis, self.size
        half, D = self.chunks[0][0].shape[1:]
        self.R = R = sum(lo.shape[0] for lo, _ in self.chunks)
        self.pieces = pieces = {0: [], 1 << bits[-1]: []}
        at = 0
        for chunk in self.chunks:
            for name, v in zip(pieces, chunk):
                pieces[name].append((v, (), at, v.shape[0], 0))
            at += chunk[0].shape[0]
        for bit in reversed(bits[:-1]):
            half //= 2
            names = list(pieces)
            join = lambda vs: vs[0] if len(vs) == 1 else jnp.concatenate(vs, 0)
            send = jnp.stack([
                join([v[front + (slice(None), slice(token + half, token + 2 * half))] for v, front, _, _, token in pieces[name]])
                for name in names
            ], 0)
            send = late(send, tick)
            self.came = flip(send, axis, size, bit)
            for i, name in enumerate(names):
                pieces[name | (1 << bit)] = [(self.came, (i,), 0, R, 0)]
        self.shape = (size * R, half, D)

    def result(self, me, tick):
        half, D = self.shape[1:]
        entries = [(name,) + source for name, sources in self.pieces.items() for source in sources]
        block = functools.reduce(math.gcd, [rows for _, _, _, _, rows, _ in entries])
        starts = [sum(e[4] // block for e in entries[:i]) for i in range(len(entries) + 1)]
        R = self.R

        def source_spec(e, start, stop):
            _, v, front, _, _, _ = e
            lead = (1,) * len(front)

            def at(i, me):
                return front + (jnp.clip(i, start, stop - 1) - start, 0, 0)

            return pl.BlockSpec(lead + (block, half, D), at)

        def target(i, me):
            where = 0
            for (name, _, _, row, _, _), start, stop in zip(entries, starts, starts[1:]):
                here = ((me[0] ^ name) * R + row) // block + i - start
                where = jnp.where((i >= start) & (i < stop), here, where)
            return (where, 0, 0)

        def kernel(me_ref, *refs):
            i, out = pl.program_id(0), refs[-1]
            for ref, start, stop in zip(refs, starts, starts[1:]):
                @pl.when((i >= start) & (i < stop))
                def _(ref=ref):
                    out[...] = ref[...].reshape(out.shape)

        return pl.pallas_call(
            kernel,
            grid_spec=pltpu.PrefetchScalarGridSpec(
                num_scalar_prefetch=1,
                grid=(starts[-1],),
                in_specs=[source_spec(e, a, b) for e, a, b in zip(entries, starts, starts[1:])] + [ANY],
                out_specs=pl.BlockSpec((block, half, D), target),
            ),
            out_shape=shape_of(self.shape, BF16),
            compiler_params=params(16 * MIB),
            cost_estimate=cost(1, 1),
            name="place",
        )(me, *[e[1] for e in entries], tick)


class Sum:
    def __init__(self, halves, dp, seq, order):
        self.sizes = {"dp": dp, "seq": seq}
        self.order = list(order)
        self.send, self.keep = halves

    def begin(self, send=None):
        self.go("seq", 0, [self.send if send is None else send])

    def go(self, name, bit, sends):
        self.came = [flip(v, name, self.sizes[name], bit) for v in sends]

    def result(self, tick=None, start=0, stop=None):
        came = self.came[0][:, start:stop]
        return late(self.keep[:, start:stop].astype(F32) + came.astype(F32), tick)


def fold_kernel(me_ref, *refs, shapes, ndep, nthrough):
    nin = sum(2 + 2 * took for took, _ in shapes)
    ins, outs = refs[:nin], refs[nin + ndep + nthrough : len(refs) - nthrough]
    outs[-1][...] = jnp.zeros_like(outs[-1])
    for took, gave in shapes:
        keep, came, ins = ins[:2], (ins[2 : 2 + took], ins[2 + took : 2 + 2 * took]), ins[2 + 2 * took :]
        send_refs, keep_ref, outs = outs[:gave], outs[gave], outs[gave + 1 :]
        sums = []
        for base, parts in zip(keep, came):
            part = jnp.concatenate([ref[0] for ref in parts], 1) if took > 1 else parts[0][0]
            sums.append((base[0].astype(F32) + part.astype(F32)).astype(BF16))
        width = sums[0].shape[1] // gave
        for i, ref in enumerate(send_refs):
            ref[...] = sums[0][:, i * width : (i + 1) * width]
        keep_ref[...] = sums[1]


def fold(me, chains, deps=(), split=1, through=()):
    items = [chain.order.pop(0) for chain in chains]
    rows = [chain.keep.shape[0] // 2 for chain in chains]
    steps = max(s for s in (4, 2, 1) if s == 1 or all(r % (16 * s) == 0 for r in rows))
    ins, in_specs, out_specs, out_shape, shapes = [], [], [], [], []
    for chain, (name, bit), r in zip(chains, items, rows):
        tile, width = r // steps, chain.keep.shape[1]
        row = 0 if name == "dp" else 1
        gave = split if chain is chains[-1] else 1

        def half(other, width, row=row, bit=bit, tile=tile):
            return pl.BlockSpec(
                (1, tile, width), lambda i, me: (((me[row] >> bit) & 1) ^ other, i, 0)
            )

        view = lambda v, r=r: v.reshape(2, r, v.shape[1])
        ins += [view(chain.keep)] * 2 + [view(v) for v in chain.came] * 2
        in_specs += [half(1, width), half(0, width)]
        in_specs += [half(other, v.shape[1]) for other in (1, 0) for v in chain.came]
        out_specs += [pl.BlockSpec((tile, width // gave), lambda i, me: (i, 0))] * gave
        out_specs += [pl.BlockSpec((tile, width), lambda i, me: (i, 0))]
        out_shape += [shape_of((r, width // gave), BF16)] * gave
        out_shape += [jax.ShapeDtypeStruct((r, width), BF16)]
        shapes.append((len(chain.came), gave))
    res = pl.pallas_call(
        functools.partial(fold_kernel, shapes=shapes, ndep=len(deps), nthrough=len(through)),
        grid_spec=pltpu.PrefetchScalarGridSpec(
            num_scalar_prefetch=1,
            grid=(steps,),
            in_specs=in_specs + [ANY] * (len(deps) + len(through)),
            out_specs=out_specs + [pl.BlockSpec((1, 1), lambda i, me: (0, 0))] + [ANY] * len(through),
        ),
        out_shape=out_shape + [TICK] + [jax.ShapeDtypeStruct(v.shape, v.dtype) for v in through],
        input_output_aliases={
            1 + len(ins) + len(deps) + i: len(out_shape) + 1 + i for i in range(len(through))
        },
        compiler_params=params(16 * MIB),
        cost_estimate=cost(1, 1),
        name="fold",
    )(me, *ins, *deps, *through)
    tick, on = res[len(out_shape)], res[len(out_shape) + 1 :]
    sends = []
    for chain, (name, bit), (_, gave) in zip(chains, items, shapes):
        chain.go(name, bit, res[:gave])
        chain.keep = res[gave]
        sends += res[:gave]
        res = res[gave + 1 :]
    return (sends, tick, on) if through else (sends, tick)


def chunks_of(count, sizes):
    out, at = [], 0
    for size in sizes:
        stop = min(count, at + size)
        if stop > at:
            out.append((at, stop))
        at = stop
    return out + ([(at, count)] if at < count else [])


def shards(
    dp, seq, hidden_in, segment_ids, cluster_perm, w_qkv, bias_qv, w_out, bias_out, gain_attn,
    shift_attn, w_up, bias_up, w_down, bias_down, gain_ffn, shift_ffn, grad_out,
):
    row_count, block_len, D = hidden_in.shape
    heads = cluster_perm.shape[1]
    hs = D // heads
    L = segment_ids.shape[1]
    FF = w_up.shape[1]
    R = row_count // seq
    T = R * L
    group = 4
    scale = 1.0 / math.sqrt(hs)
    mine = lax.axis_index("seq")
    me = mine.reshape(1).astype(jnp.int32)
    both = jnp.stack([lax.axis_index("dp"), mine]).astype(jnp.int32)

    hidden, gout = Rows(hidden_in, "seq", seq), Rows(grad_out, "seq", seq)
    halves = chunks_of(R, (R // 2,))
    bits = bits_of(seq)
    exchange(me, [(hidden, 0, 0, 1)])
    for bit in bits[1:]:
        first_sent = exchange(me, [(hidden, bit, 0, 1)])
    rest = [(hidden, 0, 1, R)] if R > 1 else []
    exchange(me, rest + [(gout, 0, 0, R)], first_sent)

    bias = jnp.concatenate([bias_qv[:D], jnp.zeros((D,), F32), bias_qv[D:]])
    bias = jnp.broadcast_to(bias, (8, 3 * D))
    none = jnp.zeros((D,), F32)
    vec = jnp.stack([bias_out, gain_attn, shift_attn, bias_down, gain_ffn, shift_ffn, none, none])
    wt, bt, code = prepare(me, seq, w_qkv, bias, cluster_perm.transpose(1, 0, 2), segment_ids, group, first_sent)

    jobs = [(hidden, row, row + 1) for row in range(1, R)] + [(gout, *half) for half in halves]
    early = len(bits) == 2
    if early:
        queue = list(zip(jobs, gather(me, [(rows, bits[-1], a, b) for rows, a, b in jobs], first_sent)))
    else:
        queue = [(job, None) for job in jobs]

    def launch(after):
        if not queue:
            return after
        (rows, start, stop), send = queue.pop(0)
        if early:
            (send,) = pass_on([send], after)
            rows.send(bits[-1], start, send)
            return [send]
        for bit in bits[1:]:
            after = exchange(me, [(rows, bit, start, stop)], after)
        return after

    held, tick = (), None
    for row in range(R):
        deps = launch(first_sent if tick is None else [tick]) if row < R - 1 else []
        if row == R - 2:
            deps = deps + launch([tick] if tick is not None else first_sent)
        res = attend(
            me, hidden.parts(row), row, R, code, wt, bt, w_out, vec, heads, hs, scale, group, deps, held,
        )
        held, tick = res[:8], res[8]
    x, qkv, p, il, att, first, n1, s1 = held
    first = first.reshape(T, D)

    held, out_blocks, sums_ffn = (), Blocks("seq", seq), []
    for i, (start, stop) in enumerate(halves):
        deps = launch([tick])
        lo, hi, *held, sums, tick = ffn(
            me, first, gout.parts(start), start, stop - start, R, w_up, bias_up.reshape(1, -1), w_down,
            vec, deps, held,
        )
        out_blocks.send(lo, hi)
        sums_ffn.append(sums)
    gffn, act, slope = held

    low = [("dp", b) for b in bits_of(dp)]
    high = [("seq", b) for b in bits_of(seq)[1:]]
    turned = low[1:2] + low[:1] + high + low[2:]

    n = dp * seq
    came_out = [v for _, v in out_blocks.chunks]
    down = Sum(down_grad(me, dp, seq, low + high, act, gffn, far(*came_out[:1])), dp, seq, low + high)
    down.begin()
    held, sums_attn, sums_up, deps = (), [], [], []
    for i, (start, stop) in enumerate(halves):
        *held, sums1, sums2, tick = ffn_back(
            start, stop - start, gffn, slope, w_up, w_down, w_out, n1, s1, vec, att, il, heads, hs,
            deps, held,
        )
        sums_attn.append(sums1)
        sums_up.append(sums2)
        deps = []
        if i == 0:
            deps, _ = fold(both, [down], [tick] + far(*came_out[1:]))
            deps = far(*deps)
    gpre, gbr, do, de = held
    d_up, tick = up_out_grad(me, dp, seq, low + high, first, gpre, att, gbr, deps)
    up = Sum(d_up, dp, seq, low + high)
    deps, _, (send,) = fold(both, [down], [tick], 1, [up.send])
    deps = far(*deps)
    up.begin(send)
    g, in_blocks, sums_qkv = None, Blocks("seq", seq), []
    for start, stop in halves:
        lo = hi = None
        for row in range(start, stop):
            if row == 1:
                sends, _ = fold(both, [down, up] if down.order else [up], [tick], 2)
                sends = far(*sends)
                deps = sends[:-1]
            elif row == 2:
                deps = [sends[-1], up.came[0]]
            elif row == 3:
                deps, _ = fold(both, [down, up] if down.order else [up], [tick])
                deps = far(*deps)
            elif row:
                deps = []
            g, lo, hi, sums, tick = attend_back(
                row, 1, stop - start, row - start, qkv, p, do, de, gbr, wt, heads, hs, scale, group,
                deps, (g, lo, hi),
            )
            sums_qkv.append(sums)
        in_blocks.send(lo, hi)
    g = g.reshape(R, 3 * D, L)
    deps, _ = fold(both, [up], [tick] + far(in_blocks.chunks[0][1]))
    deps = far(*deps)

    sums = sums_qkv + sums_attn + sums_up + sums_ffn
    kinds = [sums_qkv, sums_attn, sums_up, sums_ffn]
    firsts = [sum(len(v) for v in kinds[:i]) for i in range(4)]
    span = lambda kind, row, *cols: (range(firsts[kind], firsts[kind] + len(kinds[kind])), row, cols)
    spans = [
        span(0, 0, (0, D), (2 * D, 3 * D)), span(1, 0, (0, D)), span(1, 1, (0, D)), span(1, 2, (0, D)),
        span(2, 0, (0, FF)), span(3, 0, (0, D)), span(3, 1, (0, D)), span(3, 2, (0, D)),
    ]
    per = [sum(hi - lo for lo, hi in cols) // n for _, _, cols in spans]
    orders = [low + high, turned, high[:1] + low[2:] + low[:2] + high[1:]]
    d_qkv, tick = qkv_grad(me, dp, seq, orders, x, g, sums, spans, deps)
    lasts = [Sum(halves_, dp, seq, order) for halves_, order in zip(d_qkv, orders)]
    while len(up.order) > 1:
        _, tick = fold(both, [up], [tick])
    _, tick, sends = fold(
        both, [up], [tick] + far(*[v for _, v in in_blocks.chunks[1:]]), 1, [s.send for s in lasts]
    )
    for s, send in zip(lasts, sends):
        s.begin(send)
    while down.order:
        _, tick = fold(both, [down], [tick])
    out_blocks.turn(me, tick)
    in_blocks.turn(me, tick)
    stage, done = 0, []
    while lasts[0].order:
        _, tick = fold(both, ([up] if up.order else []) + lasts, [tick] + done)
        done = []
        if stage == 0:
            out_hidden = out_blocks.result(me, tick)
            done = far(out_hidden)
        if stage == 1:
            grad_in = in_blocks.result(me, tick)
            done = far(grad_in)
        if stage == 2:
            r_down, r_up, r_out = down.result(tick), up.result(tick, 0, FF), up.result(tick, FF)
            done = far(r_down, r_up, r_out)
        stage += 1
    r_qkv = [s.result() for s in lasts]
    vec = r_qkv[-1][: spots(per)[-1] // 128 + 1, D:].reshape(-1)
    cuts = [vec[at : at + width] for at, width in zip(spots(per), per)]
    b_qv, b_out, g_attn, s_attn, b_up, b_down, g_ffn, s_ffn = cuts
    return (
        out_hidden, grad_in, jnp.concatenate(r_qkv[:-1] + [r_qkv[-1][:, :D]], 1), b_qv,
        r_out, b_out, g_attn, s_attn, r_up, b_up, r_down, b_down, g_ffn, s_ffn,
    )


def solution(mesh):
    tok = P("dp", "seq", None)
    both = ("dp", "seq")
    return jax.shard_map(
        functools.partial(shards, mesh.shape["dp"], mesh.shape["seq"]),
        mesh=mesh,
        in_specs=(tok, P("dp", None), P("dp", None, None)) + (P(),) * 12 + (tok,),
        out_specs=(
            tok, tok, P(both, None), P(both), P(both, None), P(both), P(both), P(both),
            P(both, None), P(both), P(both, None), P(both), P(both), P(both),
        ),
        check_vma=False,
    )
```

```python
import functools
import math

import jax
import jax.numpy as jnp
from jax import lax
from jax.experimental import pallas as pl
from jax.experimental.pallas import tpu as pltpu
from jax.sharding import PartitionSpec as P

CL = 128
DOCS = 3
CODES = 16
NORM_EPS = 1e-05
BIG = 2.0**50
NO_SHIFT = 40.0
F32 = jnp.float32
BF16 = jnp.bfloat16
NN = (((1,), (0,)), ((), ()))
NT = (((1,), (1,)), ((), ()))
TN = (((0,), (0,)), ((), ()))
MIB = 2**20
FFN_CUT = 2
BACK_CUT = 1
VMEM = 32 * MIB
ATTEND_VMEM = 28 * MIB
FFN_VMEM = 30 * MIB
BACK_VMEM = 26 * MIB
ATTEND_BACK_VMEM = 24 * MIB
WHOLE = pl.BlockSpec(memory_space=pltpu.VMEM)
TICK = jax.ShapeDtypeStruct((1, 1), jnp.float32)
TICK1 = pl.BlockSpec((1, 1), lambda i: (0, 0))
TICK2 = pl.BlockSpec((1, 1), lambda i, g: (0, 0))
TICK3 = pl.BlockSpec((1, 1), lambda i, g, me: (0, 0))
ANY = pl.BlockSpec(memory_space=pl.ANY)


def mm(a, b, dims=NN):
    return lax.dot_general(a, b, dims, preferred_element_type=F32)


def far(*arrays):
    return [pltpu.with_memory_space_constraint(v, pltpu.HBM) for v in arrays]


def whole(shape):
    return pl.BlockSpec(shape, lambda i: (0,) * len(shape), pipeline_mode=pl.Buffered(1))


def lead(shape):
    return pl.BlockSpec((1,) + shape, lambda i: (i,) + (0,) * len(shape))


def rows_of(tile, width):
    return pl.BlockSpec((tile, width), lambda i: (i, 0))


def shape_of(shape, dtype):
    return pltpu.HBM(shape, dtype)


def params(limit=VMEM):
    return pltpu.CompilerParams(vmem_limit_bytes=limit)


def cost(flops, nbytes):
    return pl.CostEstimate(flops=int(flops), bytes_accessed=int(nbytes), transcendentals=0)


def part_specs(parts, R, at, block_len, D):
    own = pl.BlockSpec((1, block_len, D), lambda i, g, me: (me[0] * R + at + i, 0, 0))
    specs = [own]
    for bit, (part, base) in enumerate(parts[1:]):
        shape = (1, 1) + part.shape[2:]
        place = lambda bit, base, i, g, me: (me[0] >> (bit + 1), at + i - base, 0, 0)
        specs.append(pl.BlockSpec(shape, functools.partial(place, bit, base)))
    return specs


def arrays_of(parts):
    return [parts[0]] + [part for part, _ in parts[1:]]


def merge(refs):
    return jnp.concatenate([refs[0][0]] + [ref[0, 0] for ref in refs[1:]], 0)


def attend_kernel(me_ref, *refs, nparts, heads, hs, group, scale, nio, row, ncarry):
    carried, refs = refs[:ncarry], refs[ncarry:]
    parts, (code_ref, wt_ref, bt_ref, wo_ref, vec_ref) = refs[:nparts], refs[nparts : nparts + 5]
    outs = refs[nparts + 5 + nio :]
    x_far, qkv_far, p_ref, il_ref, att_ref, first_ref, n_ref, s_ref, tick_ref = outs[:9]
    kept, (x_ref, qkv_ref, sems) = outs[9:-3], outs[-3:]
    tick_ref[...] = jnp.zeros_like(tick_ref)
    D = heads * hs
    L = x_ref.shape[1]
    step = pl.program_id(1)
    copies = [
        pltpu.make_async_copy(x_ref, x_far.at[pl.ds(row, 1)], sems.at[0]),
        pltpu.make_async_copy(qkv_ref, qkv_far.at[pl.ds(row, 1)], sems.at[1]),
    ] + [pltpu.make_async_copy(a, b, sems.at[2 + i]) for i, (a, b) in enumerate(zip(carried, kept))]

    @pl.when(step == 0)
    def _():
        x_ref[0] = merge(parts)
        f = mm(wt_ref[...], x_ref[0], NT) + bt_ref[:, 0:1]
        qkv_ref[0, :D, :] = (f[:D].astype(BF16).astype(F32) * scale).astype(BF16)
        qkv_ref[0, D:, :] = f[D:].astype(BF16)
        for copy in copies:
            copy.start()

    it = lax.broadcasted_iota(jnp.int32, (CODES, L), 0)

    def head(i):
        at = pl.multiple_of((step * group + i) * hs, hs)
        return [qkv_ref[0, pl.ds(j * D + at, hs), :] for j in range(3)]

    bound = jnp.zeros((1, 1), F32)
    for i in range(group):
        q, k, _ = head(i)
        norms = [
            jnp.max(jnp.sum(v.astype(F32) * v.astype(F32), axis=0, keepdims=True), axis=1, keepdims=True)
            for v in (q, k)
        ]
        bound = jnp.maximum(bound, norms[0] * norms[1])
    small = bound[0, 0] <= NO_SHIFT * NO_SHIFT

    def attend_group(shifted):
        for i in range(group):
            at = pl.multiple_of((step * group + i) * hs, hs)
            q, k, v = head(i)
            same = it == code_ref[0, 0, i : i + 1, :]
            qa = jnp.concatenate([q, jnp.where(same, BIG, 0.0).astype(BF16)], 0)
            ka = jnp.concatenate([k, jnp.where(same, 0.0, -BIG).astype(BF16)], 0)
            s = mm(ka, qa, TN)
            if shifted:
                s = s - jnp.max(s, axis=0, keepdims=True)
            p = jnp.exp(s).astype(BF16)
            p_ref[0, i] = p
            o = mm(jnp.concatenate([v, jnp.ones((16, L), BF16)], 0), p)
            il = 1.0 / o[hs : hs + 1]
            il_ref[0, 0, i : i + 1, :] = il
            att_ref[0, pl.ds(at, hs), :] = (o[:hs] * il).astype(BF16)

    @pl.when(small)
    def _():
        attend_group(False)

    @pl.when(jnp.logical_not(small))
    def _():
        attend_group(True)

    @pl.when(step == heads // group - 1)
    def _():
        v1 = x_ref[0].astype(F32) + mm(att_ref[0], wo_ref[...], TN) + vec_ref[0:1, :]
        c = v1 - jnp.mean(v1, -1, keepdims=True)
        s1 = lax.rsqrt(jnp.mean(c * c, -1, keepdims=True) + NORM_EPS)
        n1 = c * s1
        first_ref[0] = (n1 * vec_ref[1:2, :] + vec_ref[2:3, :]).astype(BF16)
        n_ref[0] = n1.astype(BF16)
        s_ref[0] = jnp.broadcast_to(s1, (L, 128))
        for copy in copies:
            copy.wait()


def attend(me, parts, at, R, code, wt, bt, wo, vec, heads, hs, scale, group, deps, held, carry=()):
    r = 1
    D = wo.shape[0]
    L = code.shape[-1]
    here = lambda shape: pl.BlockSpec((1,) + shape, lambda i, g, me: (at + i,) + (0,) * len(shape))
    grouped = lambda shape: pl.BlockSpec((1, 1) + shape, lambda i, g, me: (at + i, g, 0, 0))
    shapes = [
        shape_of((R, L, D), BF16),
        shape_of((R, 3 * D, L), BF16), shape_of((R, heads, L, L), BF16),
        shape_of((R, heads // group, group, L), F32), shape_of((R, D, L), BF16),
        shape_of((R, L, D), BF16), shape_of((R, L, D), BF16), shape_of((R, L, 128), F32),
        TICK,
    ]
    nio = len(held) + len(deps)
    np_ = len(parts)
    return pl.pallas_call(
        functools.partial(
            attend_kernel, nparts=np_, heads=heads, hs=hs, group=group, scale=scale, nio=nio,
            row=at, ncarry=len(carry),
        ),
        grid_spec=pltpu.PrefetchScalarGridSpec(
            num_scalar_prefetch=1,
            grid=(r, heads // group),
            in_specs=[ANY] * len(carry) + part_specs(parts, R, at, parts[0].shape[1], D) + [
                grouped((group, L)), WHOLE, WHOLE, WHOLE, WHOLE,
            ] + [ANY] * nio,
            out_specs=[
                ANY, ANY, pl.BlockSpec((1, group, L, L), lambda i, g, me: (at + i, g, 0, 0)),
                grouped((group, L)), here((D, L)), here((L, D)), here((L, D)), here((L, 128)),
                TICK3,
            ] + [WHOLE] * len(carry),
            scratch_shapes=[
                pltpu.VMEM((1, L, D), BF16), pltpu.VMEM((1, 3 * D, L), BF16),
                pltpu.SemaphoreType.DMA((2 + len(carry),)),
            ],
        ),
        out_shape=shapes + [pltpu.VMEM(v.shape, v.dtype) for v in carry],
        input_output_aliases={1 + len(carry) + np_ + 5 + len(deps) + i: i for i in range(len(held))},
        compiler_params=params(ATTEND_VMEM),
        cost_estimate=cost(r * (8 * L * D * D + 4 * 4 * heads * L * L * hs), r * 2 * heads * L * L),
        name="attend",
    )(me, *carry, *arrays_of(parts), code, wt, bt, wo, vec, *deps, *held)


def prepare_kernel(me_ref, w_ref, b_ref, perm_ref, seg_ref, *rest, seq):
    wt_ref, bt_ref, code_ref = rest[-3:]
    wt_ref[...] = w_ref[...].T
    bt_ref[...] = b_ref[...].T
    heads, _, L = perm_ref.shape
    R, _, group = code_ref.shape[:3]
    me = me_ref[0]
    block = L // seq
    high = lax.broadcasted_iota(jnp.int32, (8, L), 0)
    low = lax.broadcasted_iota(jnp.int32, (128, L), 0)
    member = (lax.broadcasted_iota(jnp.int32, (8, L), 1) // CL).astype(F32)
    for r in range(R):
        seg = seg_ref[pl.ds(me * R + r, 1), :]
        for bit in bits_of(seq):
            blocks = [seg[:, i * block : (i + 1) * block] for i in range(seq)]
            turned = jnp.concatenate([blocks[i ^ (1 << bit)] for i in range(seq)], 1)
            seg = jnp.where(((me >> bit) & 1) == 1, turned, seg)
        for h in range(heads):
            place = perm_ref[h, pl.ds(me * R + r, 1), :] ^ (me * block)
            a = jnp.where((place >> 7) == high, member, 0.0).astype(BF16)
            b = ((place & 127) == low).astype(BF16)
            table = mm(a, b, NT)
            row = jnp.concatenate([table[i : i + 1, :] for i in range(L // 128)], 1)
            code_ref[r, h // group, h % group : h % group + 1, :] = row.astype(jnp.int32) * DOCS + seg


def prepare(me, seq, w, b, perm, segs, group, deps):
    heads, rows, L = perm.shape
    R = rows // seq
    D, D3 = w.shape
    full = lambda shape: pl.BlockSpec(shape, lambda i, me: (0,) * len(shape))
    codes = (R, heads // group, group, L)
    return pl.pallas_call(
        functools.partial(prepare_kernel, seq=seq),
        grid_spec=pltpu.PrefetchScalarGridSpec(
            num_scalar_prefetch=1,
            grid=(1,),
            in_specs=[
                full((D, D3)), full((8, D3)), full(perm.shape),
                full(segs.shape),
            ] + [ANY] * len(deps),
            out_specs=[full((D3, D)), full((D3, 8)), full(codes)],
        ),
        out_shape=[
            jax.ShapeDtypeStruct((D3, D), BF16), jax.ShapeDtypeStruct((D3, 8), F32),
            jax.ShapeDtypeStruct(codes, jnp.int32),
        ],
        compiler_params=params(32 * MIB),
        cost_estimate=cost(4e9, 8e6),
        name="prepare",
    )(me, w, b, perm, segs, *deps)


def ffn_kernel(me_ref, *refs, nparts, nio):
    parts, (first_ref, wu_ref, bu_ref, wd_ref, vec_ref) = refs[:nparts], refs[nparts : nparts + 5]
    lo_ref, hi_ref, gffn_ref, act_ref, slope_ref, sums_ref, tick_ref = refs[nparts + 5 + nio :]
    tick_ref[...] = jnp.zeros_like(tick_ref)
    @pl.when(pl.program_id(0) == 0)
    def _():
        sums_ref[...] = jnp.zeros_like(sums_ref)

    go_all = merge(parts)
    tile = first_ref.shape[0]
    sub = tile // FFN_CUT
    for cut in range(FFN_CUT):
        here = slice(cut * sub, (cut + 1) * sub)
        first = first_ref[here, :]
        u = mm(first, wu_ref[...]) + bu_ref[...]
        half = 0.5 * (1.0 + lax.erf(u * 0.7071067811865476))
        act = (u * half).astype(BF16)
        act_ref[here, :] = act
        slope_ref[here, :] = (half + u * jnp.exp(-0.5 * u * u) * 0.3989422804014327).astype(BF16)
        y = first.astype(F32) + mm(act, wd_ref[...]) + vec_ref[3:4, :]
        c = y - jnp.mean(y, -1, keepdims=True)
        s2 = lax.rsqrt(jnp.mean(c * c, -1, keepdims=True) + NORM_EPS)
        n2 = c * s2
        out = (n2 * vec_ref[4:5, :] + vec_ref[5:6, :]).astype(BF16)
        if cut < FFN_CUT // 2:
            lo_ref[0, here, :] = out
        elif FFN_CUT > 1:
            hi_ref[0, cut * sub - tile // 2 : (cut + 1) * sub - tile // 2, :] = out
        else:
            lo_ref[0] = out[: tile // 2]
            hi_ref[0] = out[tile // 2 :]
        go = go_all[here].astype(F32)
        e = go * vec_ref[4:5, :]
        g2 = s2 * (e - jnp.mean(e, -1, keepdims=True) - n2 * jnp.mean(e * n2, -1, keepdims=True))
        gl = g2.astype(BF16)
        gffn_ref[here, :] = gl
        sums_ref[0:1, :] += jnp.sum(gl.astype(F32), 0, keepdims=True)
        sums_ref[1:2, :] += jnp.sum(go * n2, 0, keepdims=True)
        sums_ref[2:3, :] += jnp.sum(go, 0, keepdims=True)


def ffn(me, first, parts, at, r, R, wu, bu, wd, vec, deps, held):
    T, D = first.shape
    L = T // R
    FF = wu.shape[1]
    here = lambda width: pl.BlockSpec((L, width), lambda i, g, me: (at + i, 0))
    nio = len(held) + len(deps)
    np_ = len(parts)
    half = pl.BlockSpec((1, L // 2, D), lambda i, g, me: (i, 0, 0))
    return pl.pallas_call(
        functools.partial(ffn_kernel, nparts=np_, nio=nio),
        grid_spec=pltpu.PrefetchScalarGridSpec(
            num_scalar_prefetch=1,
            grid=(r, 1),
            in_specs=part_specs(parts, R, at, parts[0].shape[1], D) + [
                here(D), WHOLE, WHOLE, WHOLE, WHOLE,
            ] + [ANY] * nio,
            out_specs=[
                half, half, here(D), here(FF), here(FF),
                pl.BlockSpec((8, D), lambda i, g, me: (0, 0)), TICK3,
            ],
        ),
        out_shape=[
            shape_of((r, L // 2, D), BF16), shape_of((r, L // 2, D), BF16), shape_of((T, D), BF16),
            shape_of((T, FF), BF16), shape_of((T, FF), BF16), shape_of((8, D), F32),
            TICK,
        ],
        input_output_aliases={1 + np_ + 5 + len(deps) + i: 2 + i for i in range(len(held))},
        compiler_params=params(FFN_VMEM),
        cost_estimate=cost(4 * r * L * D * FF * 1.3, 4 * r * L * FF + 4 * D * FF),
        name="ffn",
    )(me, *arrays_of(parts), *far(first), wu, bu, wd, vec, *deps, *held)


def by_core(total, place):
    rows, width = total.shape
    bits = len(place) + 1
    cube = total.reshape((2,) * bits + (rows >> bits, width))
    cube = cube.transpose((bits - 1,) + tuple(place) + (bits, bits + 1))
    return cube[0].reshape(rows // 2, width), cube[1].reshape(rows // 2, width)


def put_halves(me_ref, total, place, send_ref, keep_ref):
    even, odd = by_core(total, place)
    mine = me_ref[0] % 2 == 0
    send_ref[...] = jnp.where(mine, odd, even).astype(BF16)
    keep_ref[...] = jnp.where(mine, even, odd).astype(BF16)


def halves_of(me, total, place):
    even, odd = by_core(total, place)
    mine = me[0] % 2 == 0
    return jnp.where(mine, odd, even), jnp.where(mine, even, odd)


def places(dp, seq, order):
    names = [("dp", b) for b in reversed(bits_of(dp))] + [("seq", b) for b in reversed(bits_of(seq))]
    return [names.index(item) for item in order]


def splits(rows, n):
    return (rows // n) % 8 == 0


def down_grad_kernel(me_ref, act_ref, g_ref, *rest, place, ndep):
    outs = rest[ndep:]
    total = mm(act_ref[...], g_ref[...], TN)
    if len(outs) == 2:
        put_halves(me_ref, total, place, *outs)
    else:
        outs[0][...] = total.astype(BF16)


def down_grad(me, dp, seq, order, act, g, deps):
    T, FF = act.shape
    D = g.shape[1]
    n = dp * seq
    inside = splits(FF, n) and FF // dp % 128 == 0
    steps = dp if inside else 8
    tile = FF // steps
    place = places(dp, seq, order)
    inner = [p - len(bits_of(dp)) for p in place if p >= len(bits_of(dp))]
    turns = [bit for name, bit in order if name == "dp"]

    def at(i):
        where = 0
        for bit in turns:
            where = 2 * where + ((i >> bit) & 1)
        return (where, 0)

    res = pl.pallas_call(
        functools.partial(down_grad_kernel, place=inner, ndep=len(deps)),
        grid=(steps,),
        in_specs=[
            pl.BlockSpec(memory_space=pltpu.SMEM), pl.BlockSpec((T, tile), lambda i: (0, i)), whole((T, D)),
        ] + [ANY] * len(deps),
        out_specs=[pl.BlockSpec((tile // 2, D), at)] * 2 if inside else [rows_of(tile, D)],
        out_shape=[shape_of((FF // 2, D), BF16)] * 2 if inside else [shape_of((FF, D), BF16)],
        compiler_params=params(18 * MIB),
        cost_estimate=cost(2 * T * D * FF * 1.3, 2 * T * FF + 2 * D * FF),
        name="down_grad",
    )(me, *far(act, g), *deps)
    return res if inside else halves_of(me, res[0], place)


def ffn_back_kernel(
    g_ref, slope_ref, wu_ref, wd_ref, wo_ref, n_ref, s_ref, vec_ref, att_ref, il_ref, *rest,
    heads, hs,
):
    gpre_ref, gbr_ref, do_ref, de_ref, sums_ref, bsum_ref, tick_ref = rest[-7:]
    tick_ref[...] = jnp.zeros_like(tick_ref)
    @pl.when((pl.program_id(0) == 0) & (pl.program_id(1) == 0))
    def _():
        sums_ref[...] = jnp.zeros_like(sums_ref)
        bsum_ref[...] = jnp.zeros_like(bsum_ref)

    sub = g_ref.shape[0] // BACK_CUT
    for cut in range(BACK_CUT):
        here = slice(cut * sub, (cut + 1) * sub)
        g = g_ref[here, :]
        gp = (mm(g, wd_ref[...], NT) * slope_ref[here, :].astype(F32)).astype(BF16)
        gpre_ref[here, :] = gp
        gfirst = mm(gp, wu_ref[...], NT) + g.astype(F32)
        n1 = n_ref[0, here, :].astype(F32)
        e = gfirst * vec_ref[1:2, :]
        g1 = s_ref[0, here, 0:1] * (
            e - jnp.mean(e, -1, keepdims=True) - n1 * jnp.mean(e * n1, -1, keepdims=True)
        )
        gl = g1.astype(BF16)
        gbr_ref[0, here, :] = gl
        da = mm(wo_ref[...], gl, NT)
        group = il_ref.shape[2]
        for h in range(heads):
            i, j = h // group, h % group
            il = il_ref[0, i, j : j + 1, here]
            piece = da[h * hs : (h + 1) * hs, :] * il
            do_ref[0, h * hs : (h + 1) * hs, here] = piece.astype(BF16)
            att = att_ref[0, h * hs : (h + 1) * hs, here].astype(F32)
            de_ref[0, i, j : j + 1, here] = jnp.sum(piece * att, axis=0, keepdims=True)
        sums_ref[0:1, :] += jnp.sum(gl.astype(F32), 0, keepdims=True)
        sums_ref[1:2, :] += jnp.sum(gfirst * n1, 0, keepdims=True)
        sums_ref[2:3, :] += jnp.sum(gfirst, 0, keepdims=True)
        bsum_ref[0:1, :] += jnp.sum(gp.astype(F32), 0, keepdims=True)


def ffn_back(at, r, g, slope, wu, wd, wo, n1, s1, vec, att, il, heads, hs, deps, held):
    T, D = g.shape
    FF = wu.shape[1]
    R, L = n1.shape[:2]
    half = L // 2
    flat = lambda width: pl.BlockSpec((half, width), lambda i, g: (2 * (at + i) + g, 0))
    fixed = lambda shape: pl.BlockSpec(
        shape, lambda i, g: (0,) * len(shape), pipeline_mode=pl.Buffered(1)
    )
    tokens = lambda width: pl.BlockSpec((1, half, width), lambda i, g: (at + i, g, 0))
    columns = lambda *lead: pl.BlockSpec(
        (1,) + lead + (half,), lambda i, g: (at + i,) + (0,) * len(lead) + (g,)
    )
    extra = list(deps) + list(held)
    return pl.pallas_call(
        functools.partial(ffn_back_kernel, heads=heads, hs=hs),
        grid=(r, 2),
        in_specs=[
            flat(D), flat(FF), WHOLE, WHOLE, fixed((D, D)), tokens(D), tokens(128), fixed((8, D)),
            columns(D), columns(*il.shape[1:3]),
        ] + [ANY] * len(extra),
        out_specs=[
            flat(FF), tokens(D), columns(D), columns(*il.shape[1:3]),
            pl.BlockSpec((8, D), lambda i, g: (0, 0)), pl.BlockSpec((8, FF), lambda i, g: (0, 0)),
            TICK2,
        ],
        out_shape=[
            shape_of((T, FF), BF16), shape_of((R, L, D), BF16), shape_of((R, D, L), BF16),
            shape_of(il.shape, F32), shape_of((8, D), F32), shape_of((8, FF), F32),
            TICK,
        ],
        input_output_aliases={10 + len(deps) + i: i for i in range(len(held))},
        compiler_params=params(BACK_VMEM),
        cost_estimate=cost(4 * r * L * D * FF * 1.5, 4 * r * L * FF + 4 * D * FF),
        name="ffn_back",
    )(*far(g, slope), wu, wd, *far(wo, n1, s1, vec, att, il), *extra)


def up_out_grad_kernel(me_ref, x_ref, g_ref, att_far, gbr_far, *rest, place, ndep):
    outs, tick_ref, att_ref, gbr_ref, sems = rest[ndep:-4], rest[-4], rest[-3], rest[-2], rest[-1]
    tick_ref[...] = jnp.zeros_like(tick_ref)
    last = pl.num_programs(0) - 1

    def put(total):
        if len(outs) == 2:
            put_halves(me_ref, total, place, *outs)
        else:
            outs[0][...] = total.astype(BF16)

    copies = [
        pltpu.make_async_copy(att_far, att_ref, sems.at[0]),
        pltpu.make_async_copy(gbr_far, gbr_ref, sems.at[1]),
    ]

    @pl.when(pl.program_id(0) == 0)
    def _():
        for copy in copies:
            copy.start()

    @pl.when(pl.program_id(0) < last)
    def _():
        put(mm(x_ref[...], g_ref[...], TN))

    @pl.when(pl.program_id(0) == last)
    def _():
        for copy in copies:
            copy.wait()
        total = mm(att_ref[0], gbr_ref[0])
        for r in range(1, att_ref.shape[0]):
            total = total + mm(att_ref[r], gbr_ref[r])
        put(total)


def up_out_grad(me, dp, seq, order, x, g, att, gbr, deps):
    T, D = x.shape
    FF = g.shape[1]
    R, _, L = att.shape
    place = places(dp, seq, order)
    inside = splits(D, dp * seq)
    rows, count = (D // 2, 2) if inside else (D, 1)
    steps = FF // D
    *res, tick = pl.pallas_call(
        functools.partial(up_out_grad_kernel, place=place, ndep=len(deps)),
        grid=(steps + 1,),
        in_specs=[
            pl.BlockSpec(memory_space=pltpu.SMEM), whole((T, D)),
            pl.BlockSpec((T, D), lambda i: (0, jnp.minimum(i, steps - 1))), ANY, ANY,
        ] + [ANY] * len(deps),
        out_specs=[pl.BlockSpec((rows, D), lambda i: (0, i))] * count + [TICK1],
        out_shape=[jax.ShapeDtypeStruct((rows, FF + D), BF16)] * count + [TICK],
        scratch_shapes=[
            pltpu.VMEM((R, D, L), BF16), pltpu.VMEM((R, L, D), BF16), pltpu.SemaphoreType.DMA((2,)),
        ],
        compiler_params=params(),
        cost_estimate=cost(1, 1),
        name="up_out_grad",
    )(me, *far(x, g, att, gbr), *deps)
    return (res if inside else halves_of(me, res[0], place)), tick


def attend_back_kernel(
    qkv_ref, p_ref, do_ref, de_ref, gone_ref, wt_ref, *rest, heads, hs, scale, group
):
    g_out, lo_ref, hi_ref, tick_ref, g_ref = rest[-5:]
    tick_ref[...] = jnp.zeros_like(tick_ref)
    step = pl.program_id(1)
    for i in range(group):
        here = slice(i * hs, (i + 1) * hs)
        q, k, v = [qkv_ref[0, j, here, :] for j in range(3)]
        do = do_ref[0, here, :]
        p = p_ref[0, i]
        dp = mm(v, do, TN)
        ds = (p.astype(F32) * (dp - de_ref[0, 0, i : i + 1, :])).astype(BF16)
        grads = [mm(k, ds) * scale, mm(q, ds, NT), mm(do, p, NT)]
        for j in range(3):
            part = grads[j].astype(BF16)
            g_out[0, j, here, :] = part
            g_ref[j, step, here, :] = part

    @pl.when(step == heads // group - 1)
    def _():
        g = g_ref[...].reshape(3 * heads * hs, g_ref.shape[-1])
        gin = (mm(g, wt_ref[...], TN) + gone_ref[0].astype(F32)).astype(BF16)
        half_len = gin.shape[0] // 2
        lo_ref[0] = gin[:half_len]
        hi_ref[0] = gin[half_len:]


def attend_back(at, r, of, place, qkv, p, do, de, gone, wt, heads, hs, scale, group, deps, held):
    R, D3, L = qkv.shape
    D = D3 // 3
    here = lambda shape: pl.BlockSpec((1,) + shape, lambda i, g: (at + i,) + (0,) * len(shape))
    extra = list(deps) + [v for v in held if v is not None]
    aliases = {}
    for i, v in enumerate(held):
        if v is not None:
            aliases[6 + len(deps) + len(aliases)] = i
    half = pl.BlockSpec((1, L // 2, D), lambda i, g: (place + i, 0, 0))
    heads_of = pl.BlockSpec((1, 3, group * hs, L), lambda i, g: (at + i, 0, g, 0))
    g, *rest = pl.pallas_call(
        functools.partial(attend_back_kernel, heads=heads, hs=hs, scale=scale, group=group),
        grid=(r, heads // group),
        in_specs=[
            heads_of, pl.BlockSpec((1, group, L, L), lambda i, g: (at + i, g, 0, 0)),
            pl.BlockSpec((1, group * hs, L), lambda i, g: (at + i, g, 0)),
            pl.BlockSpec((1, 1, group, L), lambda i, g: (at + i, g, 0, 0)),
            here((L, D)), WHOLE,
        ] + [ANY] * len(extra),
        out_specs=[heads_of, half, half, TICK2],
        out_shape=[
            shape_of((R, 3, D, L), BF16), shape_of((of, L // 2, D), BF16),
            shape_of((of, L // 2, D), BF16), TICK,
        ],
        scratch_shapes=[pltpu.VMEM((3, heads // group, group * hs, L), BF16)],
        input_output_aliases=aliases,
        compiler_params=params(ATTEND_BACK_VMEM),
        cost_estimate=cost(r * (6 * L * D * D + 4 * 8 * heads * L * L * hs), r * 2 * heads * L * L),
        name="attend_back",
    )(*far(qkv.reshape(R, 3, D, L), p, do, de, gone), wt, *extra)
    return [g, *rest]


def spots(widths):
    out, at = [], 0
    for width in widths:
        if at % 128 + width > 128:
            at = 128 * -(-at // 128)
        out.append(at)
        at += width
    return out


def pack(sums, n, windows):
    widths = [terms[0].shape[1] // n for terms in sums]
    pieces = [jnp.zeros((n, 128), F32) for _ in range(windows)]
    for terms, width, at in zip(sums, widths, spots(widths)):
        v = functools.reduce(jnp.add, terms)
        W = v.shape[1]
        owner = lax.broadcasted_iota(jnp.int32, (n, W), 0)
        place = lax.broadcasted_iota(jnp.int32, (n, W), 1)
        a = jnp.where((place >= owner * width) & (place < (owner + 1) * width), v, 0.0).astype(BF16)
        index = lax.broadcasted_iota(jnp.int32, (W, 128), 0)
        start = ((index.astype(F32) + 0.5) * (1.0 / width)).astype(jnp.int32) * width
        b = (lax.broadcasted_iota(jnp.int32, (W, 128), 1) == index - start + at % 128).astype(BF16)
        pieces[at // 128] += mm(a, b)
    return pieces


def qkv_grad_kernel(me_ref, x_ref, g_ref, *rest, spans, nsum, ndep, n, count, place, windows):
    sums_refs, outs = rest[:nsum], rest[nsum + ndep : -3]
    tick_ref, first_ref, xt_ref = rest[-3:]
    tick_ref[...] = jnp.zeros_like(tick_ref)
    step, steps = pl.program_id(0), len(place)
    D = x_ref.shape[2]

    def put(total, which):
        refs = outs[which * count : (which + 1) * count]
        if count == 2:
            put_halves(me_ref, total, place[which], *refs)
        else:
            refs[0][...] = total.astype(BF16)

    @pl.when(step == 0)
    def _():
        for r in range(x_ref.shape[0]):
            xt_ref[r, :D, :] = x_ref[r].T
            xt_ref[r, D:, :] = jnp.ones((xt_ref.shape[1] - D, x_ref.shape[1]), BF16)

    both = mm(xt_ref[0], g_ref[0], NT)
    for r in range(1, x_ref.shape[0]):
        both = both + mm(xt_ref[r], g_ref[r], NT)
    total, over = both[:D], both[D : D + 1]

    @pl.when(step == 0)
    def _():
        first_ref[...] = over

    for which in range(steps - 1):
        @pl.when(step == which)
        def _(which=which):
            put(total, which)

    @pl.when(step == steps - 1)
    def _():
        row = lax.broadcasted_iota(jnp.int32, (n, D // n, 128), 1)
        packed = jnp.zeros((n, D // n, 128), F32)
        sums = [[jnp.concatenate([first_ref[...], over], 1)]] + [
            [jnp.concatenate([sums_refs[i][line : line + 1, lo:hi] for lo, hi in cols], 1) for i in terms]
            for terms, line, cols in spans
        ]
        for i, piece in enumerate(pack(sums, n, windows)):
            packed = jnp.where(row == i, piece[:, None, :], packed)
        put(jnp.concatenate([total, packed.reshape(D, 128)], 1), steps - 1)


def qkv_grad(me, dp, seq, orders, x, g, sums, spans, deps):
    R, L, D = x.shape
    n = dp * seq
    place = [places(dp, seq, order) for order in orders]
    real = len(place)
    inside = splits(D, n)
    rows, count = (D // 2, 2) if inside else (D, 1)
    widths = [D] * (real - 1) + [D + 128]
    parts = [2 * D // n] + [sum(hi - lo for lo, hi in cols) // n for _, _, cols in spans]
    windows = spots(parts)[-1] // 128 + 1
    *res, tick = pl.pallas_call(
        functools.partial(
            qkv_grad_kernel, spans=spans, nsum=len(sums), ndep=len(deps), n=n, count=count, place=place,
            windows=windows,
        ),
        grid=(real,),
        in_specs=[
            pl.BlockSpec(memory_space=pltpu.SMEM), whole((R, L, D)),
            pl.BlockSpec((R, D, L), lambda i: (0, i, 0)),
        ] + [whole(v.shape) for v in sums] + [ANY] * len(deps),
        out_specs=[
            pl.BlockSpec((rows, width), lambda i: (0, 0)) for width in widths for _ in range(count)
        ] + [TICK1],
        out_shape=[
            jax.ShapeDtypeStruct((rows, width), BF16) for width in widths for _ in range(count)
        ] + [TICK],
        scratch_shapes=[pltpu.VMEM((1, D), F32), pltpu.VMEM((R, D + 16, L), BF16)],
        compiler_params=params(),
        cost_estimate=cost(6 * R * L * D * D * 1.3, 8 * R * L * D),
        name="qkv_grad",
    )(me, *far(x, g), *sums, *deps)
    pieces = [res[i * count : (i + 1) * count] for i in range(real)]
    return [piece if inside else halves_of(me, piece[0], at) for piece, at in zip(pieces, place)], tick


def bits_of(size):
    return [b for b in range(size.bit_length() - 1)]


def flip(x, axis, size, bit):
    return lax.ppermute(x, axis, [(i, i ^ (1 << bit)) for i in range(size)])


def my_bit(axis, bit):
    return (lax.axis_index(axis) >> bit) & 1


def pick(x, index, axis):
    return lax.dynamic_index_in_dim(x, index, axis, keepdims=False)


def late(x, tick):
    return x if tick is None else x + tick.reshape(()).astype(x.dtype)


def move_kernel(me_ref, *refs, count, ndep, copies):
    srcs, outs, sems = refs[:count], refs[count + ndep : -1], refs[-1]
    me = me_ref[0]
    started = []
    for i, (src, at, out, to) in enumerate(copies):
        copy = pltpu.make_async_copy(srcs[src].at[at(me)], outs[out].at[to(me)], sems.at[i])
        copy.start()
        started.append(copy)
    for copy in started:
        copy.wait()


def move(me, srcs, shapes, copies, deps=()):
    return pl.pallas_call(
        functools.partial(move_kernel, count=len(srcs), ndep=len(deps), copies=copies),
        in_specs=[pl.BlockSpec(memory_space=pltpu.SMEM)] + [ANY] * (len(srcs) + len(deps)),
        out_specs=[ANY] * len(shapes),
        out_shape=[jax.ShapeDtypeStruct(shape, BF16) for shape in shapes],
        scratch_shapes=[pltpu.SemaphoreType.DMA((len(copies),))],
        compiler_params=params(4 * MIB),
        cost_estimate=cost(1, 1),
        name="move",
    )(me, *srcs, *deps)


def pass_on(arrays, after):
    return pl.pallas_call(
        lambda *refs: None,
        in_specs=[ANY] * (len(arrays) + len(after)),
        out_specs=[ANY] * len(arrays),
        out_shape=[jax.ShapeDtypeStruct(v.shape, v.dtype) for v in arrays],
        input_output_aliases={i: i for i in range(len(arrays))},
        compiler_params=params(4 * MIB),
        cost_estimate=cost(1, 1),
        name="pass_on",
    )(*arrays, *after)


class Rows:
    def __init__(self, x, axis, size):
        self.x, self.axis, self.size = x, axis, size
        self.bits = bits_of(size)
        self.R, self.B, self.D = x.shape[0] // size, x.shape[1], x.shape[2]
        self.came = [[] for _ in self.bits]

    def find(self, bit, start):
        return [(v, base) for v, base in self.came[bit] if base <= start][-1]

    def plan(self, bit, start, stop, srcs, copies, out):
        r, B, R = stop - start, self.B, self.R
        lead = 1 << (len(self.bits) - 1 - bit)
        for high in range(lead):
            def owner(me, high=high):
                return (high << (bit + 1)) + (me ^ (1 << bit)) % (1 << (bit + 1))

            def own(me, owner=owner):
                return (pl.ds(owner(me) * R + start, r),)

            def place(lo, hi, high=high):
                return lambda me: (high, slice(None), pl.ds(lo, hi - lo))

            copies.append((len(srcs), own, out, place(0, B)))
            for done in range(bit):
                got, base = self.find(done, start)

                def theirs(me, owner=owner, done=done, base=base):
                    return (owner(me) >> (done + 1), pl.ds(start - base, r))

                copies.append((len(srcs) + 1 + done, theirs, out, place(B << done, B << (done + 1))))
        srcs.append(self.x)
        srcs.extend(self.find(done, start)[0] for done in range(bit))
        return (lead, r, B << bit, self.D)

    def send(self, bit, start, send):
        self.came[bit].append((flip(send, self.axis, self.size, bit), start))

    def parts(self, start):
        return [self.x] + [self.find(bit, start) for bit in self.bits]


def gather(me, jobs, deps=()):
    srcs, copies, shapes = [], [], []
    for out, (rows, bit, start, stop) in enumerate(jobs):
        shapes.append(rows.plan(bit, start, stop, srcs, copies, out))
    return move(me, srcs, shapes, copies, deps)


def exchange(me, jobs, deps=()):
    sends = gather(me, jobs, deps)
    for (rows, bit, start, stop), send in zip(jobs, sends):
        rows.send(bit, start, send)
    return sends


class Blocks:
    def __init__(self, axis, size):
        self.axis, self.size, self.chunks = axis, size, []

    def send(self, lo, hi):
        self.chunks.append((lo, flip(hi, self.axis, self.size, bits_of(self.size)[-1])))

    def turn(self, me, tick):
        bits, axis, size = bits_of(self.size), self.axis, self.size
        half, D = self.chunks[0][0].shape[1:]
        self.R = R = sum(lo.shape[0] for lo, _ in self.chunks)
        self.pieces = pieces = {0: [], 1 << bits[-1]: []}
        at = 0
        for chunk in self.chunks:
            for name, v in zip(pieces, chunk):
                pieces[name].append((v, (), at, v.shape[0], 0))
            at += chunk[0].shape[0]
        for bit in reversed(bits[:-1]):
            half //= 2
            names = list(pieces)
            join = lambda vs: vs[0] if len(vs) == 1 else jnp.concatenate(vs, 0)
            send = jnp.stack([
                join([v[front + (slice(None), slice(token + half, token + 2 * half))] for v, front, _, _, token in pieces[name]])
                for name in names
            ], 0)
            send = late(send, tick)
            self.came = flip(send, axis, size, bit)
            for i, name in enumerate(names):
                pieces[name | (1 << bit)] = [(self.came, (i,), 0, R, 0)]
        self.shape = (size * R, half, D)

    def result(self, me, tick):
        half, D = self.shape[1:]
        entries = [(name,) + source for name, sources in self.pieces.items() for source in sources]
        block = functools.reduce(math.gcd, [rows for _, _, _, _, rows, _ in entries])
        starts = [sum(e[4] // block for e in entries[:i]) for i in range(len(entries) + 1)]
        R = self.R

        def source_spec(e, start, stop):
            _, v, front, _, _, _ = e
            lead = (1,) * len(front)

            def at(i, me):
                return front + (jnp.clip(i, start, stop - 1) - start, 0, 0)

            return pl.BlockSpec(lead + (block, half, D), at)

        def target(i, me):
            where = 0
            for (name, _, _, row, _, _), start, stop in zip(entries, starts, starts[1:]):
                here = ((me[0] ^ name) * R + row) // block + i - start
                where = jnp.where((i >= start) & (i < stop), here, where)
            return (where, 0, 0)

        def kernel(me_ref, *refs):
            i, out = pl.program_id(0), refs[-1]
            for ref, start, stop in zip(refs, starts, starts[1:]):
                @pl.when((i >= start) & (i < stop))
                def _(ref=ref):
                    out[...] = ref[...].reshape(out.shape)

        return pl.pallas_call(
            kernel,
            grid_spec=pltpu.PrefetchScalarGridSpec(
                num_scalar_prefetch=1,
                grid=(starts[-1],),
                in_specs=[source_spec(e, a, b) for e, a, b in zip(entries, starts, starts[1:])] + [ANY],
                out_specs=pl.BlockSpec((block, half, D), target),
            ),
            out_shape=shape_of(self.shape, BF16),
            compiler_params=params(16 * MIB),
            cost_estimate=cost(1, 1),
            name="place",
        )(me, *[e[1] for e in entries], tick)


class Sum:
    def __init__(self, halves, dp, seq, order):
        self.sizes = {"dp": dp, "seq": seq}
        self.order = list(order)
        self.send, self.keep = halves

    def begin(self, send=None):
        self.go("seq", 0, [self.send if send is None else send])

    def go(self, name, bit, sends):
        self.came = [flip(v, name, self.sizes[name], bit) for v in sends]

    def result(self, tick=None, start=0, stop=None):
        came = self.came[0][:, start:stop]
        return late(self.keep[:, start:stop].astype(F32) + came.astype(F32), tick)


def fold_kernel(me_ref, *refs, shapes, ndep, nthrough):
    nin = sum(2 + 2 * took for took, _ in shapes)
    ins, outs = refs[:nin], refs[nin + ndep + nthrough : len(refs) - nthrough]
    outs[-1][...] = jnp.zeros_like(outs[-1])
    for took, gave in shapes:
        keep, came, ins = ins[:2], (ins[2 : 2 + took], ins[2 + took : 2 + 2 * took]), ins[2 + 2 * took :]
        send_refs, keep_ref, outs = outs[:gave], outs[gave], outs[gave + 1 :]
        sums = []
        for base, parts in zip(keep, came):
            part = jnp.concatenate([ref[0] for ref in parts], 1) if took > 1 else parts[0][0]
            sums.append((base[0].astype(F32) + part.astype(F32)).astype(BF16))
        width = sums[0].shape[1] // gave
        for i, ref in enumerate(send_refs):
            ref[...] = sums[0][:, i * width : (i + 1) * width]
        keep_ref[...] = sums[1]


def fold(me, chains, deps=(), split=1, through=()):
    items = [chain.order.pop(0) for chain in chains]
    rows = [chain.keep.shape[0] // 2 for chain in chains]
    steps = max(s for s in (4, 2, 1) if s == 1 or all(r % (16 * s) == 0 for r in rows))
    ins, in_specs, out_specs, out_shape, shapes = [], [], [], [], []
    for chain, (name, bit), r in zip(chains, items, rows):
        tile, width = r // steps, chain.keep.shape[1]
        row = 0 if name == "dp" else 1
        gave = split if chain is chains[-1] else 1

        def half(other, width, row=row, bit=bit, tile=tile):
            return pl.BlockSpec(
                (1, tile, width), lambda i, me: (((me[row] >> bit) & 1) ^ other, i, 0)
            )

        view = lambda v, r=r: v.reshape(2, r, v.shape[1])
        ins += [view(chain.keep)] * 2 + [view(v) for v in chain.came] * 2
        in_specs += [half(1, width), half(0, width)]
        in_specs += [half(other, v.shape[1]) for other in (1, 0) for v in chain.came]
        out_specs += [pl.BlockSpec((tile, width // gave), lambda i, me: (i, 0))] * gave
        out_specs += [pl.BlockSpec((tile, width), lambda i, me: (i, 0))]
        out_shape += [shape_of((r, width // gave), BF16)] * gave
        out_shape += [jax.ShapeDtypeStruct((r, width), BF16)]
        shapes.append((len(chain.came), gave))
    res = pl.pallas_call(
        functools.partial(fold_kernel, shapes=shapes, ndep=len(deps), nthrough=len(through)),
        grid_spec=pltpu.PrefetchScalarGridSpec(
            num_scalar_prefetch=1,
            grid=(steps,),
            in_specs=in_specs + [ANY] * (len(deps) + len(through)),
            out_specs=out_specs + [pl.BlockSpec((1, 1), lambda i, me: (0, 0))] + [ANY] * len(through),
        ),
        out_shape=out_shape + [TICK] + [jax.ShapeDtypeStruct(v.shape, v.dtype) for v in through],
        input_output_aliases={
            1 + len(ins) + len(deps) + i: len(out_shape) + 1 + i for i in range(len(through))
        },
        compiler_params=params(16 * MIB),
        cost_estimate=cost(1, 1),
        name="fold",
    )(me, *ins, *deps, *through)
    tick, on = res[len(out_shape)], res[len(out_shape) + 1 :]
    sends = []
    for chain, (name, bit), (_, gave) in zip(chains, items, shapes):
        chain.go(name, bit, res[:gave])
        chain.keep = res[gave]
        sends += res[:gave]
        res = res[gave + 1 :]
    return (sends, tick, on) if through else (sends, tick)


def chunks_of(count, sizes):
    out, at = [], 0
    for size in sizes:
        stop = min(count, at + size)
        if stop > at:
            out.append((at, stop))
        at = stop
    return out + ([(at, count)] if at < count else [])


def shards(
    dp, seq, hidden_in, segment_ids, cluster_perm, w_qkv, bias_qv, w_out, bias_out, gain_attn,
    shift_attn, w_up, bias_up, w_down, bias_down, gain_ffn, shift_ffn, grad_out,
):
    row_count, block_len, D = hidden_in.shape
    heads = cluster_perm.shape[1]
    hs = D // heads
    L = segment_ids.shape[1]
    FF = w_up.shape[1]
    R = row_count // seq
    T = R * L
    group = 4
    scale = 1.0 / math.sqrt(hs)
    mine = lax.axis_index("seq")
    me = mine.reshape(1).astype(jnp.int32)
    both = jnp.stack([lax.axis_index("dp"), mine]).astype(jnp.int32)

    hidden, gout = Rows(hidden_in, "seq", seq), Rows(grad_out, "seq", seq)
    halves = chunks_of(R, (R // 2,))
    bits = bits_of(seq)
    exchange(me, [(hidden, 0, 0, 1)])
    for bit in bits[1:]:
        first_sent = exchange(me, [(hidden, bit, 0, 1)])
    rest = [(hidden, 0, 1, R)] if R > 1 else []
    exchange(me, rest + [(gout, 0, 0, R)], first_sent)

    bias = jnp.concatenate([bias_qv[:D], jnp.zeros((D,), F32), bias_qv[D:]])
    bias = jnp.broadcast_to(bias, (8, 3 * D))
    none = jnp.zeros((D,), F32)
    vec = jnp.stack([bias_out, gain_attn, shift_attn, bias_down, gain_ffn, shift_ffn, none, none])
    wt, bt, code = prepare(me, seq, w_qkv, bias, cluster_perm.transpose(1, 0, 2), segment_ids, group, first_sent)

    jobs = [(hidden, row, row + 1) for row in range(1, R)] + [(gout, *half) for half in halves]
    early = len(bits) == 2
    if early:
        queue = list(zip(jobs, gather(me, [(rows, bits[-1], a, b) for rows, a, b in jobs], first_sent)))
    else:
        queue = [(job, None) for job in jobs]

    def launch(after):
        if not queue:
            return after
        (rows, start, stop), send = queue.pop(0)
        if early:
            (send,) = pass_on([send], after)
            rows.send(bits[-1], start, send)
            return [send]
        for bit in bits[1:]:
            after = exchange(me, [(rows, bit, start, stop)], after)
        return after

    held, tick = (), None
    for row in range(R):
        deps = launch(first_sent if tick is None else [tick]) if row < R - 1 else []
        if row == R - 2:
            deps = deps + launch([tick] if tick is not None else first_sent)
        res = attend(
            me, hidden.parts(row), row, R, code, wt, bt, w_out, vec, heads, hs, scale, group, deps, held,
        )
        held, tick = res[:8], res[8]
    x, qkv, p, il, att, first, n1, s1 = held
    first = first.reshape(T, D)

    held, out_blocks, sums_ffn = (), Blocks("seq", seq), []
    for i, (start, stop) in enumerate(halves):
        deps = launch([tick])
        lo, hi, *held, sums, tick = ffn(
            me, first, gout.parts(start), start, stop - start, R, w_up, bias_up.reshape(1, -1), w_down,
            vec, deps, held,
        )
        out_blocks.send(lo, hi)
        sums_ffn.append(sums)
    gffn, act, slope = held

    low = [("dp", b) for b in bits_of(dp)]
    high = [("seq", b) for b in bits_of(seq)[1:]]
    turned = low[1:2] + low[:1] + high + low[2:]

    n = dp * seq
    came_out = [v for _, v in out_blocks.chunks]
    down = Sum(down_grad(me, dp, seq, low + high, act, gffn, far(*came_out[:1])), dp, seq, low + high)
    down.begin()
    held, sums_attn, sums_up, deps = (), [], [], []
    for i, (start, stop) in enumerate(halves):
        *held, sums1, sums2, tick = ffn_back(
            start, stop - start, gffn, slope, w_up, w_down, w_out, n1, s1, vec, att, il, heads, hs,
            deps, held,
        )
        sums_attn.append(sums1)
        sums_up.append(sums2)
        deps = []
        if i == 0:
            deps, _ = fold(both, [down], [tick] + far(*came_out[1:]))
            deps = far(*deps)
    gpre, gbr, do, de = held
    d_up, tick = up_out_grad(me, dp, seq, low + high, first, gpre, att, gbr, deps)
    up = Sum(d_up, dp, seq, low + high)
    deps, _, (send,) = fold(both, [down], [tick], 1, [up.send])
    deps = far(*deps)
    up.begin(send)
    g, in_blocks = None, Blocks("seq", seq)
    for start, stop in halves:
        lo = hi = None
        for row in range(start, stop):
            if row == 1:
                sends, _ = fold(both, [down, up] if down.order else [up], [tick], 2)
                sends = far(*sends)
                deps = sends[:-1]
            elif row == 2:
                deps = [sends[-1], up.came[0]]
            elif row == 3:
                deps, _ = fold(both, [down, up] if down.order else [up], [tick])
                deps = far(*deps)
            elif row:
                deps = []
            g, lo, hi, tick = attend_back(
                row, 1, stop - start, row - start, qkv, p, do, de, gbr, wt, heads, hs, scale, group,
                deps, (g, lo, hi),
            )
        in_blocks.send(lo, hi)
    g = g.reshape(R, 3 * D, L)
    deps, _ = fold(both, [up], [tick] + far(in_blocks.chunks[0][1]))
    deps = far(*deps)

    sums = sums_attn + sums_up + sums_ffn
    kinds = [sums_attn, sums_up, sums_ffn]
    firsts = [sum(len(v) for v in kinds[:i]) for i in range(3)]
    span = lambda kind, row, *cols: (range(firsts[kind], firsts[kind] + len(kinds[kind])), row, cols)
    spans = [
        span(0, 0, (0, D)), span(0, 1, (0, D)), span(0, 2, (0, D)), span(1, 0, (0, FF)),
        span(2, 0, (0, D)), span(2, 1, (0, D)), span(2, 2, (0, D)),
    ]
    per = [2 * D // n] + [sum(hi - lo for lo, hi in cols) // n for _, _, cols in spans]
    orders = [low + high, turned, high[:1] + low[2:] + low[:2] + high[1:]]
    d_qkv, tick = qkv_grad(me, dp, seq, orders, x, g, sums, spans, deps)
    lasts = [Sum(halves_, dp, seq, order) for halves_, order in zip(d_qkv, orders)]
    while len(up.order) > 1:
        _, tick = fold(both, [up], [tick])
    _, tick, sends = fold(
        both, [up], [tick] + far(*[v for _, v in in_blocks.chunks[1:]]), 1, [s.send for s in lasts]
    )
    for s, send in zip(lasts, sends):
        s.begin(send)
    while down.order:
        _, tick = fold(both, [down], [tick])
    out_blocks.turn(me, tick)
    in_blocks.turn(me, tick)
    stage, done = 0, []
    while lasts[0].order:
        _, tick = fold(both, ([up] if up.order else []) + lasts, [tick] + done)
        done = []
        if stage == 0:
            out_hidden = out_blocks.result(me, tick)
            done = far(out_hidden)
        if stage == 1:
            grad_in = in_blocks.result(me, tick)
            done = far(grad_in)
        if stage == 2:
            r_down, r_up, r_out = down.result(tick), up.result(tick, 0, FF), up.result(tick, FF)
            done = far(r_down, r_up, r_out)
        stage += 1
    r_qkv = [s.result() for s in lasts]
    vec = r_qkv[-1][: spots(per)[-1] // 128 + 1, D:].reshape(-1)
    cuts = [vec[at : at + width] for at, width in zip(spots(per), per)]
    b_qv, b_out, g_attn, s_attn, b_up, b_down, g_ffn, s_ffn = cuts
    return (
        out_hidden, grad_in, jnp.concatenate(r_qkv[:-1] + [r_qkv[-1][:, :D]], 1), b_qv,
        r_out, b_out, g_attn, s_attn, r_up, b_up, r_down, b_down, g_ffn, s_ffn,
    )


def solution(mesh):
    tok = P("dp", "seq", None)
    both = ("dp", "seq")
    return jax.shard_map(
        functools.partial(shards, mesh.shape["dp"], mesh.shape["seq"]),
        mesh=mesh,
        in_specs=(tok, P("dp", None), P("dp", None, None)) + (P(),) * 12 + (tok,),
        out_specs=(
            tok, tok, P(both, None), P(both), P(both, None), P(both), P(both), P(both),
            P(both, None), P(both), P(both, None), P(both), P(both), P(both),
        ),
        check_vma=False,
    )
```

```python
import functools
import math

import jax
import jax.numpy as jnp
from jax import lax
from jax.experimental import pallas as pl
from jax.experimental.pallas import tpu as pltpu
from jax.sharding import PartitionSpec as P

CL = 128
DOCS = 3
CODES = 16
NORM_EPS = 1e-05
BIG = 2.0**50
NO_SHIFT = 40.0
F32 = jnp.float32
BF16 = jnp.bfloat16
NN = (((1,), (0,)), ((), ()))
NT = (((1,), (1,)), ((), ()))
TN = (((0,), (0,)), ((), ()))
MIB = 2**20
FFN_CUT = 2
BACK_CUT = 1
VMEM = 32 * MIB
ATTEND_VMEM = 28 * MIB
FFN_VMEM = 30 * MIB
BACK_VMEM = 26 * MIB
ATTEND_BACK_VMEM = 24 * MIB
WHOLE = pl.BlockSpec(memory_space=pltpu.VMEM)
TICK = jax.ShapeDtypeStruct((1, 1), jnp.float32)
TICK1 = pl.BlockSpec((1, 1), lambda i: (0, 0))
TICK2 = pl.BlockSpec((1, 1), lambda i, g: (0, 0))
TICK3 = pl.BlockSpec((1, 1), lambda i, g, me: (0, 0))
ANY = pl.BlockSpec(memory_space=pl.ANY)


def mm(a, b, dims=NN):
    return lax.dot_general(a, b, dims, preferred_element_type=F32)


def far(*arrays):
    return [pltpu.with_memory_space_constraint(v, pltpu.HBM) for v in arrays]


def whole(shape):
    return pl.BlockSpec(shape, lambda i: (0,) * len(shape), pipeline_mode=pl.Buffered(1))


def lead(shape):
    return pl.BlockSpec((1,) + shape, lambda i: (i,) + (0,) * len(shape))


def rows_of(tile, width):
    return pl.BlockSpec((tile, width), lambda i: (i, 0))


def shape_of(shape, dtype):
    return pltpu.HBM(shape, dtype)


def params(limit=VMEM):
    return pltpu.CompilerParams(vmem_limit_bytes=limit)


def cost(flops, nbytes):
    return pl.CostEstimate(flops=int(flops), bytes_accessed=int(nbytes), transcendentals=0)


def part_specs(parts, R, at, block_len, D):
    own = pl.BlockSpec((1, block_len, D), lambda i, g, me: (me[0] * R + at + i, 0, 0))
    specs = [own]
    for bit, (part, base) in enumerate(parts[1:]):
        shape = (1, 1) + part.shape[2:]
        place = lambda bit, base, i, g, me: (me[0] >> (bit + 1), at + i - base, 0, 0)
        specs.append(pl.BlockSpec(shape, functools.partial(place, bit, base)))
    return specs


def arrays_of(parts):
    return [parts[0]] + [part for part, _ in parts[1:]]


def merge(refs):
    return jnp.concatenate([refs[0][0]] + [ref[0, 0] for ref in refs[1:]], 0)


def attend_kernel(me_ref, *refs, nparts, heads, hs, group, scale, nio, row, ncarry):
    carried, refs = refs[:ncarry], refs[ncarry:]
    parts, (code_ref, wt_ref, bt_ref, wo_ref, vec_ref) = refs[:nparts], refs[nparts : nparts + 5]
    outs = refs[nparts + 5 + nio :]
    x_far, qkv_far, p_ref, il_ref, att_ref, first_ref, n_ref, s_ref, tick_ref = outs[:9]
    kept, (x_ref, qkv_ref, sems) = outs[9:-3], outs[-3:]
    tick_ref[...] = jnp.zeros_like(tick_ref)
    D = heads * hs
    L = x_ref.shape[1]
    step = pl.program_id(1)
    copies = [
        pltpu.make_async_copy(x_ref, x_far.at[pl.ds(row, 1)], sems.at[0]),
        pltpu.make_async_copy(qkv_ref, qkv_far.at[pl.ds(row, 1)], sems.at[1]),
    ] + [pltpu.make_async_copy(a, b, sems.at[2 + i]) for i, (a, b) in enumerate(zip(carried, kept))]

    @pl.when(step == 0)
    def _():
        x_ref[0] = merge(parts)
        f = mm(wt_ref[...], x_ref[0], NT) + bt_ref[:, 0:1]
        qkv_ref[0, :D, :] = (f[:D].astype(BF16).astype(F32) * scale).astype(BF16)
        qkv_ref[0, D:, :] = f[D:].astype(BF16)
        for copy in copies:
            copy.start()

    it = lax.broadcasted_iota(jnp.int32, (CODES, L), 0)

    def head(i):
        at = pl.multiple_of((step * group + i) * hs, hs)
        return [qkv_ref[0, pl.ds(j * D + at, hs), :] for j in range(3)]

    bound = jnp.zeros((1, 1), F32)
    for i in range(group):
        q, k, _ = head(i)
        norms = [
            jnp.max(jnp.sum(v.astype(F32) * v.astype(F32), axis=0, keepdims=True), axis=1, keepdims=True)
            for v in (q, k)
        ]
        bound = jnp.maximum(bound, norms[0] * norms[1])
    small = bound[0, 0] <= NO_SHIFT * NO_SHIFT

    def attend_group(shifted):
        for i in range(group):
            at = pl.multiple_of((step * group + i) * hs, hs)
            q, k, v = head(i)
            same = it == code_ref[0, 0, i : i + 1, :]
            qa = jnp.concatenate([q, jnp.where(same, BIG, 0.0).astype(BF16)], 0)
            ka = jnp.concatenate([k, jnp.where(same, 0.0, -BIG).astype(BF16)], 0)
            s = mm(ka, qa, TN)
            if shifted:
                s = s - jnp.max(s, axis=0, keepdims=True)
            p = jnp.exp(s).astype(BF16)
            p_ref[0, i] = p
            o = mm(jnp.concatenate([v, jnp.ones((16, L), BF16)], 0), p)
            il = 1.0 / o[hs : hs + 1]
            il_ref[0, 0, i : i + 1, :] = il
            att_ref[0, pl.ds(at, hs), :] = (o[:hs] * il).astype(BF16)

    @pl.when(small)
    def _():
        attend_group(False)

    @pl.when(jnp.logical_not(small))
    def _():
        attend_group(True)

    @pl.when(step == heads // group - 1)
    def _():
        v1 = x_ref[0].astype(F32) + mm(att_ref[0], wo_ref[...], TN) + vec_ref[0:1, :]
        c = v1 - jnp.mean(v1, -1, keepdims=True)
        s1 = lax.rsqrt(jnp.mean(c * c, -1, keepdims=True) + NORM_EPS)
        n1 = c * s1
        first_ref[0] = (n1 * vec_ref[1:2, :] + vec_ref[2:3, :]).astype(BF16)
        n_ref[0] = n1.astype(BF16)
        s_ref[0] = jnp.broadcast_to(s1, (L, 128))
        for copy in copies:
            copy.wait()


def attend(me, parts, at, R, code, wt, bt, wo, vec, heads, hs, scale, group, deps, held, carry=()):
    r = 1
    D = wo.shape[0]
    L = code.shape[-1]
    here = lambda shape: pl.BlockSpec((1,) + shape, lambda i, g, me: (at + i,) + (0,) * len(shape))
    grouped = lambda shape: pl.BlockSpec((1, 1) + shape, lambda i, g, me: (at + i, g, 0, 0))
    shapes = [
        shape_of((R, L, D), BF16),
        shape_of((R, 3 * D, L), BF16), shape_of((R, heads, L, L), BF16),
        shape_of((R, heads // group, group, L), F32), shape_of((R, D, L), BF16),
        shape_of((R, L, D), BF16), shape_of((R, L, D), BF16), shape_of((R, L, 128), F32),
        TICK,
    ]
    nio = len(held) + len(deps)
    np_ = len(parts)
    return pl.pallas_call(
        functools.partial(
            attend_kernel, nparts=np_, heads=heads, hs=hs, group=group, scale=scale, nio=nio,
            row=at, ncarry=len(carry),
        ),
        grid_spec=pltpu.PrefetchScalarGridSpec(
            num_scalar_prefetch=1,
            grid=(r, heads // group),
            in_specs=[ANY] * len(carry) + part_specs(parts, R, at, parts[0].shape[1], D) + [
                grouped((group, L)), WHOLE, WHOLE, WHOLE, WHOLE,
            ] + [ANY] * nio,
            out_specs=[
                ANY, ANY, pl.BlockSpec((1, group, L, L), lambda i, g, me: (at + i, g, 0, 0)),
                grouped((group, L)), here((D, L)), here((L, D)), here((L, D)), here((L, 128)),
                TICK3,
            ] + [WHOLE] * len(carry),
            scratch_shapes=[
                pltpu.VMEM((1, L, D), BF16), pltpu.VMEM((1, 3 * D, L), BF16),
                pltpu.SemaphoreType.DMA((2 + len(carry),)),
            ],
        ),
        out_shape=shapes + [pltpu.VMEM(v.shape, v.dtype) for v in carry],
        input_output_aliases={1 + len(carry) + np_ + 5 + len(deps) + i: i for i in range(len(held))},
        compiler_params=params(ATTEND_VMEM),
        cost_estimate=cost(r * (8 * L * D * D + 4 * 4 * heads * L * L * hs), r * 2 * heads * L * L),
        name="attend",
    )(me, *carry, *arrays_of(parts), code, wt, bt, wo, vec, *deps, *held)


def prepare_kernel(me_ref, w_ref, b_ref, perm_ref, seg_ref, *rest, seq):
    wt_ref, bt_ref, code_ref = rest[-3:]
    wt_ref[...] = w_ref[...].T
    bt_ref[...] = b_ref[...].T
    heads, _, L = perm_ref.shape
    R, _, group = code_ref.shape[:3]
    me = me_ref[0]
    block = L // seq
    high = lax.broadcasted_iota(jnp.int32, (8, L), 0)
    low = lax.broadcasted_iota(jnp.int32, (128, L), 0)
    member = (lax.broadcasted_iota(jnp.int32, (8, L), 1) // CL).astype(F32)
    for r in range(R):
        seg = seg_ref[pl.ds(me * R + r, 1), :]
        for bit in bits_of(seq):
            blocks = [seg[:, i * block : (i + 1) * block] for i in range(seq)]
            turned = jnp.concatenate([blocks[i ^ (1 << bit)] for i in range(seq)], 1)
            seg = jnp.where(((me >> bit) & 1) == 1, turned, seg)
        for h in range(heads):
            place = perm_ref[h, pl.ds(me * R + r, 1), :] ^ (me * block)
            a = jnp.where((place >> 7) == high, member, 0.0).astype(BF16)
            b = ((place & 127) == low).astype(BF16)
            table = mm(a, b, NT)
            row = jnp.concatenate([table[i : i + 1, :] for i in range(L // 128)], 1)
            code_ref[r, h // group, h % group : h % group + 1, :] = row.astype(jnp.int32) * DOCS + seg


def prepare(me, seq, w, b, perm, segs, group, deps):
    heads, rows, L = perm.shape
    R = rows // seq
    D, D3 = w.shape
    full = lambda shape: pl.BlockSpec(shape, lambda i, me: (0,) * len(shape))
    codes = (R, heads // group, group, L)
    return pl.pallas_call(
        functools.partial(prepare_kernel, seq=seq),
        grid_spec=pltpu.PrefetchScalarGridSpec(
            num_scalar_prefetch=1,
            grid=(1,),
            in_specs=[
                full((D, D3)), full((8, D3)), full(perm.shape),
                full(segs.shape),
            ] + [ANY] * len(deps),
            out_specs=[full((D3, D)), full((D3, 8)), full(codes)],
        ),
        out_shape=[
            jax.ShapeDtypeStruct((D3, D), BF16), jax.ShapeDtypeStruct((D3, 8), F32),
            jax.ShapeDtypeStruct(codes, jnp.int32),
        ],
        compiler_params=params(32 * MIB),
        cost_estimate=cost(4e9, 8e6),
        name="prepare",
    )(me, w, b, perm, segs, *deps)


def ffn_kernel(me_ref, *refs, nparts, nio):
    parts, (first_ref, wu_ref, bu_ref, wd_ref, vec_ref) = refs[:nparts], refs[nparts : nparts + 5]
    lo_ref, hi_ref, gffn_ref, act_ref, slope_ref, sums_ref, tick_ref = refs[nparts + 5 + nio :]
    tick_ref[...] = jnp.zeros_like(tick_ref)
    @pl.when(pl.program_id(0) == 0)
    def _():
        sums_ref[...] = jnp.zeros_like(sums_ref)

    go_all = merge(parts)
    tile = first_ref.shape[0]
    sub = tile // FFN_CUT
    for cut in range(FFN_CUT):
        here = slice(cut * sub, (cut + 1) * sub)
        first = first_ref[here, :]
        u = mm(first, wu_ref[...]) + bu_ref[...]
        half = 0.5 * (1.0 + lax.erf(u * 0.7071067811865476))
        act = (u * half).astype(BF16)
        act_ref[here, :] = act
        slope_ref[here, :] = (half + u * jnp.exp(-0.5 * u * u) * 0.3989422804014327).astype(BF16)
        y = first.astype(F32) + mm(act, wd_ref[...]) + vec_ref[3:4, :]
        c = y - jnp.mean(y, -1, keepdims=True)
        s2 = lax.rsqrt(jnp.mean(c * c, -1, keepdims=True) + NORM_EPS)
        n2 = c * s2
        out = (n2 * vec_ref[4:5, :] + vec_ref[5:6, :]).astype(BF16)
        if cut < FFN_CUT // 2:
            lo_ref[0, here, :] = out
        elif FFN_CUT > 1:
            hi_ref[0, cut * sub - tile // 2 : (cut + 1) * sub - tile // 2, :] = out
        else:
            lo_ref[0] = out[: tile // 2]
            hi_ref[0] = out[tile // 2 :]
        go = go_all[here].astype(F32)
        e = go * vec_ref[4:5, :]
        g2 = s2 * (e - jnp.mean(e, -1, keepdims=True) - n2 * jnp.mean(e * n2, -1, keepdims=True))
        gl = g2.astype(BF16)
        gffn_ref[here, :] = gl
        sums_ref[0:1, :] += jnp.sum(gl.astype(F32), 0, keepdims=True)
        sums_ref[1:2, :] += jnp.sum(go * n2, 0, keepdims=True)
        sums_ref[2:3, :] += jnp.sum(go, 0, keepdims=True)


def ffn(me, first, parts, at, r, R, wu, bu, wd, vec, deps, held):
    T, D = first.shape
    L = T // R
    FF = wu.shape[1]
    here = lambda width: pl.BlockSpec((L, width), lambda i, g, me: (at + i, 0))
    nio = len(held) + len(deps)
    np_ = len(parts)
    half = pl.BlockSpec((1, L // 2, D), lambda i, g, me: (i, 0, 0))
    return pl.pallas_call(
        functools.partial(ffn_kernel, nparts=np_, nio=nio),
        grid_spec=pltpu.PrefetchScalarGridSpec(
            num_scalar_prefetch=1,
            grid=(r, 1),
            in_specs=part_specs(parts, R, at, parts[0].shape[1], D) + [
                here(D), WHOLE, WHOLE, WHOLE, WHOLE,
            ] + [ANY] * nio,
            out_specs=[
                half, half, here(D), here(FF), here(FF),
                pl.BlockSpec((8, D), lambda i, g, me: (0, 0)), TICK3,
            ],
        ),
        out_shape=[
            shape_of((r, L // 2, D), BF16), shape_of((r, L // 2, D), BF16), shape_of((T, D), BF16),
            shape_of((T, FF), BF16), shape_of((T, FF), BF16), shape_of((8, D), F32),
            TICK,
        ],
        input_output_aliases={1 + np_ + 5 + len(deps) + i: 2 + i for i in range(len(held))},
        compiler_params=params(FFN_VMEM),
        cost_estimate=cost(4 * r * L * D * FF * 1.3, 4 * r * L * FF + 4 * D * FF),
        name="ffn",
    )(me, *arrays_of(parts), *far(first), wu, bu, wd, vec, *deps, *held)


def by_core(total, place):
    rows, width = total.shape
    bits = len(place) + 1
    cube = total.reshape((2,) * bits + (rows >> bits, width))
    cube = cube.transpose((bits - 1,) + tuple(place) + (bits, bits + 1))
    return cube[0].reshape(rows // 2, width), cube[1].reshape(rows // 2, width)


def put_halves(me_ref, total, place, send_ref, keep_ref):
    even, odd = by_core(total, place)
    mine = me_ref[0] % 2 == 0
    send_ref[...] = jnp.where(mine, odd, even).astype(BF16)
    keep_ref[...] = jnp.where(mine, even, odd).astype(BF16)


def halves_of(me, total, place):
    even, odd = by_core(total, place)
    mine = me[0] % 2 == 0
    return jnp.where(mine, odd, even), jnp.where(mine, even, odd)


def places(dp, seq, order):
    names = [("dp", b) for b in reversed(bits_of(dp))] + [("seq", b) for b in reversed(bits_of(seq))]
    return [names.index(item) for item in order]


def splits(rows, n):
    return (rows // n) % 8 == 0


def down_grad_kernel(me_ref, act_ref, g_ref, *rest, place, ndep):
    outs = rest[ndep:]
    total = mm(act_ref[...], g_ref[...], TN)
    if len(outs) == 2:
        put_halves(me_ref, total, place, *outs)
    else:
        outs[0][...] = total.astype(BF16)


def down_grad(me, dp, seq, order, act, g, deps):
    T, FF = act.shape
    D = g.shape[1]
    n = dp * seq
    inside = splits(FF, n) and FF // dp % 128 == 0
    steps = dp if inside else 8
    tile = FF // steps
    place = places(dp, seq, order)
    inner = [p - len(bits_of(dp)) for p in place if p >= len(bits_of(dp))]
    turns = [bit for name, bit in order if name == "dp"]

    def at(i):
        where = 0
        for bit in turns:
            where = 2 * where + ((i >> bit) & 1)
        return (where, 0)

    res = pl.pallas_call(
        functools.partial(down_grad_kernel, place=inner, ndep=len(deps)),
        grid=(steps,),
        in_specs=[
            pl.BlockSpec(memory_space=pltpu.SMEM), pl.BlockSpec((T, tile), lambda i: (0, i)), whole((T, D)),
        ] + [ANY] * len(deps),
        out_specs=[pl.BlockSpec((tile // 2, D), at)] * 2 if inside else [rows_of(tile, D)],
        out_shape=[shape_of((FF // 2, D), BF16)] * 2 if inside else [shape_of((FF, D), BF16)],
        compiler_params=params(18 * MIB),
        cost_estimate=cost(2 * T * D * FF * 1.3, 2 * T * FF + 2 * D * FF),
        name="down_grad",
    )(me, *far(act, g), *deps)
    return res if inside else halves_of(me, res[0], place)


def ffn_back_kernel(
    g_ref, slope_ref, wu_ref, wd_ref, wo_ref, n_ref, s_ref, vec_ref, att_ref, il_ref, *rest,
    heads, hs,
):
    gpre_ref, gbr_ref, do_ref, de_ref, sums_ref, bsum_ref, tick_ref = rest[-7:]
    tick_ref[...] = jnp.zeros_like(tick_ref)
    @pl.when((pl.program_id(0) == 0) & (pl.program_id(1) == 0))
    def _():
        sums_ref[...] = jnp.zeros_like(sums_ref)
        bsum_ref[...] = jnp.zeros_like(bsum_ref)

    sub = g_ref.shape[0] // BACK_CUT
    for cut in range(BACK_CUT):
        here = slice(cut * sub, (cut + 1) * sub)
        g = g_ref[here, :]
        gp = (mm(g, wd_ref[...], NT) * slope_ref[here, :].astype(F32)).astype(BF16)
        gpre_ref[here, :] = gp
        gfirst = mm(gp, wu_ref[...], NT) + g.astype(F32)
        n1 = n_ref[0, here, :].astype(F32)
        e = gfirst * vec_ref[1:2, :]
        g1 = s_ref[0, here, 0:1] * (
            e - jnp.mean(e, -1, keepdims=True) - n1 * jnp.mean(e * n1, -1, keepdims=True)
        )
        gl = g1.astype(BF16)
        gbr_ref[0, here, :] = gl
        da = mm(wo_ref[...], gl, NT)
        group = il_ref.shape[2]
        for h in range(heads):
            i, j = h // group, h % group
            il = il_ref[0, i, j : j + 1, here]
            piece = da[h * hs : (h + 1) * hs, :] * il
            do_ref[0, h * hs : (h + 1) * hs, here] = piece.astype(BF16)
            att = att_ref[0, h * hs : (h + 1) * hs, here].astype(F32)
            de_ref[0, i, j : j + 1, here] = jnp.sum(piece * att, axis=0, keepdims=True)
        sums_ref[0:1, :] += jnp.sum(gl.astype(F32), 0, keepdims=True)
        sums_ref[1:2, :] += jnp.sum(gfirst * n1, 0, keepdims=True)
        sums_ref[2:3, :] += jnp.sum(gfirst, 0, keepdims=True)
        bsum_ref[0:1, :] += jnp.sum(gp.astype(F32), 0, keepdims=True)


def ffn_back(at, r, g, slope, wu, wd, wo, n1, s1, vec, att, il, heads, hs, deps, held):
    T, D = g.shape
    FF = wu.shape[1]
    R, L = n1.shape[:2]
    half = L // 2
    flat = lambda width: pl.BlockSpec((half, width), lambda i, g: (2 * (at + i) + g, 0))
    fixed = lambda shape: pl.BlockSpec(
        shape, lambda i, g: (0,) * len(shape), pipeline_mode=pl.Buffered(1)
    )
    tokens = lambda width: pl.BlockSpec((1, half, width), lambda i, g: (at + i, g, 0))
    columns = lambda *lead: pl.BlockSpec(
        (1,) + lead + (half,), lambda i, g: (at + i,) + (0,) * len(lead) + (g,)
    )
    extra = list(deps) + list(held)
    return pl.pallas_call(
        functools.partial(ffn_back_kernel, heads=heads, hs=hs),
        grid=(r, 2),
        in_specs=[
            flat(D), flat(FF), WHOLE, WHOLE, fixed((D, D)), tokens(D), tokens(128), fixed((8, D)),
            columns(D), columns(*il.shape[1:3]),
        ] + [ANY] * len(extra),
        out_specs=[
            flat(FF), tokens(D), columns(D), columns(*il.shape[1:3]),
            pl.BlockSpec((8, D), lambda i, g: (0, 0)), pl.BlockSpec((8, FF), lambda i, g: (0, 0)),
            TICK2,
        ],
        out_shape=[
            shape_of((T, FF), BF16), shape_of((R, L, D), BF16), shape_of((R, D, L), BF16),
            shape_of(il.shape, F32), shape_of((8, D), F32), shape_of((8, FF), F32),
            TICK,
        ],
        input_output_aliases={10 + len(deps) + i: i for i in range(len(held))},
        compiler_params=params(BACK_VMEM),
        cost_estimate=cost(4 * r * L * D * FF * 1.5, 4 * r * L * FF + 4 * D * FF),
        name="ffn_back",
    )(*far(g, slope), wu, wd, *far(wo, n1, s1, vec, att, il), *extra)


def up_out_grad_kernel(me_ref, x_ref, g_ref, att_far, gbr_far, *rest, place, ndep):
    outs, tick_ref, att_ref, gbr_ref, sems = rest[ndep:-4], rest[-4], rest[-3], rest[-2], rest[-1]
    tick_ref[...] = jnp.zeros_like(tick_ref)
    last = pl.num_programs(0) - 1

    def put(total):
        if len(outs) == 2:
            put_halves(me_ref, total, place, *outs)
        else:
            outs[0][...] = total.astype(BF16)

    copies = [
        pltpu.make_async_copy(att_far, att_ref, sems.at[0]),
        pltpu.make_async_copy(gbr_far, gbr_ref, sems.at[1]),
    ]

    @pl.when(pl.program_id(0) == 0)
    def _():
        for copy in copies:
            copy.start()

    @pl.when(pl.program_id(0) < last)
    def _():
        put(mm(x_ref[...], g_ref[...], TN))

    @pl.when(pl.program_id(0) == last)
    def _():
        for copy in copies:
            copy.wait()
        total = mm(att_ref[0], gbr_ref[0])
        for r in range(1, att_ref.shape[0]):
            total = total + mm(att_ref[r], gbr_ref[r])
        put(total)


def up_out_grad(me, dp, seq, order, x, g, att, gbr, deps):
    T, D = x.shape
    FF = g.shape[1]
    R, _, L = att.shape
    place = places(dp, seq, order)
    inside = splits(D, dp * seq)
    rows, count = (D // 2, 2) if inside else (D, 1)
    steps = FF // D
    *res, tick = pl.pallas_call(
        functools.partial(up_out_grad_kernel, place=place, ndep=len(deps)),
        grid=(steps + 1,),
        in_specs=[
            pl.BlockSpec(memory_space=pltpu.SMEM), whole((T, D)),
            pl.BlockSpec((T, D), lambda i: (0, jnp.minimum(i, steps - 1))), ANY, ANY,
        ] + [ANY] * len(deps),
        out_specs=[pl.BlockSpec((rows, D), lambda i: (0, i))] * count + [TICK1],
        out_shape=[jax.ShapeDtypeStruct((rows, FF + D), BF16)] * count + [TICK],
        scratch_shapes=[
            pltpu.VMEM((R, D, L), BF16), pltpu.VMEM((R, L, D), BF16), pltpu.SemaphoreType.DMA((2,)),
        ],
        compiler_params=params(),
        cost_estimate=cost(1, 1),
        name="up_out_grad",
    )(me, *far(x, g, att, gbr), *deps)
    return (res if inside else halves_of(me, res[0], place)), tick


def attend_back_kernel(
    qkv_ref, p_ref, do_ref, de_ref, gone_ref, wt_ref, *rest, heads, hs, scale, group
):
    g_out, lo_ref, hi_ref, tick_ref, g_ref = rest[-5:]
    tick_ref[...] = jnp.zeros_like(tick_ref)
    step = pl.program_id(1)
    for i in range(group):
        here = slice(i * hs, (i + 1) * hs)
        q, k, v = [qkv_ref[0, j, here, :] for j in range(3)]
        do = do_ref[0, here, :]
        p = p_ref[0, i]
        dp = mm(v, do, TN)
        ds = (p.astype(F32) * (dp - de_ref[0, 0, i : i + 1, :])).astype(BF16)
        grads = [mm(k, ds) * scale, mm(q, ds, NT), mm(do, p, NT)]
        for j in range(3):
            part = grads[j].astype(BF16)
            g_out[0, j, here, :] = part
            g_ref[j, step, here, :] = part

    @pl.when(step == heads // group - 1)
    def _():
        g = g_ref[...].reshape(3 * heads * hs, g_ref.shape[-1])
        gin = (mm(g, wt_ref[...], TN) + gone_ref[0].astype(F32)).astype(BF16)
        half_len = gin.shape[0] // 2
        lo_ref[0] = gin[:half_len]
        hi_ref[0] = gin[half_len:]


def attend_back(at, r, of, place, qkv, p, do, de, gone, wt, heads, hs, scale, group, deps, held):
    R, D3, L = qkv.shape
    D = D3 // 3
    here = lambda shape: pl.BlockSpec((1,) + shape, lambda i, g: (at + i,) + (0,) * len(shape))
    extra = list(deps) + [v for v in held if v is not None]
    aliases = {}
    for i, v in enumerate(held):
        if v is not None:
            aliases[6 + len(deps) + len(aliases)] = i
    half = pl.BlockSpec((1, L // 2, D), lambda i, g: (place + i, 0, 0))
    heads_of = pl.BlockSpec((1, 3, group * hs, L), lambda i, g: (at + i, 0, g, 0))
    g, *rest = pl.pallas_call(
        functools.partial(attend_back_kernel, heads=heads, hs=hs, scale=scale, group=group),
        grid=(r, heads // group),
        in_specs=[
            heads_of, pl.BlockSpec((1, group, L, L), lambda i, g: (at + i, g, 0, 0)),
            pl.BlockSpec((1, group * hs, L), lambda i, g: (at + i, g, 0)),
            pl.BlockSpec((1, 1, group, L), lambda i, g: (at + i, g, 0, 0)),
            here((L, D)), WHOLE,
        ] + [ANY] * len(extra),
        out_specs=[heads_of, half, half, TICK2],
        out_shape=[
            shape_of((R, 3, D, L), BF16), shape_of((of, L // 2, D), BF16),
            shape_of((of, L // 2, D), BF16), TICK,
        ],
        scratch_shapes=[pltpu.VMEM((3, heads // group, group * hs, L), BF16)],
        input_output_aliases=aliases,
        compiler_params=params(ATTEND_BACK_VMEM),
        cost_estimate=cost(r * (6 * L * D * D + 4 * 8 * heads * L * L * hs), r * 2 * heads * L * L),
        name="attend_back",
    )(*far(qkv.reshape(R, 3, D, L), p, do, de, gone), wt, *extra)
    return [g, *rest]


def spots(widths):
    out, at = [], 0
    for width in widths:
        if at % 128 + width > 128:
            at = 128 * -(-at // 128)
        out.append(at)
        at += width
    return out


def pack(sums, n, windows):
    widths = [terms[0].shape[1] // n for terms in sums]
    pieces = [jnp.zeros((n, 128), F32) for _ in range(windows)]
    for terms, width, at in zip(sums, widths, spots(widths)):
        v = functools.reduce(jnp.add, terms)
        W = v.shape[1]
        owner = lax.broadcasted_iota(jnp.int32, (n, W), 0)
        place = lax.broadcasted_iota(jnp.int32, (n, W), 1)
        a = jnp.where((place >= owner * width) & (place < (owner + 1) * width), v, 0.0).astype(BF16)
        index = lax.broadcasted_iota(jnp.int32, (W, 128), 0)
        start = ((index.astype(F32) + 0.5) * (1.0 / width)).astype(jnp.int32) * width
        b = (lax.broadcasted_iota(jnp.int32, (W, 128), 1) == index - start + at % 128).astype(BF16)
        pieces[at // 128] += mm(a, b)
    return pieces


def qkv_grad_kernel(me_ref, x_ref, g_ref, *rest, spans, nsum, ndep, n, count, place, windows):
    sums_refs, outs = rest[:nsum], rest[nsum + ndep : -3]
    tick_ref, first_ref, xt_ref = rest[-3:]
    tick_ref[...] = jnp.zeros_like(tick_ref)
    step, steps = pl.program_id(0), len(place)
    D = x_ref.shape[2]

    def put(total, which):
        refs = outs[which * count : (which + 1) * count]
        if count == 2:
            put_halves(me_ref, total, place[which], *refs)
        else:
            refs[0][...] = total.astype(BF16)

    @pl.when(step == 0)
    def _():
        for r in range(x_ref.shape[0]):
            xt_ref[r, :D, :] = x_ref[r].T
            xt_ref[r, D:, :] = jnp.ones((xt_ref.shape[1] - D, x_ref.shape[1]), BF16)

    both = mm(xt_ref[0], g_ref[0], NT)
    for r in range(1, x_ref.shape[0]):
        both = both + mm(xt_ref[r], g_ref[r], NT)
    total, over = both[:D], both[D : D + 1]

    @pl.when(step == 0)
    def _():
        first_ref[...] = over

    for which in range(steps - 1):
        @pl.when(step == which)
        def _(which=which):
            put(total, which)

    @pl.when(step == steps - 1)
    def _():
        row = lax.broadcasted_iota(jnp.int32, (n, D // n, 128), 1)
        packed = jnp.zeros((n, D // n, 128), F32)
        sums = [[jnp.concatenate([first_ref[...], over], 1)]] + [
            [jnp.concatenate([sums_refs[i][line : line + 1, lo:hi] for lo, hi in cols], 1) for i in terms]
            for terms, line, cols in spans
        ]
        for i, piece in enumerate(pack(sums, n, windows)):
            packed = jnp.where(row == i, piece[:, None, :], packed)
        put(jnp.concatenate([total, packed.reshape(D, 128)], 1), steps - 1)


def qkv_grad(me, dp, seq, orders, x, g, sums, spans, deps):
    R, L, D = x.shape
    n = dp * seq
    place = [places(dp, seq, order) for order in orders]
    real = len(place)
    inside = splits(D, n)
    rows, count = (D // 2, 2) if inside else (D, 1)
    widths = [D] * (real - 1) + [D + 128]
    parts = [2 * D // n] + [sum(hi - lo for lo, hi in cols) // n for _, _, cols in spans]
    windows = spots(parts)[-1] // 128 + 1
    *res, tick = pl.pallas_call(
        functools.partial(
            qkv_grad_kernel, spans=spans, nsum=len(sums), ndep=len(deps), n=n, count=count, place=place,
            windows=windows,
        ),
        grid=(real,),
        in_specs=[
            pl.BlockSpec(memory_space=pltpu.SMEM), whole((R, L, D)),
            pl.BlockSpec((R, D, L), lambda i: (0, i, 0)),
        ] + [whole(v.shape) for v in sums] + [ANY] * len(deps),
        out_specs=[
            pl.BlockSpec((rows, width), lambda i: (0, 0)) for width in widths for _ in range(count)
        ] + [TICK1],
        out_shape=[
            jax.ShapeDtypeStruct((rows, width), BF16) for width in widths for _ in range(count)
        ] + [TICK],
        scratch_shapes=[pltpu.VMEM((1, D), F32), pltpu.VMEM((R, D + 16, L), BF16)],
        compiler_params=params(),
        cost_estimate=cost(6 * R * L * D * D * 1.3, 8 * R * L * D),
        name="qkv_grad",
    )(me, *far(x, g), *sums, *deps)
    pieces = [res[i * count : (i + 1) * count] for i in range(real)]
    return [piece if inside else halves_of(me, piece[0], at) for piece, at in zip(pieces, place)], tick


def bits_of(size):
    return [b for b in range(size.bit_length() - 1)]


def flip(x, axis, size, bit):
    return lax.ppermute(x, axis, [(i, i ^ (1 << bit)) for i in range(size)])


def my_bit(axis, bit):
    return (lax.axis_index(axis) >> bit) & 1


def pick(x, index, axis):
    return lax.dynamic_index_in_dim(x, index, axis, keepdims=False)


def late(x, tick):
    return x if tick is None else x + tick.reshape(()).astype(x.dtype)


def move_kernel(me_ref, *refs, count, ndep, copies):
    srcs, outs, sems = refs[:count], refs[count + ndep : -1], refs[-1]
    me = me_ref[0]
    started = []
    for i, (src, at, out, to) in enumerate(copies):
        copy = pltpu.make_async_copy(srcs[src].at[at(me)], outs[out].at[to(me)], sems.at[i])
        copy.start()
        started.append(copy)
    for copy in started:
        copy.wait()


def move(me, srcs, shapes, copies, deps=()):
    return pl.pallas_call(
        functools.partial(move_kernel, count=len(srcs), ndep=len(deps), copies=copies),
        in_specs=[pl.BlockSpec(memory_space=pltpu.SMEM)] + [ANY] * (len(srcs) + len(deps)),
        out_specs=[ANY] * len(shapes),
        out_shape=[jax.ShapeDtypeStruct(shape, BF16) for shape in shapes],
        scratch_shapes=[pltpu.SemaphoreType.DMA((len(copies),))],
        compiler_params=params(4 * MIB),
        cost_estimate=cost(1, 1),
        name="move",
    )(me, *srcs, *deps)


def pass_on(arrays, after):
    return pl.pallas_call(
        lambda *refs: None,
        in_specs=[ANY] * (len(arrays) + len(after)),
        out_specs=[ANY] * len(arrays),
        out_shape=[jax.ShapeDtypeStruct(v.shape, v.dtype) for v in arrays],
        input_output_aliases={i: i for i in range(len(arrays))},
        compiler_params=params(4 * MIB),
        cost_estimate=cost(1, 1),
        name="pass_on",
    )(*arrays, *after)


class Rows:
    def __init__(self, x, axis, size):
        self.x, self.axis, self.size = x, axis, size
        self.bits = bits_of(size)
        self.R, self.B, self.D = x.shape[0] // size, x.shape[1], x.shape[2]
        self.came = [[] for _ in self.bits]

    def find(self, bit, start):
        return [(v, base) for v, base in self.came[bit] if base <= start][-1]

    def plan(self, bit, start, stop, srcs, copies, out):
        r, B, R = stop - start, self.B, self.R
        lead = 1 << (len(self.bits) - 1 - bit)
        for high in range(lead):
            def owner(me, high=high):
                return (high << (bit + 1)) + (me ^ (1 << bit)) % (1 << (bit + 1))

            def own(me, owner=owner):
                return (pl.ds(owner(me) * R + start, r),)

            def place(lo, hi, high=high):
                return lambda me: (high, slice(None), pl.ds(lo, hi - lo))

            copies.append((len(srcs), own, out, place(0, B)))
            for done in range(bit):
                got, base = self.find(done, start)

                def theirs(me, owner=owner, done=done, base=base):
                    return (owner(me) >> (done + 1), pl.ds(start - base, r))

                copies.append((len(srcs) + 1 + done, theirs, out, place(B << done, B << (done + 1))))
        srcs.append(self.x)
        srcs.extend(self.find(done, start)[0] for done in range(bit))
        return (lead, r, B << bit, self.D)

    def send(self, bit, start, send):
        self.came[bit].append((flip(send, self.axis, self.size, bit), start))

    def parts(self, start):
        return [self.x] + [self.find(bit, start) for bit in self.bits]


def gather(me, jobs, deps=()):
    srcs, copies, shapes = [], [], []
    for out, (rows, bit, start, stop) in enumerate(jobs):
        shapes.append(rows.plan(bit, start, stop, srcs, copies, out))
    return move(me, srcs, shapes, copies, deps)


def exchange(me, jobs, deps=()):
    sends = gather(me, jobs, deps)
    for (rows, bit, start, stop), send in zip(jobs, sends):
        rows.send(bit, start, send)
    return sends


class Blocks:
    def __init__(self, axis, size):
        self.axis, self.size, self.chunks = axis, size, []

    def send(self, lo, hi):
        self.chunks.append((lo, flip(hi, self.axis, self.size, bits_of(self.size)[-1])))

    def turn(self, me, tick):
        bits, axis, size = bits_of(self.size), self.axis, self.size
        half, D = self.chunks[0][0].shape[1:]
        self.R = R = sum(lo.shape[0] for lo, _ in self.chunks)
        self.pieces = pieces = {0: [], 1 << bits[-1]: []}
        at = 0
        for chunk in self.chunks:
            for name, v in zip(pieces, chunk):
                pieces[name].append((v, (), at, v.shape[0], 0))
            at += chunk[0].shape[0]
        for bit in reversed(bits[:-1]):
            half //= 2
            names = list(pieces)
            join = lambda vs: vs[0] if len(vs) == 1 else jnp.concatenate(vs, 0)
            send = jnp.stack([
                join([v[front + (slice(None), slice(token + half, token + 2 * half))] for v, front, _, _, token in pieces[name]])
                for name in names
            ], 0)
            send = late(send, tick)
            self.came = flip(send, axis, size, bit)
            for i, name in enumerate(names):
                pieces[name | (1 << bit)] = [(self.came, (i,), 0, R, 0)]
        self.shape = (size * R, half, D)

    def result(self, me, tick):
        half, D = self.shape[1:]
        entries = [(name,) + source for name, sources in self.pieces.items() for source in sources]
        block = functools.reduce(math.gcd, [rows for _, _, _, _, rows, _ in entries])
        starts = [sum(e[4] // block for e in entries[:i]) for i in range(len(entries) + 1)]
        R = self.R

        def source_spec(e, start, stop):
            _, v, front, _, _, _ = e
            lead = (1,) * len(front)

            def at(i, me):
                return front + (jnp.clip(i, start, stop - 1) - start, 0, 0)

            return pl.BlockSpec(lead + (block, half, D), at)

        def target(i, me):
            where = 0
            for (name, _, _, row, _, _), start, stop in zip(entries, starts, starts[1:]):
                here = ((me[0] ^ name) * R + row) // block + i - start
                where = jnp.where((i >= start) & (i < stop), here, where)
            return (where, 0, 0)

        def kernel(me_ref, *refs):
            i, out = pl.program_id(0), refs[-1]
            for ref, start, stop in zip(refs, starts, starts[1:]):
                @pl.when((i >= start) & (i < stop))
                def _(ref=ref):
                    out[...] = ref[...].reshape(out.shape)

        return pl.pallas_call(
            kernel,
            grid_spec=pltpu.PrefetchScalarGridSpec(
                num_scalar_prefetch=1,
                grid=(starts[-1],),
                in_specs=[source_spec(e, a, b) for e, a, b in zip(entries, starts, starts[1:])] + [ANY],
                out_specs=pl.BlockSpec((block, half, D), target),
            ),
            out_shape=shape_of(self.shape, BF16),
            compiler_params=params(16 * MIB),
            cost_estimate=cost(1, 1),
            name="place",
        )(me, *[e[1] for e in entries], tick)


class Sum:
    def __init__(self, halves, dp, seq, order):
        self.sizes = {"dp": dp, "seq": seq}
        self.order = list(order)
        self.send, self.keep = halves

    def begin(self, send=None):
        self.go("seq", 0, [self.send if send is None else send])

    def go(self, name, bit, sends):
        self.came = [flip(v, name, self.sizes[name], bit) for v in sends]

    def result(self, tick=None, start=0, stop=None):
        came = self.came[0][:, start:stop]
        return late(self.keep[:, start:stop].astype(F32) + came.astype(F32), tick)


def fold_kernel(me_ref, *refs, shapes, ndep, nthrough):
    nin = sum(2 + 2 * took for took, _ in shapes)
    ins, outs = refs[:nin], refs[nin + ndep + nthrough : len(refs) - nthrough]
    outs[-1][...] = jnp.zeros_like(outs[-1])
    for took, gave in shapes:
        keep, came, ins = ins[:2], (ins[2 : 2 + took], ins[2 + took : 2 + 2 * took]), ins[2 + 2 * took :]
        send_refs, keep_ref, outs = outs[:gave], outs[gave], outs[gave + 1 :]
        sums = []
        for base, parts in zip(keep, came):
            part = jnp.concatenate([ref[0] for ref in parts], 1) if took > 1 else parts[0][0]
            sums.append((base[0].astype(F32) + part.astype(F32)).astype(BF16))
        width = sums[0].shape[1] // gave
        for i, ref in enumerate(send_refs):
            ref[...] = sums[0][:, i * width : (i + 1) * width]
        keep_ref[...] = sums[1]


def fold(me, chains, deps=(), split=1, through=()):
    items = [chain.order.pop(0) for chain in chains]
    rows = [chain.keep.shape[0] // 2 for chain in chains]
    steps = max(s for s in (2, 1) if s == 1 or all(r % (16 * s) == 0 for r in rows))
    ins, in_specs, out_specs, out_shape, shapes = [], [], [], [], []
    for chain, (name, bit), r in zip(chains, items, rows):
        tile, width = r // steps, chain.keep.shape[1]
        row = 0 if name == "dp" else 1
        gave = split if chain is chains[-1] else 1

        def half(other, width, row=row, bit=bit, tile=tile):
            return pl.BlockSpec(
                (1, tile, width), lambda i, me: (((me[row] >> bit) & 1) ^ other, i, 0)
            )

        view = lambda v, r=r: v.reshape(2, r, v.shape[1])
        ins += [view(chain.keep)] * 2 + [view(v) for v in chain.came] * 2
        in_specs += [half(1, width), half(0, width)]
        in_specs += [half(other, v.shape[1]) for other in (1, 0) for v in chain.came]
        out_specs += [pl.BlockSpec((tile, width // gave), lambda i, me: (i, 0))] * gave
        out_specs += [pl.BlockSpec((tile, width), lambda i, me: (i, 0))]
        out_shape += [shape_of((r, width // gave), BF16)] * gave
        out_shape += [jax.ShapeDtypeStruct((r, width), BF16)]
        shapes.append((len(chain.came), gave))
    res = pl.pallas_call(
        functools.partial(fold_kernel, shapes=shapes, ndep=len(deps), nthrough=len(through)),
        grid_spec=pltpu.PrefetchScalarGridSpec(
            num_scalar_prefetch=1,
            grid=(steps,),
            in_specs=in_specs + [ANY] * (len(deps) + len(through)),
            out_specs=out_specs + [pl.BlockSpec((1, 1), lambda i, me: (0, 0))] + [ANY] * len(through),
        ),
        out_shape=out_shape + [TICK] + [jax.ShapeDtypeStruct(v.shape, v.dtype) for v in through],
        input_output_aliases={
            1 + len(ins) + len(deps) + i: len(out_shape) + 1 + i for i in range(len(through))
        },
        compiler_params=params(16 * MIB),
        cost_estimate=cost(1, 1),
        name="fold",
    )(me, *ins, *deps, *through)
    tick, on = res[len(out_shape)], res[len(out_shape) + 1 :]
    sends = []
    for chain, (name, bit), (_, gave) in zip(chains, items, shapes):
        chain.go(name, bit, res[:gave])
        chain.keep = res[gave]
        sends += res[:gave]
        res = res[gave + 1 :]
    return (sends, tick, on) if through else (sends, tick)


def chunks_of(count, sizes):
    out, at = [], 0
    for size in sizes:
        stop = min(count, at + size)
        if stop > at:
            out.append((at, stop))
        at = stop
    return out + ([(at, count)] if at < count else [])


def shards(
    dp, seq, hidden_in, segment_ids, cluster_perm, w_qkv, bias_qv, w_out, bias_out, gain_attn,
    shift_attn, w_up, bias_up, w_down, bias_down, gain_ffn, shift_ffn, grad_out,
):
    row_count, block_len, D = hidden_in.shape
    heads = cluster_perm.shape[1]
    hs = D // heads
    L = segment_ids.shape[1]
    FF = w_up.shape[1]
    R = row_count // seq
    T = R * L
    group = 4
    scale = 1.0 / math.sqrt(hs)
    mine = lax.axis_index("seq")
    me = mine.reshape(1).astype(jnp.int32)
    both = jnp.stack([lax.axis_index("dp"), mine]).astype(jnp.int32)

    hidden, gout = Rows(hidden_in, "seq", seq), Rows(grad_out, "seq", seq)
    halves = chunks_of(R, (R // 2,))
    bits = bits_of(seq)
    exchange(me, [(hidden, 0, 0, 1)])
    for bit in bits[1:]:
        first_sent = exchange(me, [(hidden, bit, 0, 1)])
    rest = [(hidden, 0, 1, R)] if R > 1 else []
    exchange(me, rest + [(gout, 0, 0, R)], first_sent)

    bias = jnp.concatenate([bias_qv[:D], jnp.zeros((D,), F32), bias_qv[D:]])
    bias = jnp.broadcast_to(bias, (8, 3 * D))
    none = jnp.zeros((D,), F32)
    vec = jnp.stack([bias_out, gain_attn, shift_attn, bias_down, gain_ffn, shift_ffn, none, none])
    wt, bt, code = prepare(me, seq, w_qkv, bias, cluster_perm.transpose(1, 0, 2), segment_ids, group, first_sent)

    jobs = [(hidden, row, row + 1) for row in range(1, R)] + [(gout, *half) for half in halves]
    early = len(bits) == 2
    if early:
        queue = list(zip(jobs, gather(me, [(rows, bits[-1], a, b) for rows, a, b in jobs], first_sent)))
    else:
        queue = [(job, None) for job in jobs]

    def launch(after):
        if not queue:
            return after
        (rows, start, stop), send = queue.pop(0)
        if early:
            (send,) = pass_on([send], after)
            rows.send(bits[-1], start, send)
            return [send]
        for bit in bits[1:]:
            after = exchange(me, [(rows, bit, start, stop)], after)
        return after

    held, tick = (), None
    for row in range(R):
        deps = launch(first_sent if tick is None else [tick]) if row < R - 1 else []
        if row == R - 2:
            deps = deps + launch([tick] if tick is not None else first_sent)
        res = attend(
            me, hidden.parts(row), row, R, code, wt, bt, w_out, vec, heads, hs, scale, group, deps, held,
        )
        held, tick = res[:8], res[8]
    x, qkv, p, il, att, first, n1, s1 = held
    first = first.reshape(T, D)

    held, out_blocks, sums_ffn = (), Blocks("seq", seq), []
    for i, (start, stop) in enumerate(halves):
        deps = launch([tick])
        lo, hi, *held, sums, tick = ffn(
            me, first, gout.parts(start), start, stop - start, R, w_up, bias_up.reshape(1, -1), w_down,
            vec, deps, held,
        )
        out_blocks.send(lo, hi)
        sums_ffn.append(sums)
    gffn, act, slope = held

    low = [("dp", b) for b in bits_of(dp)]
    high = [("seq", b) for b in bits_of(seq)[1:]]
    turned = low[1:2] + low[:1] + high + low[2:]

    n = dp * seq
    came_out = [v for _, v in out_blocks.chunks]
    down = Sum(down_grad(me, dp, seq, low + high, act, gffn, far(*came_out[:1])), dp, seq, low + high)
    down.begin()
    held, sums_attn, sums_up, deps = (), [], [], []
    for i, (start, stop) in enumerate(halves):
        *held, sums1, sums2, tick = ffn_back(
            start, stop - start, gffn, slope, w_up, w_down, w_out, n1, s1, vec, att, il, heads, hs,
            deps, held,
        )
        sums_attn.append(sums1)
        sums_up.append(sums2)
        deps = []
        if i == 0:
            deps, _ = fold(both, [down], [tick] + far(*came_out[1:]))
            deps = far(*deps)
    gpre, gbr, do, de = held
    d_up, tick = up_out_grad(me, dp, seq, low + high, first, gpre, att, gbr, deps)
    up = Sum(d_up, dp, seq, low + high)
    deps, _, (send,) = fold(both, [down], [tick], 1, [up.send])
    deps = far(*deps)
    up.begin(send)
    g, in_blocks = None, Blocks("seq", seq)
    for start, stop in halves:
        lo = hi = None
        for row in range(start, stop):
            if row == 1:
                sends, _ = fold(both, [down, up] if down.order else [up], [tick], 2)
                sends = far(*sends)
                deps = sends[:-1]
            elif row == 2:
                deps = [sends[-1], up.came[0]]
            elif row == 3:
                deps, _ = fold(both, [down, up] if down.order else [up], [tick])
                deps = far(*deps)
            elif row:
                deps = []
            g, lo, hi, tick = attend_back(
                row, 1, stop - start, row - start, qkv, p, do, de, gbr, wt, heads, hs, scale, group,
                deps, (g, lo, hi),
            )
        in_blocks.send(lo, hi)
    g = g.reshape(R, 3 * D, L)
    deps, _ = fold(both, [up], [tick] + far(in_blocks.chunks[0][1]))
    deps = far(*deps)

    sums = sums_attn + sums_up + sums_ffn
    kinds = [sums_attn, sums_up, sums_ffn]
    firsts = [sum(len(v) for v in kinds[:i]) for i in range(3)]
    span = lambda kind, row, *cols: (range(firsts[kind], firsts[kind] + len(kinds[kind])), row, cols)
    spans = [
        span(0, 0, (0, D)), span(0, 1, (0, D)), span(0, 2, (0, D)), span(1, 0, (0, FF)),
        span(2, 0, (0, D)), span(2, 1, (0, D)), span(2, 2, (0, D)),
    ]
    per = [2 * D // n] + [sum(hi - lo for lo, hi in cols) // n for _, _, cols in spans]
    orders = [low + high, turned, high[:1] + low[2:] + low[:2] + high[1:]]
    d_qkv, tick = qkv_grad(me, dp, seq, orders, x, g, sums, spans, deps)
    lasts = [Sum(halves_, dp, seq, order) for halves_, order in zip(d_qkv, orders)]
    while len(up.order) > 1:
        _, tick = fold(both, [up], [tick])
    _, tick, sends = fold(
        both, [up], [tick] + far(*[v for _, v in in_blocks.chunks[1:]]), 1, [s.send for s in lasts]
    )
    for s, send in zip(lasts, sends):
        s.begin(send)
    while down.order:
        _, tick = fold(both, [down], [tick])
    out_blocks.turn(me, tick)
    stage, done = 0, []
    while lasts[0].order:
        _, tick = fold(both, ([up] if up.order else []) + lasts, [tick] + done)
        done = []
        if stage == 0:
            in_blocks.turn(me, tick)
            out_hidden = out_blocks.result(me, tick)
            done = far(out_hidden)
        if stage == 1:
            grad_in = in_blocks.result(me, tick)
            done = far(grad_in)
        if stage == 2:
            r_down, r_up, r_out = down.result(tick), up.result(tick, 0, FF), up.result(tick, FF)
            done = far(r_down, r_up, r_out)
        stage += 1
    r_qkv = [s.result() for s in lasts]
    vec = r_qkv[-1][: spots(per)[-1] // 128 + 1, D:].reshape(-1)
    cuts = [vec[at : at + width] for at, width in zip(spots(per), per)]
    b_qv, b_out, g_attn, s_attn, b_up, b_down, g_ffn, s_ffn = cuts
    return (
        out_hidden, grad_in, jnp.concatenate(r_qkv[:-1] + [r_qkv[-1][:, :D]], 1), b_qv,
        r_out, b_out, g_attn, s_attn, r_up, b_up, r_down, b_down, g_ffn, s_ffn,
    )


def solution(mesh):
    tok = P("dp", "seq", None)
    both = ("dp", "seq")
    return jax.shard_map(
        functools.partial(shards, mesh.shape["dp"], mesh.shape["seq"]),
        mesh=mesh,
        in_specs=(tok, P("dp", None), P("dp", None, None)) + (P(),) * 12 + (tok,),
        out_specs=(
            tok, tok, P(both, None), P(both), P(both, None), P(both), P(both), P(both),
            P(both, None), P(both), P(both, None), P(both), P(both), P(both),
        ),
        check_vma=False,
    )
```
